32 devices in a mesh: rep: 8 (over z, core), shard: 4 (over y, x).
Axes of the slice: x: 2, y: 2, z: 4, core: 2. Of those that a mesh axis runs over, the one named last changes fastest.
Arguments:
- layer_input: bfloat16 [32768, 1024], P(('rep', 'shard')), may hold values from -6 to 6
- seq_lengths: int32 [32], P(('rep', 'shard')), may hold values from 256 to 1024, as said below
- out_grad: bfloat16 [32768, 1024], P(('rep', 'shard')), may hold values from -6 to 6
- attn_gain: bfloat16 [1024], P('shard'), may hold values from 0.5 to 1.5
- attn_shift: bfloat16 [1024], P('shard'), may hold values from -1 to 1
- mlp_gain: bfloat16 [1024], P('shard'), may hold values from 0.5 to 1.5
- mlp_shift: bfloat16 [1024], P('shard'), may hold values from -1 to 1
- qkv_weight: bfloat16 [1024, 3072], P('shard'), may hold values from -0.1875 to 0.1875
- qkv_bias: bfloat16 [3072], P('shard'), may hold values from -1 to 1
- dense_weight: bfloat16 [1024, 1024], P('shard'), may hold values from -3 to 3
- dense_bias: bfloat16 [1024], P('shard'), may hold values from -1 to 1
- inner_weight: bfloat16 [1024, 4096], P('shard'), may hold values from -0.1875 to 0.1875
- inner_bias: bfloat16 [4096], P('shard'), may hold values from -1 to 1
- outer_weight: bfloat16 [4096, 1024], P('shard'), may hold values from -0.09375 to 0.09375
- outer_bias: bfloat16 [1024], P('shard'), may hold values from -1 to 1
Outputs:
- layer_output: float32 [32768, 1024], P(('rep', 'shard'))
- input_grad: float32 [32768, 1024], P(('rep', 'shard'))
- attn_gain_grad: float32 [1024], P('shard')
- attn_shift_grad: float32 [1024], P('shard')
- mlp_gain_grad: float32 [1024], P('shard')
- mlp_shift_grad: float32 [1024], P('shard')
- qkv_weight_grad: float32 [1024, 3072], P('shard')
- qkv_bias_grad: float32 [3072], P('shard')
- dense_weight_grad: float32 [1024, 1024], P('shard')
- dense_bias_grad: float32 [1024], P('shard')
- inner_weight_grad: float32 [1024, 4096], P('shard')
- inner_bias_grad: float32 [4096], P('shard')
- outer_weight_grad: float32 [4096, 1024], P('shard')
- outer_bias_grad: float32 [1024], P('shard')
The draws below stay inside these ranges and needn't reach their ends.
Inputs may be any that keep to these rules, and one draw needn't show every extreme that they name: Each slot holds one sequence in its first seq_lengths positions; at least one slot is full.
All inputs are finite; a program needn't handle non-finite values.
Results may differ from the reference program's by a relative error of at most 0.0089.
Values may be sent and summed in bfloat16 or wider, within the bound.
No kernel may reach another device: no remote copies, remote signals or barrier semaphores. Data moves between devices by JAX's collectives and lax.ppermute only.
A program may use at most 384 MiB of HBM per device.

```python
import jax
import jax.numpy as jnp
from jax import lax

D = 1024
H = 16
FF = 4096
HD = 64
ROT = 16
SLOT = 1024
QB = 512
SLOTS = 32
TOKENS = 32768


def draw_seq_lengths(key, part):
    key = jax.random.fold_in(key, 11)
    draw_key, pick_key = jax.random.split(key)
    drawn = jax.random.randint(draw_key, (SLOTS,), SLOT // 4, SLOT + 1, dtype=jnp.int32)
    chosen = jax.random.randint(pick_key, (), 0, SLOTS, dtype=jnp.int32)
    return jnp.where(jnp.arange(SLOTS, dtype=jnp.int32) == chosen, SLOT, drawn).astype(jnp.int32)


def with_spikes(values, rng, source, target, shards_of, factor):
    def block_of(position):
        return (jnp.arange(values.shape[position]) // (values.shape[position] // shards_of)).reshape((-1,) + (1,) * (values.ndim - 1 - position))

    near = jax.random.permutation(rng, shards_of)[block_of(target)]
    other_side = (block_of(target) + shards_of // 2) % shards_of
    return jnp.where((block_of(source) == near) | (block_of(source) == other_side), factor * values, values)


def shard_levels(own_key, shape, shards, least, high):
    level = 1.0
    for position, parts in shards:
        steps = jax.random.uniform(jax.random.fold_in(jax.random.fold_in(own_key, 6), position), (parts,), jnp.float32, least / len(shards), high / len(shards))
        level = level * jnp.repeat(jnp.exp(steps), shape[position] // parts).reshape((-1,) + (1,) * (len(shape) - 1 - position))
    return level


def scatter_about(stream_key, shape, spread, bound, pieces=(), kind=jnp.bfloat16):
    result = jax.random.normal(stream_key, shape, jnp.float32) * spread
    if len(pieces) > 0:
        result = shard_levels(stream_key, shape, pieces, -0.22, 0.18) * result
    return jnp.clip(result, min=-bound, max=bound).astype(kind)


def noise_with(rng, shape, deviation, limit, cuts, heavy, kind=jnp.bfloat16):
    values = deviation * jax.random.normal(rng, shape, jnp.float32)
    if cuts:
        values = values * shard_levels(rng, shape, cuts, -0.22, 0.18)
    return jnp.clip(with_spikes(values, jax.random.fold_in(rng, 3), *heavy), -limit, limit).astype(kind)


def setup_inputs(seed: int = 0) -> dict:
    arg_keys = jax.random.split(jax.random.key(seed), 16)
    layer_input = scatter_about(arg_keys[0], (TOKENS, D), 1.0, 6.0, ((0, 32),))
    seq_lengths = draw_seq_lengths(jax.random.fold_in(arg_keys[15], 71), 0)
    out_grad = noise_with(arg_keys[2], (TOKENS, D), 1.0, 6.0, ((0, 32),), (0, 1, 32, 2.75))
    attn_gain = jnp.clip(1.0 + 0.1 * jax.random.normal(arg_keys[3], (D,), jnp.float32), 0.5, 1.5).astype(jnp.bfloat16)
    attn_shift = scatter_about(arg_keys[4], (D,), 0.2, 1.0, ((0, 4),))
    mlp_gain = jnp.clip(1.0 + 0.1 * jax.random.normal(arg_keys[5], (D,), jnp.float32), 0.5, 1.5).astype(jnp.bfloat16)
    mlp_shift = scatter_about(arg_keys[6], (D,), 0.2, 1.0, ((0, 4),))
    qkv_weight = scatter_about(arg_keys[7], (D, 3 * D), D ** -0.5, 0.1875, ((0, 4),))
    qkv_bias = scatter_about(arg_keys[8], (3 * D,), 0.2, 1.0, ((0, 4),))
    dense_weight = scatter_about(arg_keys[9], (D, D), (max(1, 4 * D // SLOT)) ** -0.5, 3.0, ((0, 4),))
    dense_bias = scatter_about(arg_keys[10], (D,), 0.2, 1.0, ((0, 4),))
    inner_weight = scatter_about(arg_keys[11], (D, FF), D ** -0.5, 0.1875, ((0, 4),))
    inner_bias = scatter_about(arg_keys[12], (FF,), 0.2, 1.0, ((0, 4),))
    outer_weight = scatter_about(arg_keys[13], (FF, D), FF ** -0.5, 0.09375, ((0, 4),))
    outer_bias = scatter_about(arg_keys[14], (D,), 0.2, 1.0, ((0, 4),))
    return {"layer_input": layer_input, "seq_lengths": seq_lengths, "out_grad": out_grad, "attn_gain": attn_gain, "attn_shift": attn_shift, "mlp_gain": mlp_gain, "mlp_shift": mlp_shift, "qkv_weight": qkv_weight, "qkv_bias": qkv_bias, "dense_weight": dense_weight, "dense_bias": dense_bias, "inner_weight": inner_weight, "inner_bias": inner_bias, "outer_weight": outer_weight, "outer_bias": outer_bias}


@jax.custom_vjp
def low(v):
    return lax.optimization_barrier(v.astype(jnp.bfloat16)).astype(jnp.float32)

@jax.custom_vjp
def low_back(v):
    return v

def low_keep(v):
    return (low(v), None)

def low_pass(kept, grad):
    return (grad,)

def back_keep(v):
    return (v, None)

def back_low(kept, grad):
    return (low(grad),)
low.defvjp(low_keep, low_pass)
low_back.defvjp(back_keep, back_low)
EPSILON = 1e-05
PRECISE = lax.Precision.HIGHEST
MASKED = -1e+30

def matmul_high(left, right):
    return jnp.dot(left, right, precision=PRECISE, preferred_element_type=jnp.float32)

def layer_norm(values, gain, shift):
    average = lax.optimization_barrier(jnp.mean(values, axis=-1, keepdims=True))
    centered = values - average
    variance = lax.optimization_barrier(jnp.mean(centered * centered, axis=-1, keepdims=True))
    return centered * lax.rsqrt(variance + EPSILON) * gain + shift

def rotary_tables():
    positions = jnp.arange(SLOT, dtype=jnp.float32)
    rot_half = ROT // 2
    inverse = 1.0 / 10000.0 ** (jnp.arange(rot_half, dtype=jnp.float32) * (2.0 / ROT))
    angles = positions[:, None] * inverse[None, :]
    angles = jnp.concatenate([angles, angles], axis=1)
    padding = HD - ROT
    cosine_table = jnp.concatenate([jnp.cos(angles), jnp.ones((SLOT, padding), jnp.float32)], axis=1)
    sine_table = jnp.concatenate([jnp.sin(angles), jnp.zeros((SLOT, padding), jnp.float32)], axis=1)
    return (cosine_table[:, None, :], sine_table[:, None, :])

def rotate(vectors, cosine_table, sine_table):
    rot_half = ROT // 2
    partner = jnp.concatenate([-vectors[..., rot_half:ROT], vectors[..., :rot_half], jnp.zeros_like(vectors[..., ROT:])], axis=-1)
    return vectors * cosine_table + partner * sine_table

def attend(queries, all_keys, all_values, length):
    key_index = jnp.arange(SLOT, dtype=jnp.int32)

    def one_block(block_index):
        row_start = block_index * QB
        block_queries = lax.dynamic_slice_in_dim(queries, row_start, QB, 0)
        raw = jnp.einsum('qhd,khd->hqk', block_queries, all_keys, precision=PRECISE)
        scores = low_back(0.125 * raw)
        query_rows = row_start + jnp.arange(QB, dtype=jnp.int32)
        allowed = (key_index[None, :] <= query_rows[:, None]) & (key_index[None, :] < length)
        masked = jnp.where(allowed[None], scores, MASKED)
        row_max = lax.optimization_barrier(jnp.max(masked, axis=-1, keepdims=True))
        exponent = jnp.exp(masked - row_max)
        probs = exponent / lax.optimization_barrier(jnp.sum(exponent, axis=-1, keepdims=True))
        return jnp.einsum('hqk,khd->qhd', low(probs), all_values, precision=PRECISE)
    blocks = lax.map(jax.checkpoint(one_block), jnp.arange(SLOT // QB, dtype=jnp.int32))
    return blocks.reshape(SLOT, D)

def slot_forward(params, layer_slot, length):
    attn_gain, attn_shift, mlp_gain, mlp_shift, qkv_weight, qkv_bias, dense_weight, dense_bias, inner_weight, inner_bias, outer_weight, outer_bias = params
    normed_attn = low(layer_norm(layer_slot, attn_gain, attn_shift))
    normed_mlp = low(layer_norm(layer_slot, mlp_gain, mlp_shift))
    projected = low_back(matmul_high(normed_attn, qkv_weight) + qkv_bias)
    cosine_table, sine_table = rotary_tables()
    queries = low(rotate(projected[:, :D].reshape(SLOT, H, HD), cosine_table, sine_table))
    all_keys = low(rotate(projected[:, D:2 * D].reshape(SLOT, H, HD), cosine_table, sine_table))
    all_values = low(projected[:, 2 * D:].reshape(SLOT, H, HD))
    context = low(low_back(attend(queries, all_keys, all_values, length)))
    attn_out = matmul_high(context, dense_weight) + dense_bias
    inner = low_back(matmul_high(normed_mlp, inner_weight) + inner_bias)
    activated = low(jax.nn.gelu(inner, approximate=False))
    mlp_out = matmul_high(activated, outer_weight) + outer_bias
    return layer_slot + attn_out + mlp_out

def reference(layer_input, seq_lengths, out_grad, attn_gain, attn_shift, mlp_gain, mlp_shift, qkv_weight, qkv_bias, dense_weight, dense_bias, inner_weight, inner_bias, outer_weight, outer_bias):
    params = tuple((member.astype(jnp.float32) for member in (attn_gain, attn_shift, mlp_gain, mlp_shift, qkv_weight, qkv_bias, dense_weight, dense_bias, inner_weight, inner_bias, outer_weight, outer_bias)))
    input_slots = layer_input.astype(jnp.float32).reshape(SLOTS, SLOT, D)
    positions = jnp.arange(SLOT, dtype=jnp.int32)
    valid = (positions[None, :] < seq_lengths[:, None]).astype(jnp.float32)
    cotangent = out_grad.astype(jnp.float32).reshape(SLOTS, SLOT, D) * valid[..., None]

    def whole_layer(params_in, slots_in):

        def slot_step(running, operands):
            slot_rows, length = operands
            return (running, jax.checkpoint(slot_forward)(params_in, slot_rows, length))
        unused, outputs = lax.scan(slot_step, jnp.zeros((), jnp.float32), (slots_in, seq_lengths))
        return outputs
    outputs, pullback = jax.vjp(whole_layer, params, input_slots)
    param_grads, slot_grads = pullback(cotangent)
    return (outputs.reshape(TOKENS, D), slot_grads.reshape(TOKENS, D), param_grads[0], param_grads[1], param_grads[2], param_grads[3], param_grads[4], param_grads[5], param_grads[6], param_grads[7], param_grads[8], param_grads[9], param_grads[10], param_grads[11])
```

```python
import functools

import jax
import jax.numpy as jnp
import numpy as np
from jax import lax
from jax.experimental import pallas as pl
from jax.experimental.pallas import tpu as pltpu
from jax.sharding import Mesh, PartitionSpec as P

D = 1024
H = 16
FF = 4096
HD = 64
ROT = 16
T = 1024
GROUP = 256
HEADS = GROUP // HD
ROWS = 256
EPSILON = 1e-05
MASKED = -1e30
BF = jnp.bfloat16
F32 = jnp.float32
VMEM = 60 * 2**20


def nn(a, b):
    return lax.dot_general(a, b, (((1,), (0,)), ((), ())), preferred_element_type=F32)


def nt(a, b):
    return lax.dot_general(a, b, (((1,), (1,)), ((), ())), preferred_element_type=F32)


def tn(a, b):
    return lax.dot_general(a, b, (((0,), (0,)), ((), ())), preferred_element_type=F32)


def rows_of(index, size):
    return slice(index * size, (index + 1) * size)


def rotary_tables():
    half = ROT // 2
    inverse = 1.0 / np.float32(10000.0) ** (np.arange(half, dtype=np.float32) * np.float32(2.0 / ROT))
    angles = np.arange(T, dtype=np.float32)[:, None] * inverse.astype(np.float32)[None, :]
    cosine = np.ones((T, HD), np.float32)
    ahead = np.zeros((T, HD), np.float32)
    behind = np.zeros((T, HD), np.float32)
    cosine[:, :half] = np.cos(angles)
    cosine[:, half:ROT] = np.cos(angles)
    ahead[:, :half] = -np.sin(angles)
    behind[:, half:ROT] = np.sin(angles)
    return [np.tile(table, (1, 2)) for table in (cosine, ahead, behind)]


def add_columns(ref, rows, value, order):
    width = value.shape[1] // len(order)
    for place, block in enumerate(order):
        ref[rows, rows_of(block, width)] += value[:, rows_of(place, width)]


def mlp_kernel(order, nm, gr, wi, bi, wo, out, dn, gwi, gwo, gbi, act, ig):
    @pl.when(pl.program_id(0) == 0)
    def _():
        out[...] = jnp.zeros_like(out)
        dn[...] = jnp.zeros_like(dn)

    bias_sum = jnp.zeros(gbi.shape, F32)
    for t in range(T // ROWS):
        r = rows_of(t, ROWS)
        inner = nn(nm[r, :], wi[...]) + bi[...]
        grad = nt(gr[r, :], wo[...])
        normal = 0.5 * lax.erf(inner * 0.7071067811865476) + 0.5
        slope = normal + inner * jnp.exp(-0.5 * inner * inner) * 0.3989422804014327
        act[r, :] = (inner * normal).astype(BF)
        inner_grad = (grad * slope).astype(BF)
        ig[r, :] = inner_grad
        bias_sum += jnp.sum(inner_grad.astype(F32), axis=0, keepdims=True)
    gbi[...] = bias_sum
    for t in range(T // ROWS):
        r = rows_of(t, ROWS)
        out[r, :] += nn(act[r, :], wo[...])
        add_columns(dn, r, nt(ig[r, :], wi[...]), order)
    for d in range(D // ROWS):
        r = rows_of(d, ROWS)
        gwi[r, :] = tn(nm[:, r], ig[...]).astype(BF)
    step = min(ROWS, act.shape[1])
    for f in range(act.shape[1] // step):
        r = rows_of(f, step)
        gwo[r, :] = tn(act[:, r], gr[...]).astype(BF)


def mlp(order, nm, gr, wi, bi, wo):
    tile = FF // len(order)
    half = len(order) // 2
    one = pl.Buffered(1)
    whole = lambda: pl.BlockSpec((T, D), lambda i: (0, 0), pipeline_mode=one)
    total = lambda: pl.BlockSpec((T, D), lambda i: (0, 0))
    columns = lambda rows: pl.BlockSpec((rows, tile), lambda i: (0, (i % half) * 2 + i // half))
    return pl.pallas_call(
        functools.partial(mlp_kernel, order),
        grid=(FF // tile,),
        in_specs=[whole(), whole(), columns(D), columns(1), pl.BlockSpec((tile, D), lambda i: (i, 0))],
        out_specs=[total(), total(), columns(D), pl.BlockSpec((tile, D), lambda i: (i, 0)), columns(1)],
        out_shape=[
            jax.ShapeDtypeStruct((T, D), F32),
            jax.ShapeDtypeStruct((T, D), F32),
            jax.ShapeDtypeStruct((D, FF), BF),
            jax.ShapeDtypeStruct((FF, D), BF),
            jax.ShapeDtypeStruct((1, FF), F32),
        ],
        scratch_shapes=[pltpu.VMEM((T, tile), BF), pltpu.VMEM((T, tile), BF)],
        compiler_params=pltpu.CompilerParams(vmem_limit_bytes=VMEM),
        cost_estimate=pl.CostEstimate(flops=12 * T * D * FF, bytes_accessed=60 * 2**20, transcendentals=2 * T * FF),
        name="mlp",
    )(nm, gr, wi, bi, wo)


def attn_kernel(
    order, length, na, gr, wq, wk, wv, bq, bk, bv, wd, cosine, ahead, behind,
    out, dn, gwq, gwk, gwv, gwd, gb,
    q, k, v, dc, ctx, dq, dk, dv, grads,
):
    @pl.when(pl.program_id(0) == 0)
    def _():
        out[...] = jnp.zeros_like(out)
        dn[...] = jnp.zeros_like(dn)

    def turn(x, r, back):
        parts = []
        for p in range(GROUP // 128):
            pair = x[:, rows_of(p, 128)]
            straight = pair * cosine[r, :]
            across = (
                pltpu.roll(pair, 128 - ROT // 2, 1) * ahead[r, :]
                + pltpu.roll(pair, ROT // 2, 1) * behind[r, :]
            )
            parts.append(straight - across if back else straight + across)
        return jnp.concatenate(parts, axis=1)

    for t in range(T // ROWS):
        r = rows_of(t, ROWS)
        x = na[r, :]
        queries = (turn(nn(x, wq[...]) + bq[...], r, False).astype(BF) * 0.125).astype(BF)
        keys = turn(nn(x, wk[...]) + bk[...], r, False).astype(BF)
        values = (nn(x, wv[...]) + bv[...]).astype(BF)
        context_grad = nt(gr[r, :], wd[...]).astype(BF)
        for h in range(HEADS):
            c = rows_of(h, HD)
            q[h, r, :] = queries[:, c]
            k[h, r, :] = keys[:, c]
            v[h, r, :] = values[:, c]
            dc[h, r, :] = context_grad[:, c]

    block = 256
    inside = lax.broadcasted_iota(jnp.int32, (1, T), 1) < length[0]
    bias = jnp.where(inside, 0.0, MASKED).astype(F32)
    below = lax.broadcasted_iota(jnp.int32, (block, block), 1) <= lax.broadcasted_iota(jnp.int32, (block, block), 0)
    causal = jnp.where(below, 0.0, MASKED).astype(F32)

    def head(h, carry):
        dk[h] = jnp.zeros((T, HD), F32)
        dv[h] = jnp.zeros((T, HD), F32)
        for i in range(T // block):
            r = rows_of(i, block)
            spans = ([slice(0, i * block)] if i else []) + [r]
            query = q[h, r, :]
            scores = [nt(query, k[h, c, :]) + bias[:, c] for c in spans]
            scores[-1] += causal
            top = functools.reduce(jnp.maximum, [jnp.max(s, axis=1, keepdims=True) for s in scores])
            weights = [jnp.exp(s - top) for s in scores]
            scale = 1.0 / sum(jnp.sum(w, axis=1, keepdims=True) for w in weights)
            low = [w.astype(BF) for w in weights]
            context = sum(nn(w, v[h, c, :]) for w, c in zip(low, spans))
            ctx[h, r, :] = (context * scale).astype(BF)
            scaled_grad = (dc[h, r, :].astype(F32) * scale).astype(BF)
            probs_grad = [nt(scaled_grad, v[h, c, :]) for c in spans]
            inner = scale * sum(jnp.sum(w * p, axis=1, keepdims=True) for w, p in zip(weights, probs_grad))
            score_grad = [(w * (p - inner)).astype(BF) for w, p in zip(weights, probs_grad)]
            dq[h, r, :] = sum(nn(s, k[h, c, :]) for s, c in zip(score_grad, spans))
            for s, w, c in zip(score_grad, low, spans):
                dk[h, c, :] += tn(s, query)
                dv[h, c, :] += tn(w, scaled_grad)
        return carry

    lax.fori_loop(0, HEADS, head, 0)

    sums = [jnp.zeros((1, GROUP), F32) for _ in range(3)]
    together = lambda ref, r: jnp.concatenate([ref[h, r, :] for h in range(HEADS)], axis=1)
    for t in range(T // ROWS):
        r = rows_of(t, ROWS)
        context = together(ctx, r)
        grads[r, 3 * GROUP :] = context
        out[r, :] += nn(context, wd[...])
        pieces = (
            turn(together(dq, r) * 0.125, r, True).astype(BF),
            turn(together(dk, r), r, True).astype(BF),
            together(dv, r).astype(BF),
        )
        for p, piece in enumerate(pieces):
            grads[r, rows_of(p, GROUP)] = piece
            sums[p] += jnp.sum(piece.astype(F32), axis=0, keepdims=True)
        normed_grad = sum(nt(piece, w[...]) for piece, w in zip(pieces, (wq, wk, wv)))
        add_columns(dn, r, normed_grad, order)
    for p in range(3):
        gb[p : p + 1, :] = sums[p]
    for d in range(D // ROWS):
        r = rows_of(d, ROWS)
        x = na[:, r]
        for p, g in enumerate((gwq, gwk, gwv)):
            g[r, :] = tn(x, grads[:, rows_of(p, GROUP)]).astype(BF)
    gwd[...] = tn(grads[:, 3 * GROUP :], gr[...]).astype(BF)


def attn(order, length, na, gr, weight, bias, wd):
    groups = D // GROUP
    one = pl.Buffered(1)
    whole = lambda shape: pl.BlockSpec(shape, lambda i: (0, 0), pipeline_mode=one)
    total = lambda: pl.BlockSpec((T, D), lambda i: (0, 0))
    columns = lambda rows, part=0: pl.BlockSpec((rows, GROUP), lambda i: (0, i + part * groups))
    head_rows = lambda dtype: pltpu.VMEM((HEADS, T, HD), dtype)
    return pl.pallas_call(
        functools.partial(attn_kernel, order),
        grid=(groups,),
        in_specs=[pl.BlockSpec(memory_space=pltpu.SMEM), whole((T, D)), whole((T, D))]
        + [columns(D, p) for p in range(3)]
        + [columns(1, p) for p in range(3)]
        + [pl.BlockSpec((GROUP, D), lambda i: (i, 0))]
        + [whole((T, 128))] * 3,
        out_specs=[total(), total()] + [columns(D)] * 3 + [pl.BlockSpec((GROUP, D), lambda i: (i, 0)), columns(3)],
        out_shape=[jax.ShapeDtypeStruct((T, D), F32)] * 2
        + [jax.ShapeDtypeStruct((D, D), BF)] * 4
        + [jax.ShapeDtypeStruct((3, D), F32)],
        scratch_shapes=[head_rows(BF)] * 5 + [head_rows(F32)] * 3 + [pltpu.VMEM((T, 4 * GROUP), BF)],
        compiler_params=pltpu.CompilerParams(vmem_limit_bytes=VMEM),
        cost_estimate=pl.CostEstimate(flops=90 * 10**9, bytes_accessed=40 * 2**20, transcendentals=10 * 2**20),
        name="attn",
    )(length, na, gr, weight, weight, weight, bias, bias, bias, wd, *map(jnp.asarray, rotary_tables()))


def shards(
    layer_input, seq_lengths, out_grad, attn_gain, attn_shift, mlp_gain, mlp_shift, qkv_weight, qkv_bias,
    dense_weight, dense_bias, inner_weight, inner_bias, outer_weight, outer_bias,
):
    groupings = ("core", "y", "x")
    shard_count = lax.axis_size("y") * lax.axis_size("x")
    core = lax.axis_index("core")
    order = [2 * a + h for h in range(2) for a in range(shard_count)]

    def gather(piece):
        half = piece.shape[0] // 2
        mine = lax.dynamic_slice_in_dim(piece, core * half, half, 0)
        return lax.all_gather(mine, groupings, axis=0, tiled=True)

    def natural(rows):
        return jnp.swapaxes(rows.reshape(2, shard_count, -1, rows.shape[1]), 0, 1).reshape(rows.shape)

    def halves_first(rows):
        return jnp.swapaxes(rows.reshape(shard_count, 2, -1, rows.shape[1]), 0, 1).reshape(rows.shape)

    vectors = jnp.concatenate(
        [attn_gain, attn_shift, mlp_gain, mlp_shift, dense_bias, outer_bias, qkv_bias, inner_bias]
    )
    vectors = lax.all_gather(vectors, ("y", "x"), axis=0, tiled=False).astype(F32)
    sizes = [D] * 6 + [3 * D, FF]
    cuts = np.cumsum([size // shard_count for size in sizes])[:-1]
    gain_a, shift_a, gain_m, shift_m, bias_d, bias_o, bias_qkv, bias_i = (
        part.reshape(1, -1) for part in jnp.split(vectors, cuts, axis=1)
    )
    wi = gather(inner_weight)
    wo = gather(outer_weight)
    wqkv = gather(qkv_weight)
    wd = natural(gather(dense_weight))

    x = layer_input.astype(F32)
    mean = jnp.mean(x, axis=1, keepdims=True)
    centered = x - mean
    inverse = lax.rsqrt(jnp.mean(centered * centered, axis=1, keepdims=True) + EPSILON)
    unit = centered * inverse
    valid = jnp.arange(T, dtype=jnp.int32)[:, None] < seq_lengths[0]
    gr = jnp.where(valid, out_grad, jnp.zeros_like(out_grad))
    blocked = lambda rows: jnp.swapaxes(rows.reshape(T, shard_count, 2, -1), 1, 2).reshape(T, D)
    nm = blocked((unit * gain_m + shift_m).astype(BF))
    na = blocked((unit * gain_a + shift_a).astype(BF))

    out_m, dnm, gwi, gwo, gbi = mlp(order, nm, gr, wi, bias_i, wo)
    out_a, dna, gwq, gwk, gwv, gwd, gbqkv = attn(order, seq_lengths, na, gr, wqkv, bias_qkv, wd)

    def reduce(grad):
        part = lax.psum_scatter(grad, "core", scatter_dimension=0, tiled=True)
        part = lax.psum_scatter(part, ("y", "x"), scatter_dimension=0, tiled=True)
        part = lax.psum(part, "z")
        return lax.all_gather(part, "core", axis=0, tiled=True).astype(F32)

    grad_wi = reduce(gwi)
    grad_wo = reduce(gwo)
    grad_d = reduce(halves_first(gwd))
    grad_qkv = jnp.concatenate([reduce(g) for g in (gwq, gwk, gwv)], axis=1)

    layer_output = x + out_m + out_a + (bias_d + bias_o)
    g = dna * gain_a + dnm * gain_m
    gr32 = gr.astype(F32)
    input_grad = gr32 + inverse * (
        g - jnp.mean(g, axis=1, keepdims=True) - unit * jnp.mean(g * unit, axis=1, keepdims=True)
    )
    column = lambda rows: jnp.sum(rows, axis=0)
    parts = [column(dna * unit), column(dna), column(dnm * unit), column(dnm), column(gr32), gbqkv, gbi]
    small = jnp.concatenate([p.reshape(shard_count, -1) for p in parts], axis=1)
    small = lax.psum_scatter(small, ("y", "x"), scatter_dimension=0, tiled=True)
    small = lax.psum(small, ("z", "core"))
    cuts = np.cumsum([size // shard_count for size in [D] * 5 + [3 * D, FF]])[:-1]
    g_ga, g_sa, g_gm, g_sm, g_bd, g_bqkv, g_bi = (p.reshape(-1) for p in jnp.split(small, cuts, axis=1))
    return (
        layer_output, input_grad, g_ga, g_sa, g_gm, g_sm, grad_qkv, g_bqkv, grad_d, g_bd, grad_wi, g_bi, grad_wo, g_bd,
    )


def solution(mesh):
    replicas, shard_count = mesh.shape["rep"], mesh.shape["shard"]
    shape = (replicas // 2, 2, 2, shard_count // 2)
    cut = Mesh(mesh.devices.reshape(shape), ("z", "core", "y", "x"))
    both = P(("z", "core", "y", "x"), None)
    shard = P(("y", "x"))
    matrix = P(("y", "x"), None)
    weights = (shard,) * 4 + (matrix, shard) * 4
    return jax.shard_map(
        shards,
        mesh=cut,
        in_specs=(both, P(("z", "core", "y", "x")), both) + weights,
        out_specs=(both, both) + weights,
        check_vma=False,
    )
```

```python
import functools

import jax
import jax.numpy as jnp
import numpy as np
from jax import lax
from jax.experimental import pallas as pl
from jax.experimental.pallas import tpu as pltpu
from jax.sharding import Mesh, PartitionSpec as P

D = 1024
H = 16
FF = 4096
HD = 64
ROT = 16
T = 1024
GROUP = 256
HEADS = GROUP // HD
ROWS = 256
EPSILON = 1e-05
MASKED = -1e30
BF = jnp.bfloat16
F32 = jnp.float32
VMEM = 60 * 2**20


def nn(a, b):
    return lax.dot_general(a, b, (((1,), (0,)), ((), ())), preferred_element_type=F32)


def nt(a, b):
    return lax.dot_general(a, b, (((1,), (1,)), ((), ())), preferred_element_type=F32)


def tn(a, b):
    return lax.dot_general(a, b, (((0,), (0,)), ((), ())), preferred_element_type=F32)


def rows_of(index, size):
    return slice(index * size, (index + 1) * size)


def rotary_tables():
    half = ROT // 2
    inverse = 1.0 / np.float32(10000.0) ** (np.arange(half, dtype=np.float32) * np.float32(2.0 / ROT))
    angles = np.arange(T, dtype=np.float32)[:, None] * inverse.astype(np.float32)[None, :]
    cosine = np.ones((T, HD), np.float32)
    ahead = np.zeros((T, HD), np.float32)
    behind = np.zeros((T, HD), np.float32)
    cosine[:, :half] = np.cos(angles)
    cosine[:, half:ROT] = np.cos(angles)
    ahead[:, :half] = -np.sin(angles)
    behind[:, half:ROT] = np.sin(angles)
    return [np.tile(table, (1, 2)) for table in (cosine, ahead, behind)]


def add_columns(ref, rows, value, order):
    width = value.shape[1] // len(order)
    for place, block in enumerate(order):
        ref[rows, rows_of(block, width)] += value[:, rows_of(place, width)]


def mlp_kernel(order, nm, gr, wi, bi, wo, out, dn, gwi, gwo, gbi, act, ig):
    @pl.when(pl.program_id(0) == 0)
    def _():
        out[...] = jnp.zeros_like(out)
        dn[...] = jnp.zeros_like(dn)

    bias_sum = jnp.zeros(gbi.shape, F32)
    for t in range(T // ROWS):
        r = rows_of(t, ROWS)
        inner = nn(nm[r, :], wi[...]) + bi[...]
        grad = nt(gr[r, :], wo[...])
        normal = 0.5 * lax.erf(inner * 0.7071067811865476) + 0.5
        slope = normal + inner * jnp.exp(-0.5 * inner * inner) * 0.3989422804014327
        act[r, :] = (inner * normal).astype(BF)
        inner_grad = (grad * slope).astype(BF)
        ig[r, :] = inner_grad
        bias_sum += jnp.sum(inner_grad.astype(F32), axis=0, keepdims=True)
    gbi[...] = bias_sum
    for t in range(T // ROWS):
        r = rows_of(t, ROWS)
        out[r, :] += nn(act[r, :], wo[...])
        add_columns(dn, r, nt(ig[r, :], wi[...]), order)
    for d in range(D // ROWS):
        r = rows_of(d, ROWS)
        gwi[r, :] = tn(nm[:, r], ig[...]).astype(BF)
    step = min(ROWS, act.shape[1])
    for f in range(act.shape[1] // step):
        r = rows_of(f, step)
        gwo[r, :] = tn(act[:, r], gr[...]).astype(BF)


def mlp(order, nm, gr, wi, bi, wo):
    tile = FF // len(order)
    half = len(order) // 2
    one = pl.Buffered(1)
    whole = lambda: pl.BlockSpec((T, D), lambda i: (0, 0), pipeline_mode=one)
    total = lambda: pl.BlockSpec((T, D), lambda i: (0, 0))
    columns = lambda rows: pl.BlockSpec((rows, tile), lambda i: (0, (i % half) * 2 + i // half))
    return pl.pallas_call(
        functools.partial(mlp_kernel, order),
        grid=(FF // tile,),
        in_specs=[whole(), whole(), columns(D), columns(1), pl.BlockSpec((tile, D), lambda i: (i, 0))],
        out_specs=[total(), total(), columns(D), pl.BlockSpec((tile, D), lambda i: (i, 0)), columns(1)],
        out_shape=[
            jax.ShapeDtypeStruct((T, D), F32),
            jax.ShapeDtypeStruct((T, D), F32),
            jax.ShapeDtypeStruct((D, FF), BF),
            jax.ShapeDtypeStruct((FF, D), BF),
            jax.ShapeDtypeStruct((1, FF), F32),
        ],
        scratch_shapes=[pltpu.VMEM((T, tile), BF), pltpu.VMEM((T, tile), BF)],
        compiler_params=pltpu.CompilerParams(vmem_limit_bytes=VMEM),
        cost_estimate=pl.CostEstimate(flops=12 * T * D * FF, bytes_accessed=60 * 2**20, transcendentals=2 * T * FF),
        name="mlp",
    )(nm, gr, wi, bi, wo)


def attn_kernel(
    order, length, na, gr, wq, wk, wv, bq, bk, bv, wd, cosine, ahead, behind,
    out, dn, gwq, gwk, gwv, gwd, gb,
    q, k, v, dc, ctx, dq, dk, dv, grads,
):
    @pl.when(pl.program_id(0) == 0)
    def _():
        out[...] = jnp.zeros_like(out)
        dn[...] = jnp.zeros_like(dn)

    def turn(x, r, back):
        parts = []
        for p in range(GROUP // 128):
            pair = x[:, rows_of(p, 128)]
            straight = pair * cosine[r, :]
            across = (
                pltpu.roll(pair, 128 - ROT // 2, 1) * ahead[r, :]
                + pltpu.roll(pair, ROT // 2, 1) * behind[r, :]
            )
            parts.append(straight - across if back else straight + across)
        return jnp.concatenate(parts, axis=1)

    for t in range(T // ROWS):
        r = rows_of(t, ROWS)
        x = na[r, :]
        queries = (turn(nn(x, wq[...]) + bq[...], r, False).astype(BF) * 0.125).astype(BF)
        keys = turn(nn(x, wk[...]) + bk[...], r, False).astype(BF)
        values = (nn(x, wv[...]) + bv[...]).astype(BF)
        context_grad = nt(gr[r, :], wd[...]).astype(BF)
        for h in range(HEADS):
            c = rows_of(h, HD)
            q[h, r, :] = queries[:, c]
            k[h, r, :] = keys[:, c]
            v[h, r, :] = values[:, c]
            dc[h, r, :] = context_grad[:, c]

    block = 256
    inside = lax.broadcasted_iota(jnp.int32, (1, T), 1) < length[0]
    bias = jnp.where(inside, 0.0, MASKED).astype(F32)
    below = lax.broadcasted_iota(jnp.int32, (block, block), 1) <= lax.broadcasted_iota(jnp.int32, (block, block), 0)
    causal = jnp.where(below, 0.0, MASKED).astype(F32)

    def head(h, carry):
        dk[h] = jnp.zeros((T, HD), F32)
        dv[h] = jnp.zeros((T, HD), F32)
        for i in range(T // block):
            r = rows_of(i, block)
            spans = ([slice(0, i * block)] if i else []) + [r]
            query = q[h, r, :]
            scores = [nt(query, k[h, c, :]) + bias[:, c] for c in spans]
            scores[-1] += causal
            top = functools.reduce(jnp.maximum, [jnp.max(s, axis=1, keepdims=True) for s in scores])
            weights = [jnp.exp(s - top) for s in scores]
            scale = 1.0 / sum(jnp.sum(w, axis=1, keepdims=True) for w in weights)
            low = [w.astype(BF) for w in weights]
            context = sum(nn(w, v[h, c, :]) for w, c in zip(low, spans))
            ctx[h, r, :] = (context * scale).astype(BF)
            scaled_grad = (dc[h, r, :].astype(F32) * scale).astype(BF)
            probs_grad = [nt(scaled_grad, v[h, c, :]) for c in spans]
            inner = scale * sum(jnp.sum(w * p, axis=1, keepdims=True) for w, p in zip(weights, probs_grad))
            score_grad = [(w * (p - inner)).astype(BF) for w, p in zip(weights, probs_grad)]
            dq[h, r, :] = sum(nn(s, k[h, c, :]) for s, c in zip(score_grad, spans))
            for s, w, c in zip(score_grad, low, spans):
                dk[h, c, :] += tn(s, query)
                dv[h, c, :] += tn(w, scaled_grad)
        return carry

    lax.fori_loop(0, HEADS, head, 0)

    sums = [jnp.zeros((1, GROUP), F32) for _ in range(3)]
    together = lambda ref, r: jnp.concatenate([ref[h, r, :] for h in range(HEADS)], axis=1)
    for t in range(T // ROWS):
        r = rows_of(t, ROWS)
        context = together(ctx, r)
        grads[r, 3 * GROUP :] = context
        out[r, :] += nn(context, wd[...])
        pieces = (
            turn(together(dq, r) * 0.125, r, True).astype(BF),
            turn(together(dk, r), r, True).astype(BF),
            together(dv, r).astype(BF),
        )
        for p, piece in enumerate(pieces):
            grads[r, rows_of(p, GROUP)] = piece
            sums[p] += jnp.sum(piece.astype(F32), axis=0, keepdims=True)
        normed_grad = sum(nt(piece, w[...]) for piece, w in zip(pieces, (wq, wk, wv)))
        add_columns(dn, r, normed_grad, order)
    for p in range(3):
        gb[p : p + 1, :] = sums[p]
    for d in range(D // ROWS):
        r = rows_of(d, ROWS)
        x = na[:, r]
        for p, g in enumerate((gwq, gwk, gwv)):
            g[r, :] = tn(x, grads[:, rows_of(p, GROUP)]).astype(BF)
    gwd[...] = tn(grads[:, 3 * GROUP :], gr[...]).astype(BF)


def attn(order, length, na, gr, weight, bias, wd):
    groups = D // GROUP
    one = pl.Buffered(1)
    whole = lambda shape: pl.BlockSpec(shape, lambda i: (0, 0), pipeline_mode=one)
    total = lambda: pl.BlockSpec((T, D), lambda i: (0, 0))
    columns = lambda rows, part=0: pl.BlockSpec((rows, GROUP), lambda i: (0, i + part * groups))
    head_rows = lambda dtype: pltpu.VMEM((HEADS, T, HD), dtype)
    return pl.pallas_call(
        functools.partial(attn_kernel, order),
        grid=(groups,),
        in_specs=[pl.BlockSpec(memory_space=pltpu.SMEM), whole((T, D)), whole((T, D))]
        + [columns(D, p) for p in range(3)]
        + [columns(1, p) for p in range(3)]
        + [pl.BlockSpec((GROUP, D), lambda i: (i, 0))]
        + [whole((T, 128))] * 3,
        out_specs=[total(), total()] + [columns(D)] * 3 + [pl.BlockSpec((GROUP, D), lambda i: (i, 0)), columns(3)],
        out_shape=[jax.ShapeDtypeStruct((T, D), F32)] * 2
        + [jax.ShapeDtypeStruct((D, D), BF)] * 4
        + [jax.ShapeDtypeStruct((3, D), F32)],
        scratch_shapes=[head_rows(BF)] * 5 + [head_rows(F32)] * 3 + [pltpu.VMEM((T, 4 * GROUP), BF)],
        compiler_params=pltpu.CompilerParams(vmem_limit_bytes=VMEM),
        cost_estimate=pl.CostEstimate(flops=90 * 10**9, bytes_accessed=40 * 2**20, transcendentals=10 * 2**20),
        name="attn",
    )(length, na, gr, weight, weight, weight, bias, bias, bias, wd, *map(jnp.asarray, rotary_tables()))


def general_shards(
    layer_input, seq_lengths, out_grad, attn_gain, attn_shift, mlp_gain, mlp_shift, qkv_weight, qkv_bias,
    dense_weight, dense_bias, inner_weight, inner_bias, outer_weight, outer_bias,
):
    groupings = ("core", "y", "x")
    shard_count = lax.axis_size("y") * lax.axis_size("x")
    core = lax.axis_index("core")
    order = [2 * a + h for h in range(2) for a in range(shard_count)]

    def gather(piece):
        half = piece.shape[0] // 2
        mine = lax.dynamic_slice_in_dim(piece, core * half, half, 0)
        return lax.all_gather(mine, groupings, axis=0, tiled=True)

    def natural(rows):
        return jnp.swapaxes(rows.reshape(2, shard_count, -1, rows.shape[1]), 0, 1).reshape(rows.shape)

    def halves_first(rows):
        return jnp.swapaxes(rows.reshape(shard_count, 2, -1, rows.shape[1]), 0, 1).reshape(rows.shape)

    vectors = jnp.concatenate(
        [attn_gain, attn_shift, mlp_gain, mlp_shift, dense_bias, outer_bias, qkv_bias, inner_bias]
    )
    vectors = lax.all_gather(vectors, ("y", "x"), axis=0, tiled=False).astype(F32)
    sizes = [D] * 6 + [3 * D, FF]
    cuts = np.cumsum([size // shard_count for size in sizes])[:-1]
    gain_a, shift_a, gain_m, shift_m, bias_d, bias_o, bias_qkv, bias_i = (
        part.reshape(1, -1) for part in jnp.split(vectors, cuts, axis=1)
    )
    wi = gather(inner_weight)
    wo = gather(outer_weight)
    wqkv = gather(qkv_weight)
    wd = natural(gather(dense_weight))

    x = layer_input.astype(F32)
    mean = jnp.mean(x, axis=1, keepdims=True)
    centered = x - mean
    inverse = lax.rsqrt(jnp.mean(centered * centered, axis=1, keepdims=True) + EPSILON)
    unit = centered * inverse
    valid = jnp.arange(T, dtype=jnp.int32)[:, None] < seq_lengths[0]
    gr = jnp.where(valid, out_grad, jnp.zeros_like(out_grad))
    blocked = lambda rows: jnp.swapaxes(rows.reshape(T, shard_count, 2, -1), 1, 2).reshape(T, D)
    nm = blocked((unit * gain_m + shift_m).astype(BF))
    na = blocked((unit * gain_a + shift_a).astype(BF))

    out_m, dnm, gwi, gwo, gbi = mlp(order, nm, gr, wi, bias_i, wo)
    out_a, dna, gwq, gwk, gwv, gwd, gbqkv = attn(order, seq_lengths, na, gr, wqkv, bias_qkv, wd)

    def reduce(grad):
        part = lax.psum_scatter(grad, "core", scatter_dimension=0, tiled=True)
        part = lax.psum_scatter(part, ("y", "x"), scatter_dimension=0, tiled=True)
        part = lax.psum(part, "z")
        return lax.all_gather(part, "core", axis=0, tiled=True).astype(F32)

    grad_wi = reduce(gwi)
    grad_wo = reduce(gwo)
    grad_d = reduce(halves_first(gwd))
    grad_qkv = jnp.concatenate([reduce(g) for g in (gwq, gwk, gwv)], axis=1)

    layer_output = x + out_m + out_a + (bias_d + bias_o)
    g = dna * gain_a + dnm * gain_m
    gr32 = gr.astype(F32)
    input_grad = gr32 + inverse * (
        g - jnp.mean(g, axis=1, keepdims=True) - unit * jnp.mean(g * unit, axis=1, keepdims=True)
    )
    column = lambda rows: jnp.sum(rows, axis=0)
    parts = [column(dna * unit), column(dna), column(dnm * unit), column(dnm), column(gr32), gbqkv, gbi]
    small = jnp.concatenate([p.reshape(shard_count, -1) for p in parts], axis=1)
    small = lax.psum_scatter(small, ("y", "x"), scatter_dimension=0, tiled=True)
    small = lax.psum(small, ("z", "core"))
    cuts = np.cumsum([size // shard_count for size in [D] * 5 + [3 * D, FF]])[:-1]
    g_ga, g_sa, g_gm, g_sm, g_bd, g_bqkv, g_bi = (p.reshape(-1) for p in jnp.split(small, cuts, axis=1))
    return (
        layer_output, input_grad, g_ga, g_sa, g_gm, g_sm, grad_qkv, g_bqkv, grad_d, g_bd, grad_wi, g_bi, grad_wo, g_bd,
    )


WIDE = 512
VMEM_UNIT = 56 * 2**20
LONG = pl.CostEstimate(flops=10**13, bytes_accessed=2**20, transcendentals=0)


def columns_at(start, size):
    return pl.ds(pl.multiple_of(start, 128), size)


def norm_kernel(table, x, grad, gain_a, shift_a, gain_m, shift_m, na, nm, gr):
    values = x[...].astype(F32)
    mean = jnp.mean(values, axis=1, keepdims=True)
    centered = values - mean
    unit = centered * lax.rsqrt(jnp.mean(centered * centered, axis=1, keepdims=True) + EPSILON)
    rows = x.shape[0]
    position = pl.program_id(0) * rows + lax.broadcasted_iota(jnp.int32, (rows, 1), 0)
    gr[...] = jnp.where(position < table[1], grad[...].astype(F32), 0.0).astype(BF)
    for out, gain, shift in ((na, gain_a, shift_a), (nm, gain_m, shift_m)):
        normed = (unit * gain[...] + shift[...]).astype(BF)
        for a in range(4):
            for h in range(2):
                place = (table[2 + a] * 2 + (table[0] ^ h)) * 128
                out[:, columns_at(place, 128)] = normed[:, rows_of(a * 2 + h, 128)]


def norm(table, x, grad, vectors):
    tile = pl.BlockSpec((ROWS, D), lambda i: (i, 0))
    row = pl.BlockSpec((1, D), lambda i: (0, 0))
    return pl.pallas_call(
        norm_kernel,
        grid=(T // ROWS,),
        in_specs=[pl.BlockSpec(memory_space=pltpu.SMEM), tile, tile] + [row] * 4,
        out_specs=[tile] * 3,
        out_shape=[jax.ShapeDtypeStruct((T, D), BF)] * 3,
        compiler_params=pltpu.CompilerParams(vmem_limit_bytes=VMEM),
        cost_estimate=pl.CostEstimate(flops=10 * T * D, bytes_accessed=10 * T * D, transcendentals=T),
        name="norm",
    )(table, x, grad, *vectors)


def output_kernel(x, out, bias, layer_output):
    layer_output[...] = x[...].astype(F32) + out[...] + bias[...]


def output(x, out, bias):
    tile = pl.BlockSpec((ROWS, D), lambda i: (i, 0))
    row = pl.BlockSpec((1, D), lambda i: (0, 0))
    return pl.pallas_call(
        output_kernel,
        grid=(T // ROWS,),
        in_specs=[tile, tile, row],
        out_specs=tile,
        out_shape=jax.ShapeDtypeStruct((T, D), F32),
        cost_estimate=LONG,
        name="output",
    )(x, out, bias)


def finish_kernel(table, x, gr, dna, dnm, gain_a, gain_m, *refs):
    *bias_sums, input_grad, small, sums = refs
    values = x[...].astype(F32)
    mean = jnp.mean(values, axis=1, keepdims=True)
    centered = values - mean
    inverse = lax.rsqrt(jnp.mean(centered * centered, axis=1, keepdims=True) + EPSILON)
    unit = centered * inverse

    def natural(ref):
        places = [(table[2 + a] * 2 + (table[0] ^ h)) * 128 for a in range(4) for h in range(2)]
        return jnp.concatenate([ref[:, columns_at(place, 128)] for place in places], axis=1)

    normed_a, normed_m = natural(dna), natural(dnm)
    upper = gr[...].astype(F32)
    g = normed_a * gain_a[...] + normed_m * gain_m[...]
    input_grad[...] = upper + inverse * (
        g - jnp.mean(g, axis=1, keepdims=True) - unit * jnp.mean(g * unit, axis=1, keepdims=True)
    )

    @pl.when(pl.program_id(0) == 0)
    def _():
        sums[...] = jnp.zeros_like(sums)

    for i, rows in enumerate((normed_a * unit, normed_a, normed_m * unit, normed_m, upper)):
        sums[i : i + 1, :] += jnp.sum(rows, axis=0, keepdims=True)

    @pl.when(pl.program_id(0) == T // ROWS - 1)
    def _():
        for i in range(5):
            for a in range(4):
                small[a : a + 1, rows_of(i, 256)] = sums[i : i + 1, rows_of(a, 256)]
        *pairs, first_unit, second_unit = bias_sums
        for pair in range(2):
            for a, b in qkv_blocks(pair):
                small[a // 768 : a // 768 + 1, pl.ds(1280 + a % 768, 128)] = pairs[pair][:, pl.ds(b, 128)]
        for unit_index, value in enumerate((first_unit, second_unit)):
            for a in range(4):
                small[a : a + 1, pl.ds(2048 + unit_index * 512, 512)] = value[:, rows_of(a, 512)]


def finish(table, x, gr, dna, dnm, vectors, bias_sums):
    tile = pl.BlockSpec((ROWS, D), lambda i: (i, 0))
    row = lambda value: pl.BlockSpec(value.shape, lambda i: (0, 0))
    return pl.pallas_call(
        finish_kernel,
        grid=(T // ROWS,),
        in_specs=[pl.BlockSpec(memory_space=pltpu.SMEM)] + [tile] * 4 + [row(v) for v in (*vectors, *bias_sums)],
        out_specs=[tile, pl.BlockSpec((4, 3072), lambda i: (0, 0))],
        out_shape=[jax.ShapeDtypeStruct((T, D), F32), jax.ShapeDtypeStruct((4, 3072), F32)],
        scratch_shapes=[pltpu.VMEM((5, D), F32)],
        compiler_params=pltpu.CompilerParams(vmem_limit_bytes=VMEM),
        cost_estimate=LONG,
        name="finish",
    )(table, x, gr, dna, dnm, *vectors, *bias_sums)


class Totals:
    def __init__(self, refs_in, refs_out, scratch, sems):
        self.fresh = [ref is None for ref in refs_in]
        self.refs_in, self.refs_out, self.scratch, self.sems = refs_in, refs_out, scratch, sems

    def loads(self):
        return [
            pltpu.make_async_copy(source, self.scratch[i], self.sems.at[i])
            for i, source in enumerate(self.refs_in)
            if source is not None
        ]

    def stores(self):
        return [
            pltpu.make_async_copy(source, target, self.sems.at[i])
            for i, (source, target) in enumerate(zip(self.scratch, self.refs_out))
        ]

    def begin(self):
        for copy in self.loads():
            copy.start()
        for target, source in zip(self.scratch, self.refs_in):
            if source is None:
                target[...] = jnp.zeros_like(target)

    def ready(self):
        for copy in self.loads():
            copy.wait()


def start_all(copies):
    for copy in copies:
        copy.start()


def wait_all(copies):
    for copy in copies:
        copy.wait()


def mlp_unit_kernel(first, count, given, table, nm, gr, bi, pieces, *refs):
    refs = list(refs)
    olds = [refs.pop(0) if is_given else None for is_given in given]
    keep, send, gbi, out_ref, dn_ref, wi, wo, act, ig, out, dn, inner_stage, outer_stage, sems, out_sems, total_sems = refs
    step = pl.program_id(0)
    core = table[0]
    totals = Totals(olds[2:], (out_ref, dn_ref), (out, dn), total_sems)

    def copies(index):
        slot, tile = index % 2, first + index
        made = []
        for t in range(4):
            for half in range(2):
                piece = (core ^ half) * 4 + table[6 + t]
                source = pieces.at[piece, 0, :, columns_at(tile * WIDE, WIDE)]
                made.append((source, wi.at[slot, pl.ds(t * 256 + half * 128, 128), :]))
        for h in range(2):
            for part in range(2):
                source = pieces.at[h * 4 + tile, 1, :, pl.ds(part * D, D)]
                made.append((source, wo.at[slot, pl.ds(h * 256 + part * 128, 128), :]))
        return [pltpu.make_async_copy(a, b, sems.at[slot, i]) for i, (a, b) in enumerate(made)]

    def results(index):
        slot, tile = index % 2, first + index
        made = []
        for side, target in enumerate((keep, send)):
            inner_part = target.at[:, pl.ds(pl.multiple_of(tile // 2 * 128, 128), 128), columns_at((tile % 2) * WIDE, WIDE)]
            made.append((inner_stage.at[slot, side], inner_part))
            made.append((outer_stage.at[slot, side], target.at[table[2 + tile], pl.ds(256, 256)]))
        return [pltpu.make_async_copy(a, b, out_sems.at[slot, i]) for i, (a, b) in enumerate(made)]

    @pl.when(step == 0)
    def _():
        start_all(copies(step))
        totals.begin()

    @pl.when(step < count - 1)
    def _():
        start_all(copies(step + 1))

    wait_all(copies(step))
    slot = step % 2

    bias_sum = jnp.zeros(gbi.shape, F32)
    for t in range(T // ROWS):
        r = rows_of(t, ROWS)
        inner = nn(nm[r, :], wi[slot]) + bi[...]
        grad = nt(gr[r, :], wo[slot])
        normal = 0.5 * lax.erf(inner * 0.7071067811865476) + 0.5
        slope = normal + inner * jnp.exp(-0.5 * inner * inner) * 0.3989422804014327
        act[r, :] = (inner * normal).astype(BF)
        inner_grad = (grad * slope).astype(BF)
        ig[r, :] = inner_grad
        bias_sum += jnp.sum(inner_grad.astype(F32), axis=0, keepdims=True)
    gbi[...] = bias_sum

    @pl.when(step == 0)
    def _():
        totals.ready()

    for t in range(T // ROWS):
        r = rows_of(t, ROWS)
        out[r, :] += nn(act[r, :], wo[slot])
        dn[r, :] += nt(ig[r, :], wi[slot])

    @pl.when(step == count - 1)
    def _():
        start_all(totals.stores())

    if count > 2:

        @pl.when(step >= 2)
        def _():
            wait_all(results(step - 2))

    for t in range(4):
        grad = tn(nm[:, rows_of(t, 256)], ig[...]).astype(BF)
        inner_stage[slot, 0, t] = grad[:128]
        inner_stage[slot, 1, t] = grad[128:]
    for f in range(2):
        grad = tn(act[:, rows_of(f, 256)], gr[...])
        low, high = grad[:, :WIDE], grad[:, WIDE:]
        sides = (jnp.where(core == 0, low, high).astype(BF), jnp.where(core == 0, high, low).astype(BF))
        for side, value in enumerate(sides):
            for half in range(2):
                outer_stage[slot, side, rows_of(f, 128), rows_of(half, WIDE)] = value[rows_of(half, 128)]
    start_all(results(step))

    @pl.when(step == count - 1)
    def _():
        if count > 1:
            wait_all(results(step - 1))
        wait_all(results(step))
        wait_all(totals.stores())


def mlp_unit(first, count, table, nm, gr, bi, pieces, parts, totals):
    olds = list(parts) + list(totals)
    given = tuple(old is not None for old in olds)
    inputs = [old for old in olds if old is not None]
    aliases = {5 + n: (0, 1, 3, 4)[i] for n, i in enumerate(i for i in range(4) if given[i])}
    whole = pl.BlockSpec((T, D), lambda i: (0, 0), pipeline_mode=pl.Buffered(1))
    anywhere = pl.BlockSpec(memory_space=pl.ANY)
    return pl.pallas_call(
        functools.partial(mlp_unit_kernel, first, count, given),
        grid=(count,),
        in_specs=[pl.BlockSpec(memory_space=pltpu.SMEM), whole, whole, pl.BlockSpec((1, WIDE), lambda i: (0, first + i)), anywhere]
        + [anywhere] * len(inputs),
        out_specs=[anywhere, anywhere, pl.BlockSpec((1, WIDE), lambda i: (0, i)), anywhere, anywhere],
        out_shape=[jax.ShapeDtypeStruct((4, 512, D), BF)] * 2
        + [jax.ShapeDtypeStruct((1, count * WIDE), F32)]
        + [jax.ShapeDtypeStruct((T, D), F32)] * 2,
        input_output_aliases=aliases,
        scratch_shapes=[
            pltpu.VMEM((2, D, WIDE), BF),
            pltpu.VMEM((2, WIDE, D), BF),
            pltpu.VMEM((T, WIDE), BF),
            pltpu.VMEM((T, WIDE), BF),
            pltpu.VMEM((T, D), F32),
            pltpu.VMEM((T, D), F32),
            pltpu.VMEM((2, 2, 4, 128, WIDE), BF),
            pltpu.VMEM((2, 2, 256, D), BF),
            pltpu.SemaphoreType.DMA((2, 12)),
            pltpu.SemaphoreType.DMA((2, 4)),
            pltpu.SemaphoreType.DMA((2,)),
        ],
        compiler_params=pltpu.CompilerParams(vmem_limit_bytes=VMEM_UNIT),
        cost_estimate=LONG,
        name="mlp_unit",
    )(table, nm, gr, bi, pieces, *inputs)


def attn_unit_kernel(first, count, given, table, na, gr, bias, cosine, ahead, behind, pieces, *refs):
    refs = list(refs)
    olds = [refs.pop(0) if is_given else None for is_given in given]
    (
        keep, send, gb, out_ref, dn_ref,
        w, wd, q, k, v, dc, ctx, dq, dk, dv, grads, out, dn, qkv_stage, dense_stage, sems, out_sems, total_sems,
    ) = refs
    step = pl.program_id(0)
    core = table[0]
    totals = Totals(olds[2:], (out_ref, dn_ref), (out, dn), total_sems)

    def copies(index):
        group = first + index
        made = []
        for t in range(4):
            for half in range(2):
                piece = (core ^ half) * 4 + table[6 + t]
                source = pieces.at[piece, :, columns_at(group * 768, 768)]
                made.append((source, w.at[index, pl.ds(t * 256 + half * 128, 128), :]))
        for pair in range(2):
            for h in range(2):
                source = pieces.at[h * 4 + group * 2 + pair, :, pl.ds(1536, 512)]
                made.append((source, wd.at[index, pl.ds(pair * 128, 128), pl.ds(h * 512, 512)]))
        return [pltpu.make_async_copy(a, b, sems.at[index, i]) for i, (a, b) in enumerate(made)]

    def results(index):
        group = first + index
        made = []
        for side, target in enumerate((keep, send)):
            made.append((qkv_stage.at[index, side], target.at[:, :, columns_at(group * 768, 768)]))
            for pair in range(2):
                place = target.at[table[2 + group * 2 + pair], :, pl.ds(1536, 512)]
                made.append((dense_stage.at[index, side, pair], place))
        return [pltpu.make_async_copy(a, b, out_sems.at[index, i]) for i, (a, b) in enumerate(made)]

    @pl.when(step == 0)
    def _():
        for index in range(count):
            start_all(copies(index))
        totals.begin()

    wait_all(copies(step))

    def turn(x, r, back):
        parts = []
        for p in range(GROUP // 128):
            pair = x[:, rows_of(p, 128)]
            straight = pair * cosine[r, :]
            across = (
                pltpu.roll(pair, 128 - ROT // 2, 1) * ahead[r, :]
                + pltpu.roll(pair, ROT // 2, 1) * behind[r, :]
            )
            parts.append(straight - across if back else straight + across)
        return jnp.concatenate(parts, axis=1)

    part = [slice(p * GROUP, (p + 1) * GROUP) for p in range(4)]
    for t in range(T // ROWS):
        r = rows_of(t, ROWS)
        x = na[r, :]
        projected = nn(x, w[step]) + bias[...]
        queries = (turn(projected[:, part[0]], r, False).astype(BF) * 0.125).astype(BF)
        keys = turn(projected[:, part[1]], r, False).astype(BF)
        values = projected[:, part[2]].astype(BF)
        context_grad = nt(gr[r, :], wd[step]).astype(BF)
        for h in range(HEADS):
            c = rows_of(h, HD)
            q[h, r, :] = queries[:, c]
            k[h, r, :] = keys[:, c]
            v[h, r, :] = values[:, c]
            dc[h, r, :] = context_grad[:, c]

    block = 256
    inside = lax.broadcasted_iota(jnp.int32, (1, T), 1) < table[1]
    outside = jnp.where(inside, 0.0, MASKED).astype(F32)
    below = lax.broadcasted_iota(jnp.int32, (block, block), 1) <= lax.broadcasted_iota(jnp.int32, (block, block), 0)
    causal = jnp.where(below, 0.0, MASKED).astype(F32)

    def head(h, carry):
        dk[h] = jnp.zeros((T, HD), F32)
        dv[h] = jnp.zeros((T, HD), F32)
        for i in range(T // block):
            r = rows_of(i, block)
            spans = ([slice(0, i * block)] if i else []) + [r]
            query = q[h, r, :]
            scores = [nt(query, k[h, c, :]) + outside[:, c] for c in spans]
            scores[-1] += causal
            top = functools.reduce(jnp.maximum, [jnp.max(s, axis=1, keepdims=True) for s in scores])
            weights = [jnp.exp(s - top) for s in scores]
            scale = 1.0 / sum(jnp.sum(e, axis=1, keepdims=True) for e in weights)
            low = [e.astype(BF) for e in weights]
            context = sum(nn(e, v[h, c, :]) for e, c in zip(low, spans))
            ctx[h, r, :] = (context * scale).astype(BF)
            scaled_grad = (dc[h, r, :].astype(F32) * scale).astype(BF)
            probs_grad = [nt(scaled_grad, v[h, c, :]) for c in spans]
            inner = scale * sum(jnp.sum(e * p, axis=1, keepdims=True) for e, p in zip(weights, probs_grad))
            score_grad = [(e * (p - inner)).astype(BF) for e, p in zip(weights, probs_grad)]
            dq[h, r, :] = sum(nn(s, k[h, c, :]) for s, c in zip(score_grad, spans))
            for s, e, c in zip(score_grad, low, spans):
                dk[h, c, :] += tn(s, query)
                dv[h, c, :] += tn(e, scaled_grad)
        return carry

    lax.fori_loop(0, HEADS, head, 0)

    @pl.when(step == 0)
    def _():
        totals.ready()

    sums = jnp.zeros((1, 3 * GROUP), F32)
    together = lambda ref, r: jnp.concatenate([ref[h, r, :] for h in range(HEADS)], axis=1)
    for t in range(T // ROWS):
        r = rows_of(t, ROWS)
        context = together(ctx, r)
        grads[r, part[3]] = context
        out[r, :] += nn(context, wd[step])
        projected_grad = jnp.concatenate(
            [
                turn(together(dq, r) * 0.125, r, True).astype(BF),
                turn(together(dk, r), r, True).astype(BF),
                together(dv, r).astype(BF),
            ],
            axis=1,
        )
        grads[r, : 3 * GROUP] = projected_grad
        sums += jnp.sum(projected_grad.astype(F32), axis=0, keepdims=True)
        dn[r, :] += nt(projected_grad, w[step])
    gb[...] = sums

    @pl.when(step == count - 1)
    def _():
        start_all(totals.stores())

    for t in range(4):
        grad = tn(na[:, rows_of(t, 256)], grads[:, : 3 * GROUP]).astype(BF)
        qkv_stage[step, 0, t] = grad[:128]
        qkv_stage[step, 1, t] = grad[128:]
    grad = tn(grads[:, part[3]], gr[...])
    first_half, second_half = grad[:, :WIDE], grad[:, WIDE:]
    sides = (
        jnp.where(core == 0, first_half, second_half).astype(BF),
        jnp.where(core == 0, second_half, first_half).astype(BF),
    )
    for side, value in enumerate(sides):
        for pair in range(2):
            dense_stage[step, side, pair] = value[rows_of(pair, 128)]
    start_all(results(step))

    @pl.when(step == count - 1)
    def _():
        for index in range(count):
            wait_all(results(index))
        wait_all(totals.stores())


def attn_unit(first, count, table, na, gr, bias, tables, pieces, parts, totals):
    olds = list(parts) + list(totals)
    given = tuple(old is not None for old in olds)
    inputs = [old for old in olds if old is not None]
    aliases = {8 + n: (0, 1, 3, 4)[i] for n, i in enumerate(i for i in range(4) if given[i])}
    one = pl.Buffered(1)
    whole = pl.BlockSpec((T, D), lambda i: (0, 0), pipeline_mode=one)
    turns = pl.BlockSpec((T, 128), lambda i: (0, 0), pipeline_mode=one)
    anywhere = pl.BlockSpec(memory_space=pl.ANY)
    head_rows = lambda dtype: pltpu.VMEM((HEADS, T, HD), dtype)
    return pl.pallas_call(
        functools.partial(attn_unit_kernel, first, count, given),
        grid=(count,),
        in_specs=[pl.BlockSpec(memory_space=pltpu.SMEM), whole, whole, pl.BlockSpec((1, 3 * GROUP), lambda i: (0, first + i))]
        + [turns] * 3
        + [anywhere] * (1 + len(inputs)),
        out_specs=[anywhere, anywhere, pl.BlockSpec((1, 3 * GROUP), lambda i: (0, i)), anywhere, anywhere],
        out_shape=[jax.ShapeDtypeStruct((4, 128, 2 * D), BF)] * 2
        + [jax.ShapeDtypeStruct((1, 3 * GROUP * count), F32)]
        + [jax.ShapeDtypeStruct((T, D), F32)] * 2,
        input_output_aliases=aliases,
        scratch_shapes=[pltpu.VMEM((count, D, 3 * GROUP), BF), pltpu.VMEM((count, GROUP, D), BF)]
        + [head_rows(BF)] * 5
        + [head_rows(F32)] * 3
        + [
            pltpu.VMEM((T, 4 * GROUP), BF),
            pltpu.VMEM((T, D), F32),
            pltpu.VMEM((T, D), F32),
            pltpu.VMEM((count, 2, 4, 128, 3 * GROUP), BF),
            pltpu.VMEM((count, 2, 2, 128, WIDE), BF),
            pltpu.SemaphoreType.DMA((count, 12)),
            pltpu.SemaphoreType.DMA((count, 6)),
            pltpu.SemaphoreType.DMA((2,)),
        ],
        compiler_params=pltpu.CompilerParams(vmem_limit_bytes=VMEM_UNIT),
        cost_estimate=LONG,
        name="attn_unit",
    )(table, na, gr, bias, *tables, pieces, *inputs)


def qkv_blocks(pair):
    return [
        (part * D + (2 * group + shard) * 256 + pair * 128, group * 768 + part * 256 + shard * 128)
        for group in range(2)
        for part in range(3)
        for shard in range(2)
    ]


def attn_pack_kernel(pair, table, qkv, dense, piece, sems):
    core = table[0]
    rows = pl.ds(pl.multiple_of(core * 128, 128), 128)
    made = [(qkv.at[rows, pl.ds(a, 128)], piece.at[0, :, pl.ds(b, 128)]) for a, b in qkv_blocks(pair)]
    made.append((dense.at[pl.ds(pair * 128, 128), columns_at(core * 512, 512)], piece.at[0, :, pl.ds(1536, 512)]))
    copies = [pltpu.make_async_copy(a, b, sems.at[i]) for i, (a, b) in enumerate(made)]
    start_all(copies)
    wait_all(copies)


def mlp_pack_kernel(unit, table, inner, outer, piece, sems):
    core = table[0]
    rows = pl.ds(pl.multiple_of(core * 128, 128), 128)
    made = [(inner.at[rows, pl.ds(a * 1024 + unit * 512, 512)], piece.at[0, 0, :, pl.ds(a * 512, 512)]) for a in range(4)]
    for part in range(2):
        source = outer.at[pl.ds(pl.multiple_of(unit * 512 + core * 256 + part * 128, 128), 128), :]
        made.append((source, piece.at[0, 1, :, pl.ds(part * D, D)]))
    copies = [pltpu.make_async_copy(a, b, sems.at[i]) for i, (a, b) in enumerate(made)]
    start_all(copies)
    wait_all(copies)


def pack(kernel, shape, count, name, table, *weights):
    anywhere = pl.BlockSpec(memory_space=pl.ANY)
    return pl.pallas_call(
        kernel,
        in_specs=[pl.BlockSpec(memory_space=pltpu.SMEM)] + [anywhere] * len(weights),
        out_specs=pl.BlockSpec(memory_space=pltpu.VMEM),
        out_shape=jax.ShapeDtypeStruct(shape, BF),
        scratch_shapes=[pltpu.SemaphoreType.DMA((count,))],
        name=name,
    )(table, *weights)


def attn_place_kernel(table, *refs):
    *values, grad_qkv, grad_d = refs
    core = table[0]
    for pair in range(2):
        for side in range(2):
            value = values[pair * 2 + side]
            half = core ^ side
            rows = pl.ds(pl.multiple_of(half * 128, 128), 128)
            for a, b in qkv_blocks(pair):
                grad_qkv[rows, pl.ds(a, 128)] = value[0, :, pl.ds(b, 128)].astype(F32)
            grad_d[rows_of(pair, 128), columns_at(half * 512, 512)] = value[0, :, pl.ds(1536, 512)].astype(F32)


def mlp_place_kernel(table, *refs):
    *values, grad_wi, grad_wo = refs
    core = table[0]
    for unit in range(2):
        for side in range(2):
            value = values[unit * 2 + side]
            half = core ^ side
            rows = pl.ds(pl.multiple_of(half * 128, 128), 128)
            for tile in range(4):
                grad_wi[rows, pl.ds(tile * 1024 + unit * 512, 512)] = value[0, rows_of(tile // 2, 128), rows_of(tile % 2, 512)].astype(F32)
            for f in range(2):
                for part in range(2):
                    target = pl.ds(unit * 512 + f * 256 + part * 128, 128)
                    grad_wo[target, columns_at(half * 512, 512)] = value[0, rows_of(2 + f, 128), rows_of(part, 512)].astype(F32)


def place(kernel, shapes, name, table, *values):
    inside = pl.BlockSpec(memory_space=pltpu.VMEM)
    return pl.pallas_call(
        kernel,
        in_specs=[pl.BlockSpec(memory_space=pltpu.SMEM)] + [inside] * len(values),
        out_specs=[inside] * len(shapes),
        out_shape=[jax.ShapeDtypeStruct(shape, F32) for shape in shapes],
        compiler_params=pltpu.CompilerParams(vmem_limit_bytes=VMEM),
        name=name,
    )(table, *values)


def add_kernel(*refs):
    *sources, target = refs
    target[...] = sum(source[...].astype(F32) for source in sources).astype(BF)


def add(*sources, count=1):
    rows, columns = sources[0][0].shape[1:]
    steps = 2
    read = lambda first, stride: pl.BlockSpec(
        (1, rows // steps, columns), lambda i: (first + stride * (i // steps), i % steps, 0)
    )
    return pl.pallas_call(
        add_kernel,
        grid=(count * steps,),
        in_specs=[read(first, stride) for _, first, stride in sources],
        out_specs=read(0, 1),
        out_shape=jax.ShapeDtypeStruct((count, rows, columns), BF),
        cost_estimate=LONG,
        name="add",
    )(*(array for array, _, _ in sources))


def split_add_kernel(*refs):
    *sources, first, second = refs
    total = sum(source[...].astype(F32) for source in sources).astype(BF)
    half = total.shape[1] // 2
    first[...] = total[:, :half]
    second[...] = total[:, half:]


def split_add(*arrays):
    rows, columns = arrays[0].shape[1:]
    return pl.pallas_call(
        split_add_kernel,
        grid=(1,),
        in_specs=[pl.BlockSpec((1, rows, columns), lambda i: (0, 0, 0))] * len(arrays),
        out_specs=[pl.BlockSpec((1, rows // 2, columns), lambda i: (0, 0, 0))] * 2,
        out_shape=[jax.ShapeDtypeStruct((1, rows // 2, columns), BF)] * 2,
        cost_estimate=LONG,
        name="split_add",
    )(*arrays)


def pair_add_kernel(first, got_first, second, got_second, first_out, second_out):
    first_out[...] = (first[...].astype(F32) + got_first[...].astype(F32)).astype(BF)
    second_out[...] = (second[...].astype(F32) + got_second[...].astype(F32)).astype(BF)


def join_add_kernel(first, got_first, second, got_second, total):
    half = first.shape[1]
    total[:, :half] = (first[...].astype(F32) + got_first[...].astype(F32)).astype(BF)
    total[:, half:] = (second[...].astype(F32) + got_second[...].astype(F32)).astype(BF)


def halves_add(first, got_first, second, got_second, join=False):
    block = lambda shape: pl.BlockSpec(shape, lambda i: (0, 0, 0))
    one, rows, columns = first.shape
    shapes = [(one, rows * 2, columns)] if join else [first.shape] * 2
    return pl.pallas_call(
        join_add_kernel if join else pair_add_kernel,
        grid=(1,),
        in_specs=[block(first.shape)] * 4,
        out_specs=[block(shape) for shape in shapes],
        out_shape=[jax.ShapeDtypeStruct(shape, BF) for shape in shapes],
        cost_estimate=LONG,
        name="halves_add",
    )(first, got_first, second, got_second)


AXES = ("z", "core", "y", "x")


def exchange(value, partner):
    pairs = []
    for z in range(4):
        for core in range(2):
            for shard in range(4):
                to_z, to_core, to_shard = partner(z, core, shard)
                pairs.append(((z * 2 + core) * 4 + shard, (to_z * 2 + to_core) * 4 + to_shard))
    return lax.ppermute(value, AXES, pairs)


to_core = lambda z, core, shard: (z, 1 - core, shard)
to_first = lambda z, core, shard: (z, core, shard ^ (1 + core))
to_second = lambda z, core, shard: (z, core, shard ^ (2 - core))
to_x = lambda z, core, shard: (z, core, shard ^ 1)
to_y = lambda z, core, shard: (z, core, shard ^ 2)
to_below = lambda z, core, shard: (z ^ 1, core, shard)
to_above = lambda z, core, shard: (3 - z, core, shard)


def wide(value):
    return value.astype(F32)


def shards(
    layer_input, seq_lengths, out_grad, attn_gain, attn_shift, mlp_gain, mlp_shift, qkv_weight, qkv_bias,
    dense_weight, dense_bias, inner_weight, inner_bias, outer_weight, outer_bias,
):
    core = lax.axis_index("core")
    own = lax.axis_index("y") * 2 + lax.axis_index("x")
    steps = jnp.where(core == 0, jnp.array([0, 2, 1, 3], jnp.int32), jnp.array([0, 1, 2, 3], jnp.int32))
    shard_of = own ^ steps
    difference = own ^ jnp.arange(4, dtype=jnp.int32)
    block_of = jnp.where(core == 1, difference, ((difference & 1) << 1) | (difference >> 1))
    table = jnp.concatenate([core[None].astype(jnp.int32), seq_lengths, block_of, shard_of]).astype(jnp.int32)

    gather = lambda piece: lax.all_gather(piece, ("core", "y", "x"), axis=0, tiled=True)
    pack_attn = lambda pair: pack(
        functools.partial(attn_pack_kernel, pair), (1, 128, 2 * D), 13, "attn_pack", table, qkv_weight, dense_weight
    )
    pack_mlp = lambda unit: pack(
        functools.partial(mlp_pack_kernel, unit), (1, 2, 128, 2 * D), 6, "mlp_pack", table, inner_weight, outer_weight
    )
    pieces = [gather(pack_attn(0)), gather(pack_mlp(0)), gather(pack_mlp(1)), gather(pack_attn(1))]

    vectors = jnp.concatenate(
        [attn_gain, attn_shift, mlp_gain, mlp_shift, dense_bias, outer_bias, qkv_bias, inner_bias]
    )
    vectors = lax.all_gather(vectors, ("y", "x"), axis=0, tiled=False).astype(F32)
    cuts = np.cumsum([256] * 6 + [768, 1024])[:-1]
    gain_a, shift_a, gain_m, shift_m, bias_d, bias_o, bias_qkv, bias_i = (
        part.reshape(1, -1) for part in jnp.split(vectors, cuts, axis=1)
    )
    bias_pairs = jnp.transpose(bias_qkv.reshape(3, 2, 2, 2, 128), (3, 1, 0, 2, 4)).reshape(2, 1, 1536)
    bias_units = jnp.swapaxes(bias_i.reshape(4, 2, 512), 0, 1).reshape(2, 1, 2048)

    na, nm, gr = norm(table, layer_input, out_grad, (gain_a, shift_a, gain_m, shift_m))
    tables = [jnp.asarray(t) for t in rotary_tables()]

    def after(done, *values):
        return lax.optimization_barrier((done,) + values)

    far_blocks = lambda keep, got: add((keep, 2, 1), (got, 1, 2), count=2)
    near_block = lambda keep, got, far: add((keep, 1, 1), (got, 2, 1), (far, 1, 1))
    own_block = lambda *arrays: add(*((array, 0, 1) for array in arrays))
    plus = lambda total, got: add((total, 0, 1), (got, 0, 1))

    none = (None, None)
    attn_call = lambda first, count, pair, parts, totals: attn_unit(
        first, count, table, na, gr, bias_pairs[pair], tables, pieces[3 * pair], parts, totals
    )
    mlp_call = lambda first, count, unit, parts, totals: mlp_unit(
        first, count, table, nm, gr, bias_units[unit], pieces[1 + unit], parts, totals
    )

    keep_a, send_a, gb0, out, dna = attn_call(0, 2, 0, none, none)
    got_a = exchange(send_a, to_core)

    keep_m, send_m, gbi0a, out, dnm = mlp_call(0, 2, 0, none, (out, None))
    out, keep_a, got_a = after(out, keep_a, got_a)
    far_a = far_blocks(keep_a, got_a)
    out, far_a = after(out, far_a)
    far_a = exchange(far_a, to_first)

    keep_m, send_m, gbi0b, out, dnm = mlp_call(2, 2, 0, (keep_m, send_m), (out, dnm))
    got_m = exchange(send_m, to_core)
    out, keep_a, got_a, far_a = after(out, keep_a, got_a, far_a)
    near_a = near_block(keep_a, got_a, far_a)
    near_a, keep_m, got_m = after(near_a, keep_m, got_m)
    far_m = far_blocks(keep_m, got_m)
    out, near_a, far_m = after(out, near_a, far_m)
    near_a = exchange(near_a, to_second)
    far_m = exchange(far_m, to_first)

    keep_n, send_n, gbi1a, out, dnm = mlp_call(0, 2, 1, none, (out, dnm))
    out, keep_a, got_a, far_a, near_a, keep_m, got_m, far_m = after(
        out, keep_a, got_a, far_a, near_a, keep_m, got_m, far_m
    )
    total_a = own_block(keep_a, got_a, far_a, near_a)
    near_m = near_block(keep_m, got_m, far_m)
    out, total_a, near_m = after(out, total_a, near_m)
    got_total_a = exchange(total_a, to_below)
    near_m = exchange(near_m, to_second)

    keep_n, send_n, gbi1b, out, dnm = mlp_call(2, 2, 1, (keep_n, send_n), (out, dnm))
    got_n = exchange(send_n, to_core)
    out, total_a, got_total_a, keep_m, got_m, far_m, near_m = after(
        out, total_a, got_total_a, keep_m, got_m, far_m, near_m
    )
    total_a = plus(total_a, got_total_a)
    total_m = own_block(keep_m, got_m, far_m, near_m)
    total_m, total_a, keep_n, got_n = after(total_m, total_a, keep_n, got_n)
    far_n = far_blocks(keep_n, got_n)
    out, total_a, total_m, far_n = after(out, total_a, total_m, far_n)
    got_total_a = exchange(total_a, to_above)
    got_total_m = exchange(total_m, to_below)
    far_n = exchange(far_n, to_first)

    keep_b, send_b, gb1a, out, dna = attn_call(0, 1, 1, none, (out, dna))
    out, total_a, got_total_a, total_m, got_total_m, keep_n, got_n, far_n = after(
        out, total_a, got_total_a, total_m, got_total_m, keep_n, got_n, far_n
    )
    total_a = plus(total_a, got_total_a)
    total_m = plus(total_m, got_total_m)
    near_n = near_block(keep_n, got_n, far_n)
    out, total_a, total_m, near_n = after(out, total_a, total_m, near_n)
    other_a = exchange(total_a, to_core)
    got_total_m = exchange(total_m, to_above)
    near_n = exchange(near_n, to_second)

    keep_b, send_b, gb1b, out, dna = attn_call(1, 1, 1, (keep_b, send_b), (out, dna))
    got_b = exchange(send_b, to_core)
    out, total_m, got_total_m, keep_n, got_n, far_n, near_n, other_a = after(
        out, total_m, got_total_m, keep_n, got_n, far_n, near_n, other_a
    )
    first_n, second_n = split_add(keep_n, got_n, far_n, near_n)
    total_m = plus(total_m, got_total_m)
    out, total_m, first_n, second_n = after(out, total_m, first_n, second_n)
    got_first_n = exchange(first_n, to_below)
    got_second_n = exchange(second_n, to_above)
    other_m = exchange(total_m, to_core)
    layer_output = output(layer_input, out, bias_d + bias_o)
    layer_output, keep_b, got_b = after(layer_output, keep_b, got_b)
    far_b = far_blocks(keep_b, got_b)

    bias_sums = [
        gb0,
        jnp.concatenate([gb1a, gb1b], axis=1),
        jnp.concatenate([gbi0a, gbi0b], axis=1),
        jnp.concatenate([gbi1a, gbi1b], axis=1),
    ]
    far_b, dna, dnm = after(far_b, dna, dnm)
    far_b = exchange(far_b, to_first)
    input_grad, small = finish(table, layer_input, gr, dna, dnm, (gain_a, gain_m), bias_sums)
    small, far_b, keep_b, got_b = after(small, far_b, keep_b, got_b)
    near_b = near_block(keep_b, got_b, far_b)
    near_b, got_first_n, got_second_n, first_n, second_n = after(near_b, got_first_n, got_second_n, first_n, second_n)
    near_b = exchange(near_b, to_second)
    first_n, second_n = halves_add(first_n, got_first_n, second_n, got_second_n)
    first_n, second_n, near_b = after(first_n, second_n, near_b)
    got_first_n = exchange(first_n, to_above)
    got_second_n = exchange(second_n, to_below)
    first_b, second_b = split_add(keep_b, got_b, far_b, near_b)
    got_first_b = exchange(first_b, to_below)
    got_second_b = exchange(second_b, to_above)
    (total_n,) = halves_add(first_n, got_first_n, second_n, got_second_n, join=True)
    other_n = exchange(total_n, to_core)
    first_b, second_b = halves_add(first_b, got_first_b, second_b, got_second_b)
    got_first_b = exchange(first_b, to_above)
    got_second_b = exchange(second_b, to_below)
    (total_b,) = halves_add(first_b, got_first_b, second_b, got_second_b, join=True)
    other_b = exchange(total_b, to_core)

    grad_wi, grad_wo = place(
        mlp_place_kernel, ((256, FF), (1024, D)), "mlp_place", table, total_m, other_m, total_n, other_n
    )
    grad_qkv, grad_d = place(
        attn_place_kernel, ((256, 3 * D), (256, D)), "attn_place", table, total_a, other_a, total_b, other_b
    )

    for partner in (to_core, to_x, to_y, to_below, to_above):
        small = small + exchange(small, partner)
    small = lax.dynamic_index_in_dim(small, own, 0, keepdims=False)
    g_ga, g_sa, g_gm, g_sm, g_bd, g_bqkv, g_bi = jnp.split(small, np.cumsum([256] * 5 + [768]))
    return (
        layer_output, input_grad, g_ga, g_sa, g_gm, g_sm, grad_qkv, g_bqkv, grad_d, g_bd, grad_wi, g_bi, grad_wo, g_bd,
    )


def solution(mesh):
    replicas, shard_count = mesh.shape["rep"], mesh.shape["shard"]
    shape = (replicas // 2, 2, 2, shard_count // 2)
    cut = Mesh(mesh.devices.reshape(shape), ("z", "core", "y", "x"))
    both = P(("z", "core", "y", "x"), None)
    shard = P(("y", "x"))
    matrix = P(("y", "x"), None)
    weights = (shard,) * 4 + (matrix, shard) * 4
    body = shards if (replicas, shard_count) == (8, 4) else general_shards
    return jax.shard_map(
        body,
        mesh=cut,
        in_specs=(both, P(("z", "core", "y", "x")), both) + weights,
        out_specs=(both, both) + weights,
        check_vma=False,
    )
```

```python
import functools

import jax
import jax.numpy as jnp
import numpy as np
from jax import lax
from jax.experimental import pallas as pl
from jax.experimental.pallas import tpu as pltpu
from jax.sharding import Mesh, PartitionSpec as P

D = 1024
H = 16
FF = 4096
HD = 64
ROT = 16
T = 1024
GROUP = 256
HEADS = GROUP // HD
ROWS = 256
EPSILON = 1e-05
MASKED = -1e30
BF = jnp.bfloat16
F32 = jnp.float32
VMEM = 60 * 2**20


def nn(a, b):
    return lax.dot_general(a, b, (((1,), (0,)), ((), ())), preferred_element_type=F32)


def nt(a, b):
    return lax.dot_general(a, b, (((1,), (1,)), ((), ())), preferred_element_type=F32)


def tn(a, b):
    return lax.dot_general(a, b, (((0,), (0,)), ((), ())), preferred_element_type=F32)


def rows_of(index, size):
    return slice(index * size, (index + 1) * size)


def rotary_tables():
    half = ROT // 2
    inverse = 1.0 / np.float32(10000.0) ** (np.arange(half, dtype=np.float32) * np.float32(2.0 / ROT))
    angles = np.arange(T, dtype=np.float32)[:, None] * inverse.astype(np.float32)[None, :]
    cosine = np.ones((T, HD), np.float32)
    ahead = np.zeros((T, HD), np.float32)
    behind = np.zeros((T, HD), np.float32)
    cosine[:, :half] = np.cos(angles)
    cosine[:, half:ROT] = np.cos(angles)
    ahead[:, :half] = -np.sin(angles)
    behind[:, half:ROT] = np.sin(angles)
    return [np.tile(table, (1, 2)) for table in (cosine, ahead, behind)]


def add_columns(ref, rows, value, order):
    width = value.shape[1] // len(order)
    for place, block in enumerate(order):
        ref[rows, rows_of(block, width)] += value[:, rows_of(place, width)]


def mlp_kernel(order, nm, gr, wi, bi, wo, out, dn, gwi, gwo, gbi, act, ig):
    @pl.when(pl.program_id(0) == 0)
    def _():
        out[...] = jnp.zeros_like(out)
        dn[...] = jnp.zeros_like(dn)

    bias_sum = jnp.zeros(gbi.shape, F32)
    for t in range(T // ROWS):
        r = rows_of(t, ROWS)
        inner = nn(nm[r, :], wi[...]) + bi[...]
        grad = nt(gr[r, :], wo[...])
        normal = 0.5 * lax.erf(inner * 0.7071067811865476) + 0.5
        slope = normal + inner * jnp.exp(-0.5 * inner * inner) * 0.3989422804014327
        act[r, :] = (inner * normal).astype(BF)
        inner_grad = (grad * slope).astype(BF)
        ig[r, :] = inner_grad
        bias_sum += jnp.sum(inner_grad.astype(F32), axis=0, keepdims=True)
    gbi[...] = bias_sum
    for t in range(T // ROWS):
        r = rows_of(t, ROWS)
        out[r, :] += nn(act[r, :], wo[...])
        add_columns(dn, r, nt(ig[r, :], wi[...]), order)
    for d in range(D // ROWS):
        r = rows_of(d, ROWS)
        gwi[r, :] = tn(nm[:, r], ig[...]).astype(BF)
    step = min(ROWS, act.shape[1])
    for f in range(act.shape[1] // step):
        r = rows_of(f, step)
        gwo[r, :] = tn(act[:, r], gr[...]).astype(BF)


def mlp(order, nm, gr, wi, bi, wo):
    tile = FF // len(order)
    half = len(order) // 2
    one = pl.Buffered(1)
    whole = lambda: pl.BlockSpec((T, D), lambda i: (0, 0), pipeline_mode=one)
    total = lambda: pl.BlockSpec((T, D), lambda i: (0, 0))
    columns = lambda rows: pl.BlockSpec((rows, tile), lambda i: (0, (i % half) * 2 + i // half))
    return pl.pallas_call(
        functools.partial(mlp_kernel, order),
        grid=(FF // tile,),
        in_specs=[whole(), whole(), columns(D), columns(1), pl.BlockSpec((tile, D), lambda i: (i, 0))],
        out_specs=[total(), total(), columns(D), pl.BlockSpec((tile, D), lambda i: (i, 0)), columns(1)],
        out_shape=[
            jax.ShapeDtypeStruct((T, D), F32),
            jax.ShapeDtypeStruct((T, D), F32),
            jax.ShapeDtypeStruct((D, FF), BF),
            jax.ShapeDtypeStruct((FF, D), BF),
            jax.ShapeDtypeStruct((1, FF), F32),
        ],
        scratch_shapes=[pltpu.VMEM((T, tile), BF), pltpu.VMEM((T, tile), BF)],
        compiler_params=pltpu.CompilerParams(vmem_limit_bytes=VMEM),
        cost_estimate=pl.CostEstimate(flops=12 * T * D * FF, bytes_accessed=60 * 2**20, transcendentals=2 * T * FF),
        name="mlp",
    )(nm, gr, wi, bi, wo)


def attn_kernel(
    order, length, na, gr, wq, wk, wv, bq, bk, bv, wd, cosine, ahead, behind,
    out, dn, gwq, gwk, gwv, gwd, gb,
    q, k, v, dc, ctx, dq, dk, dv, grads,
):
    @pl.when(pl.program_id(0) == 0)
    def _():
        out[...] = jnp.zeros_like(out)
        dn[...] = jnp.zeros_like(dn)

    def turn(x, r, back):
        parts = []
        for p in range(GROUP // 128):
            pair = x[:, rows_of(p, 128)]
            straight = pair * cosine[r, :]
            across = (
                pltpu.roll(pair, 128 - ROT // 2, 1) * ahead[r, :]
                + pltpu.roll(pair, ROT // 2, 1) * behind[r, :]
            )
            parts.append(straight - across if back else straight + across)
        return jnp.concatenate(parts, axis=1)

    for t in range(T // ROWS):
        r = rows_of(t, ROWS)
        x = na[r, :]
        queries = (turn(nn(x, wq[...]) + bq[...], r, False).astype(BF) * 0.125).astype(BF)
        keys = turn(nn(x, wk[...]) + bk[...], r, False).astype(BF)
        values = (nn(x, wv[...]) + bv[...]).astype(BF)
        context_grad = nt(gr[r, :], wd[...]).astype(BF)
        for h in range(HEADS):
            c = rows_of(h, HD)
            q[h, r, :] = queries[:, c]
            k[h, r, :] = keys[:, c]
            v[h, r, :] = values[:, c]
            dc[h, r, :] = context_grad[:, c]

    block = 256
    inside = lax.broadcasted_iota(jnp.int32, (1, T), 1) < length[0]
    bias = jnp.where(inside, 0.0, MASKED).astype(F32)
    below = lax.broadcasted_iota(jnp.int32, (block, block), 1) <= lax.broadcasted_iota(jnp.int32, (block, block), 0)
    causal = jnp.where(below, 0.0, MASKED).astype(F32)

    def head(h, carry):
        dk[h] = jnp.zeros((T, HD), F32)
        dv[h] = jnp.zeros((T, HD), F32)
        for i in range(T // block):
            r = rows_of(i, block)
            spans = ([slice(0, i * block)] if i else []) + [r]
            query = q[h, r, :]
            scores = [nt(query, k[h, c, :]) + bias[:, c] for c in spans]
            scores[-1] += causal
            top = functools.reduce(jnp.maximum, [jnp.max(s, axis=1, keepdims=True) for s in scores])
            weights = [jnp.exp(s - top) for s in scores]
            scale = 1.0 / sum(jnp.sum(w, axis=1, keepdims=True) for w in weights)
            low = [w.astype(BF) for w in weights]
            context = sum(nn(w, v[h, c, :]) for w, c in zip(low, spans))
            ctx[h, r, :] = (context * scale).astype(BF)
            scaled_grad = (dc[h, r, :].astype(F32) * scale).astype(BF)
            probs_grad = [nt(scaled_grad, v[h, c, :]) for c in spans]
            inner = scale * sum(jnp.sum(w * p, axis=1, keepdims=True) for w, p in zip(weights, probs_grad))
            score_grad = [(w * (p - inner)).astype(BF) for w, p in zip(weights, probs_grad)]
            dq[h, r, :] = sum(nn(s, k[h, c, :]) for s, c in zip(score_grad, spans))
            for s, w, c in zip(score_grad, low, spans):
                dk[h, c, :] += tn(s, query)
                dv[h, c, :] += tn(w, scaled_grad)
        return carry

    lax.fori_loop(0, HEADS, head, 0)

    sums = [jnp.zeros((1, GROUP), F32) for _ in range(3)]
    together = lambda ref, r: jnp.concatenate([ref[h, r, :] for h in range(HEADS)], axis=1)
    for t in range(T // ROWS):
        r = rows_of(t, ROWS)
        context = together(ctx, r)
        grads[r, 3 * GROUP :] = context
        out[r, :] += nn(context, wd[...])
        pieces = (
            turn(together(dq, r) * 0.125, r, True).astype(BF),
            turn(together(dk, r), r, True).astype(BF),
            together(dv, r).astype(BF),
        )
        for p, piece in enumerate(pieces):
            grads[r, rows_of(p, GROUP)] = piece
            sums[p] += jnp.sum(piece.astype(F32), axis=0, keepdims=True)
        normed_grad = sum(nt(piece, w[...]) for piece, w in zip(pieces, (wq, wk, wv)))
        add_columns(dn, r, normed_grad, order)
    for p in range(3):
        gb[p : p + 1, :] = sums[p]
    for d in range(D // ROWS):
        r = rows_of(d, ROWS)
        x = na[:, r]
        for p, g in enumerate((gwq, gwk, gwv)):
            g[r, :] = tn(x, grads[:, rows_of(p, GROUP)]).astype(BF)
    gwd[...] = tn(grads[:, 3 * GROUP :], gr[...]).astype(BF)


def attn(order, length, na, gr, weight, bias, wd):
    groups = D // GROUP
    one = pl.Buffered(1)
    whole = lambda shape: pl.BlockSpec(shape, lambda i: (0, 0), pipeline_mode=one)
    total = lambda: pl.BlockSpec((T, D), lambda i: (0, 0))
    columns = lambda rows, part=0: pl.BlockSpec((rows, GROUP), lambda i: (0, i + part * groups))
    head_rows = lambda dtype: pltpu.VMEM((HEADS, T, HD), dtype)
    return pl.pallas_call(
        functools.partial(attn_kernel, order),
        grid=(groups,),
        in_specs=[pl.BlockSpec(memory_space=pltpu.SMEM), whole((T, D)), whole((T, D))]
        + [columns(D, p) for p in range(3)]
        + [columns(1, p) for p in range(3)]
        + [pl.BlockSpec((GROUP, D), lambda i: (i, 0))]
        + [whole((T, 128))] * 3,
        out_specs=[total(), total()] + [columns(D)] * 3 + [pl.BlockSpec((GROUP, D), lambda i: (i, 0)), columns(3)],
        out_shape=[jax.ShapeDtypeStruct((T, D), F32)] * 2
        + [jax.ShapeDtypeStruct((D, D), BF)] * 4
        + [jax.ShapeDtypeStruct((3, D), F32)],
        scratch_shapes=[head_rows(BF)] * 5 + [head_rows(F32)] * 3 + [pltpu.VMEM((T, 4 * GROUP), BF)],
        compiler_params=pltpu.CompilerParams(vmem_limit_bytes=VMEM),
        cost_estimate=pl.CostEstimate(flops=90 * 10**9, bytes_accessed=40 * 2**20, transcendentals=10 * 2**20),
        name="attn",
    )(length, na, gr, weight, weight, weight, bias, bias, bias, wd, *map(jnp.asarray, rotary_tables()))


def general_shards(
    layer_input, seq_lengths, out_grad, attn_gain, attn_shift, mlp_gain, mlp_shift, qkv_weight, qkv_bias,
    dense_weight, dense_bias, inner_weight, inner_bias, outer_weight, outer_bias,
):
    groupings = ("core", "y", "x")
    shard_count = lax.axis_size("y") * lax.axis_size("x")
    core = lax.axis_index("core")
    order = [2 * a + h for h in range(2) for a in range(shard_count)]

    def gather(piece):
        half = piece.shape[0] // 2
        mine = lax.dynamic_slice_in_dim(piece, core * half, half, 0)
        return lax.all_gather(mine, groupings, axis=0, tiled=True)

    def natural(rows):
        return jnp.swapaxes(rows.reshape(2, shard_count, -1, rows.shape[1]), 0, 1).reshape(rows.shape)

    def halves_first(rows):
        return jnp.swapaxes(rows.reshape(shard_count, 2, -1, rows.shape[1]), 0, 1).reshape(rows.shape)

    vectors = jnp.concatenate(
        [attn_gain, attn_shift, mlp_gain, mlp_shift, dense_bias, outer_bias, qkv_bias, inner_bias]
    )
    vectors = lax.all_gather(vectors, ("y", "x"), axis=0, tiled=False).astype(F32)
    sizes = [D] * 6 + [3 * D, FF]
    cuts = np.cumsum([size // shard_count for size in sizes])[:-1]
    gain_a, shift_a, gain_m, shift_m, bias_d, bias_o, bias_qkv, bias_i = (
        part.reshape(1, -1) for part in jnp.split(vectors, cuts, axis=1)
    )
    wi = gather(inner_weight)
    wo = gather(outer_weight)
    wqkv = gather(qkv_weight)
    wd = natural(gather(dense_weight))

    x = layer_input.astype(F32)
    mean = jnp.mean(x, axis=1, keepdims=True)
    centered = x - mean
    inverse = lax.rsqrt(jnp.mean(centered * centered, axis=1, keepdims=True) + EPSILON)
    unit = centered * inverse
    valid = jnp.arange(T, dtype=jnp.int32)[:, None] < seq_lengths[0]
    gr = jnp.where(valid, out_grad, jnp.zeros_like(out_grad))
    blocked = lambda rows: jnp.swapaxes(rows.reshape(T, shard_count, 2, -1), 1, 2).reshape(T, D)
    nm = blocked((unit * gain_m + shift_m).astype(BF))
    na = blocked((unit * gain_a + shift_a).astype(BF))

    out_m, dnm, gwi, gwo, gbi = mlp(order, nm, gr, wi, bias_i, wo)
    out_a, dna, gwq, gwk, gwv, gwd, gbqkv = attn(order, seq_lengths, na, gr, wqkv, bias_qkv, wd)

    def reduce(grad):
        part = lax.psum_scatter(grad, "core", scatter_dimension=0, tiled=True)
        part = lax.psum_scatter(part, ("y", "x"), scatter_dimension=0, tiled=True)
        part = lax.psum(part, "z")
        return lax.all_gather(part, "core", axis=0, tiled=True).astype(F32)

    grad_wi = reduce(gwi)
    grad_wo = reduce(gwo)
    grad_d = reduce(halves_first(gwd))
    grad_qkv = jnp.concatenate([reduce(g) for g in (gwq, gwk, gwv)], axis=1)

    layer_output = x + out_m + out_a + (bias_d + bias_o)
    g = dna * gain_a + dnm * gain_m
    gr32 = gr.astype(F32)
    input_grad = gr32 + inverse * (
        g - jnp.mean(g, axis=1, keepdims=True) - unit * jnp.mean(g * unit, axis=1, keepdims=True)
    )
    column = lambda rows: jnp.sum(rows, axis=0)
    parts = [column(dna * unit), column(dna), column(dnm * unit), column(dnm), column(gr32), gbqkv, gbi]
    small = jnp.concatenate([p.reshape(shard_count, -1) for p in parts], axis=1)
    small = lax.psum_scatter(small, ("y", "x"), scatter_dimension=0, tiled=True)
    small = lax.psum(small, ("z", "core"))
    cuts = np.cumsum([size // shard_count for size in [D] * 5 + [3 * D, FF]])[:-1]
    g_ga, g_sa, g_gm, g_sm, g_bd, g_bqkv, g_bi = (p.reshape(-1) for p in jnp.split(small, cuts, axis=1))
    return (
        layer_output, input_grad, g_ga, g_sa, g_gm, g_sm, grad_qkv, g_bqkv, grad_d, g_bd, grad_wi, g_bi, grad_wo, g_bd,
    )


WIDE = 512
VMEM_UNIT = 56 * 2**20
LONG = pl.CostEstimate(flops=10**13, bytes_accessed=2**20, transcendentals=0)


def columns_at(start, size):
    return pl.ds(pl.multiple_of(start, 128), size)


def spread_kernel(table, *refs):
    *given, gain_a, shift_a, gain_m, shift_m, bias, first_pair, second_pair, first_unit, second_unit = refs
    for j, ref in enumerate(given):
        shard = table[6] ^ j
        rows = ref[...].astype(F32)
        row = lambda k: rows[k : k + 1, :]
        for i, out in enumerate((gain_a, shift_a, gain_m, shift_m)):
            for k in range(2):
                out[:, columns_at(shard * 256 + k * 128, 128)] = row(2 * i + k)
        for k in range(2):
            bias[:, columns_at(shard * 256 + k * 128, 128)] = row(8 + k) + row(10 + k)
        for k in range(6):
            column = shard * 768 + k * 128
            part, owner = column >> 10, (column & 1023) >> 8
            target = (owner >> 1) * 768 + part * 256 + (owner & 1) * 128
            (first_pair, second_pair)[k % 2][:, columns_at(target, 128)] = row(12 + k)
        for k in range(8):
            (first_unit, second_unit)[k // 4][:, columns_at(shard * 512 + k % 4 * 128, 128)] = row(18 + k)


def spread(table, given):
    inside = pl.BlockSpec(memory_space=pltpu.VMEM)
    widths = [D] * 5 + [1536] * 2 + [2048] * 2
    return pl.pallas_call(
        spread_kernel,
        in_specs=[pl.BlockSpec(memory_space=pltpu.SMEM)] + [inside] * len(given),
        out_specs=[inside] * len(widths),
        out_shape=[jax.ShapeDtypeStruct((1, width), F32) for width in widths],
        name="spread",
    )(table, *given)


def norm_kernel(table, x, grad, gain_a, shift_a, gain_m, shift_m, na, nm, gr):
    values = x[...].astype(F32)
    mean = jnp.mean(values, axis=1, keepdims=True)
    centered = values - mean
    unit = centered * lax.rsqrt(jnp.mean(centered * centered, axis=1, keepdims=True) + EPSILON)
    rows = x.shape[0]
    position = pl.program_id(0) * rows + lax.broadcasted_iota(jnp.int32, (rows, 1), 0)
    gr[...] = jnp.where(position < table[1], grad[...].astype(F32), 0.0).astype(BF)
    for out, gain, shift in ((na, gain_a, shift_a), (nm, gain_m, shift_m)):
        normed = (unit * gain[...] + shift[...]).astype(BF)
        for a in range(4):
            for h in range(2):
                place = (table[2 + a] * 2 + (table[0] ^ h)) * 128
                out[:, columns_at(place, 128)] = normed[:, rows_of(a * 2 + h, 128)]


def norm(table, x, grad, vectors):
    tile = pl.BlockSpec((ROWS, D), lambda i: (i, 0))
    row = pl.BlockSpec((1, D), lambda i: (0, 0))
    return pl.pallas_call(
        norm_kernel,
        grid=(T // ROWS,),
        in_specs=[pl.BlockSpec(memory_space=pltpu.SMEM), tile, tile] + [row] * 4,
        out_specs=[tile] * 3,
        out_shape=[jax.ShapeDtypeStruct((T, D), BF)] * 3,
        compiler_params=pltpu.CompilerParams(vmem_limit_bytes=VMEM),
        cost_estimate=LONG,
        name="norm",
    )(table, x, grad, *vectors)


def finish_kernel(table, x, gr, dna, dnm, gain_a, gain_m, *refs):
    *bias_sums, input_grad, small, sums = refs
    values = x[...].astype(F32)
    mean = jnp.mean(values, axis=1, keepdims=True)
    centered = values - mean
    inverse = lax.rsqrt(jnp.mean(centered * centered, axis=1, keepdims=True) + EPSILON)
    unit = centered * inverse

    def natural(ref):
        places = [(table[2 + a] * 2 + (table[0] ^ h)) * 128 for a in range(4) for h in range(2)]
        return jnp.concatenate([ref[:, columns_at(place, 128)] for place in places], axis=1)

    normed_a, normed_m = natural(dna), natural(dnm)
    upper = gr[...].astype(F32)
    g = normed_a * gain_a[...] + normed_m * gain_m[...]
    input_grad[...] = upper + inverse * (
        g - jnp.mean(g, axis=1, keepdims=True) - unit * jnp.mean(g * unit, axis=1, keepdims=True)
    )

    @pl.when(pl.program_id(0) == 0)
    def _():
        sums[...] = jnp.zeros_like(sums)

    for i, rows in enumerate((normed_a * unit, normed_a, normed_m * unit, normed_m, upper)):
        sums[i : i + 1, :] += jnp.sum(rows, axis=0, keepdims=True)

    @pl.when(pl.program_id(0) == T // ROWS - 1)
    def _():
        for i in range(5):
            for a in range(4):
                small[a : a + 1, rows_of(i, 256)] = sums[i : i + 1, rows_of(a, 256)]
        pair_sums, unit_sums = bias_sums[:3], bias_sums[3:]
        for pair in range(2):
            for a, b in qkv_blocks(pair):
                value = pair_sums[0] if pair == 0 else pair_sums[1 + b // 768]
                small[a // 768 : a // 768 + 1, pl.ds(1280 + a % 768, 128)] = value[:, pl.ds(b if pair == 0 else b % 768, 128)]
        for a in range(4):
            small[a : a + 1, pl.ds(2048, 512)] = unit_sums[0][:, rows_of(a, 512)]
            small[a : a + 1, pl.ds(2560, 512)] = unit_sums[1 + a // 2][:, rows_of(a % 2, 512)]


def finish(table, x, gr, dna, dnm, vectors, bias_sums):
    tile = pl.BlockSpec((ROWS, D), lambda i: (i, 0))
    row = lambda value: pl.BlockSpec(value.shape, lambda i: (0, 0))
    return pl.pallas_call(
        finish_kernel,
        grid=(T // ROWS,),
        in_specs=[pl.BlockSpec(memory_space=pltpu.SMEM)] + [tile] * 4 + [row(v) for v in (*vectors, *bias_sums)],
        out_specs=[tile, pl.BlockSpec((4, 3072), lambda i: (0, 0))],
        out_shape=[jax.ShapeDtypeStruct((T, D), F32), jax.ShapeDtypeStruct((4, 3072), F32)],
        scratch_shapes=[pltpu.VMEM((5, D), F32)],
        compiler_params=pltpu.CompilerParams(vmem_limit_bytes=VMEM),
        cost_estimate=LONG,
        name="finish",
    )(table, x, gr, dna, dnm, *vectors, *bias_sums)


class Totals:
    def __init__(self, refs_in, refs_out, scratch, sems):
        self.fresh = [ref is None for ref in refs_in]
        self.refs_in, self.refs_out, self.scratch, self.sems = refs_in, refs_out, scratch, sems

    def loads(self):
        return [
            pltpu.make_async_copy(source, self.scratch[i], self.sems.at[i])
            for i, source in enumerate(self.refs_in)
            if source is not None
        ]

    def stores(self):
        return [
            pltpu.make_async_copy(source, target, self.sems.at[i])
            for i, (source, target) in enumerate(zip(self.scratch, self.refs_out))
        ]

    def begin(self):
        for copy in self.loads():
            copy.start()
        for target, source in zip(self.scratch, self.refs_in):
            if source is None:
                target[...] = jnp.zeros_like(target)

    def ready(self):
        for copy in self.loads():
            copy.wait()


def start_all(copies):
    for copy in copies:
        copy.start()


def wait_all(copies):
    for copy in copies:
        copy.wait()


def mlp_unit_kernel(first, count, given, table, nm, gr, bi, pieces, *refs):
    refs = list(refs)
    olds = [refs.pop(0) if is_given else None for is_given in given]
    keep, send, gbi, out_ref, dn_ref, wi, wo, act, ig, out, dn, inner_stage, outer_stage, sems, out_sems, total_sems = refs
    step = pl.program_id(0)
    core = table[0]
    totals = Totals(olds[2:], (out_ref, dn_ref), (out, dn), total_sems)

    def copies(index):
        slot, tile = index % 2, first + index
        made = []
        for t in range(4):
            for half in range(2):
                piece = (core ^ half) * 4 + table[6 + t]
                source = pieces.at[piece, 0, :, columns_at(tile * WIDE, WIDE)]
                made.append((source, wi.at[slot, pl.ds(t * 256 + half * 128, 128), :]))
        for h in range(2):
            for part in range(2):
                source = pieces.at[h * 4 + tile, 1, :, pl.ds(part * D, D)]
                made.append((source, wo.at[slot, pl.ds(h * 256 + part * 128, 128), :]))
        return [pltpu.make_async_copy(a, b, sems.at[slot, i]) for i, (a, b) in enumerate(made)]

    def results(index):
        slot, tile = index % 2, first + index
        made = []
        for side, target in enumerate((keep, send)):
            inner_part = target.at[:, pl.ds(pl.multiple_of(tile // 2 * 128, 128), 128), columns_at((tile % 2) * WIDE, WIDE)]
            made.append((inner_stage.at[slot, side], inner_part))
            made.append((outer_stage.at[slot, side], target.at[table[2 + tile], pl.ds(256, 256)]))
        return [pltpu.make_async_copy(a, b, out_sems.at[slot, i]) for i, (a, b) in enumerate(made)]

    @pl.when(step == 0)
    def _():
        start_all(copies(step))
        totals.begin()

    @pl.when(step < count - 1)
    def _():
        start_all(copies(step + 1))

    wait_all(copies(step))
    slot = step % 2

    bias_sum = jnp.zeros(gbi.shape, F32)
    for t in range(T // ROWS):
        r = rows_of(t, ROWS)
        inner = nn(nm[r, :], wi[slot]) + bi[...]
        grad = nt(gr[r, :], wo[slot])
        normal = 0.5 * lax.erf(inner * 0.7071067811865476) + 0.5
        slope = normal + inner * jnp.exp(-0.5 * inner * inner) * 0.3989422804014327
        act[r, :] = (inner * normal).astype(BF)
        inner_grad = (grad * slope).astype(BF)
        ig[r, :] = inner_grad
        bias_sum += jnp.sum(inner_grad.astype(F32), axis=0, keepdims=True)
    gbi[...] = bias_sum

    @pl.when(step == 0)
    def _():
        totals.ready()

    for t in range(T // ROWS):
        r = rows_of(t, ROWS)
        out[r, :] += nn(act[r, :], wo[slot])
        dn[r, :] += nt(ig[r, :], wi[slot])

    @pl.when(step == count - 1)
    def _():
        start_all(totals.stores())

    if count > 2:

        @pl.when(step >= 2)
        def _():
            wait_all(results(step - 2))

    for t in range(4):
        grad = tn(nm[:, rows_of(t, 256)], ig[...]).astype(BF)
        inner_stage[slot, 0, t] = grad[:128]
        inner_stage[slot, 1, t] = grad[128:]
    for f in range(2):
        grad = tn(act[:, rows_of(f, 256)], gr[...])
        low, high = grad[:, :WIDE], grad[:, WIDE:]
        sides = (jnp.where(core == 0, low, high).astype(BF), jnp.where(core == 0, high, low).astype(BF))
        for side, value in enumerate(sides):
            for half in range(2):
                outer_stage[slot, side, rows_of(f, 128), rows_of(half, WIDE)] = value[rows_of(half, 128)]
    start_all(results(step))

    @pl.when(step == count - 1)
    def _():
        if count > 1:
            wait_all(results(step - 1))
        wait_all(results(step))
        wait_all(totals.stores())


def mlp_unit(first, count, table, nm, gr, bi, pieces, parts, totals):
    olds = list(parts) + list(totals)
    given = tuple(old is not None for old in olds)
    inputs = [old for old in olds if old is not None]
    aliases = {5 + n: (0, 1, 3, 4)[i] for n, i in enumerate(i for i in range(4) if given[i])}
    whole = pl.BlockSpec((T, D), lambda i: (0, 0), pipeline_mode=pl.Buffered(1))
    anywhere = pl.BlockSpec(memory_space=pl.ANY)
    return pl.pallas_call(
        functools.partial(mlp_unit_kernel, first, count, given),
        grid=(count,),
        in_specs=[pl.BlockSpec(memory_space=pltpu.SMEM), whole, whole, pl.BlockSpec((1, WIDE), lambda i: (0, first + i)), anywhere]
        + [anywhere] * len(inputs),
        out_specs=[anywhere, anywhere, pl.BlockSpec((1, WIDE), lambda i: (0, i)), anywhere, anywhere],
        out_shape=[jax.ShapeDtypeStruct((4, 512, D), BF)] * 2
        + [jax.ShapeDtypeStruct((1, count * WIDE), F32)]
        + [jax.ShapeDtypeStruct((T, D), F32)] * 2,
        input_output_aliases=aliases,
        scratch_shapes=[
            pltpu.VMEM((2, D, WIDE), BF),
            pltpu.VMEM((2, WIDE, D), BF),
            pltpu.VMEM((T, WIDE), BF),
            pltpu.VMEM((T, WIDE), BF),
            pltpu.VMEM((T, D), F32),
            pltpu.VMEM((T, D), F32),
            pltpu.VMEM((2, 2, 4, 128, WIDE), BF),
            pltpu.VMEM((2, 2, 256, D), BF),
            pltpu.SemaphoreType.DMA((2, 12)),
            pltpu.SemaphoreType.DMA((2, 4)),
            pltpu.SemaphoreType.DMA((2,)),
        ],
        compiler_params=pltpu.CompilerParams(vmem_limit_bytes=VMEM_UNIT),
        cost_estimate=LONG,
        name="mlp_unit",
    )(table, nm, gr, bi, pieces, *inputs)


def attn_unit_kernel(first, count, given, apart, last, table, na, gr, bias, cosine, ahead, behind, *refs):
    refs = list(refs)
    pieces = [refs.pop(0) for _ in range(8 if apart else 1)]
    rest = [refs.pop(0) for _ in range(2 if last else 0)]
    olds = [refs.pop(0) if is_given else None for is_given in given]
    (
        keep, send, gb, out_ref, dn_ref,
        w, wd, q, k, v, dc, ctx, dq, dk, dv, grads, out, dn, qkv_stage, dense_stage, sems, out_sems, total_sems,
    ) = refs
    step = pl.program_id(0)
    core = table[0]
    totals = Totals(olds[2:], (out_ref, dn_ref), (out, dn), total_sems)

    def copies(index):
        group = first + index
        made = []
        for t in range(4):
            for half in range(2):
                if apart:
                    piece = pieces[half * 4 + t].at[0]
                    place = wd.at[table[6 + t] // 2, pl.ds(pl.multiple_of(table[6 + t] % 2 * 128, 128), 128), columns_at((core ^ half) * 512, 512)]
                    if isinstance(index, int) and index == 0:
                        made.append((piece.at[:, pl.ds(1536, 512)], place))
                else:
                    piece = pieces[0].at[(core ^ half) * 4 + table[6 + t]]
                made.append((piece.at[:, columns_at(group * 768, 768)], w.at[index, pl.ds(t * 256 + half * 128, 128), :]))
        for pair in range(0 if apart else 2):
            for h in range(2):
                source = pieces[0].at[h * 4 + group * 2 + pair, :, pl.ds(1536, 512)]
                made.append((source, wd.at[index, pl.ds(pair * 128, 128), pl.ds(h * 512, 512)]))
        return [pltpu.make_async_copy(a, b, sems.at[index, i]) for i, (a, b) in enumerate(made)]

    def results(index):
        group = first + index
        made = []
        for side, target in enumerate((keep, send)):
            made.append((qkv_stage.at[index, side], target.at[:, :, columns_at(group * 768, 768)]))
            for pair in range(2):
                place = target.at[table[2 + group * 2 + pair], :, pl.ds(1536, 512)]
                made.append((dense_stage.at[index, side, pair], place))
        return [pltpu.make_async_copy(a, b, out_sems.at[index, i]) for i, (a, b) in enumerate(made)]

    @pl.when(step == 0)
    def _():
        for index in range(count):
            start_all(copies(index))
        totals.begin()

    for index in range(count):

        @pl.when(step == index)
        def _():
            wait_all(copies(index))

    def turn(x, r, back):
        parts = []
        for p in range(GROUP // 128):
            pair = x[:, rows_of(p, 128)]
            straight = pair * cosine[r, :]
            across = (
                pltpu.roll(pair, 128 - ROT // 2, 1) * ahead[r, :]
                + pltpu.roll(pair, ROT // 2, 1) * behind[r, :]
            )
            parts.append(straight - across if back else straight + across)
        return jnp.concatenate(parts, axis=1)

    part = [slice(p * GROUP, (p + 1) * GROUP) for p in range(4)]
    for t in range(T // ROWS):
        r = rows_of(t, ROWS)
        x = na[r, :]
        projected = nn(x, w[step]) + bias[...]
        queries = (turn(projected[:, part[0]], r, False).astype(BF) * 0.125).astype(BF)
        keys = turn(projected[:, part[1]], r, False).astype(BF)
        values = projected[:, part[2]].astype(BF)
        context_grad = nt(gr[r, :], wd[step]).astype(BF)
        for h in range(HEADS):
            c = rows_of(h, HD)
            q[h, r, :] = queries[:, c]
            k[h, r, :] = keys[:, c]
            v[h, r, :] = values[:, c]
            dc[h, r, :] = context_grad[:, c]

    block = 256
    inside = lax.broadcasted_iota(jnp.int32, (1, T), 1) < table[1]
    outside = jnp.where(inside, 0.0, MASKED).astype(F32)
    below = lax.broadcasted_iota(jnp.int32, (block, block), 1) <= lax.broadcasted_iota(jnp.int32, (block, block), 0)
    causal = jnp.where(below, 0.0, MASKED).astype(F32)

    def head(h, carry):
        dk[h] = jnp.zeros((T, HD), F32)
        dv[h] = jnp.zeros((T, HD), F32)
        for i in range(T // block):
            r = rows_of(i, block)
            spans = ([slice(0, i * block)] if i else []) + [r]
            query = q[h, r, :]
            scores = [nt(query, k[h, c, :]) + outside[:, c] for c in spans]
            scores[-1] += causal
            top = functools.reduce(jnp.maximum, [jnp.max(s, axis=1, keepdims=True) for s in scores])
            weights = [jnp.exp(s - top) for s in scores]
            scale = 1.0 / sum(jnp.sum(e, axis=1, keepdims=True) for e in weights)
            low = [e.astype(BF) for e in weights]
            context = sum(nn(e, v[h, c, :]) for e, c in zip(low, spans))
            ctx[h, r, :] = (context * scale).astype(BF)
            scaled_grad = (dc[h, r, :].astype(F32) * scale).astype(BF)
            probs_grad = [nt(scaled_grad, v[h, c, :]) for c in spans]
            inner = scale * sum(jnp.sum(e * p, axis=1, keepdims=True) for e, p in zip(weights, probs_grad))
            score_grad = [(e * (p - inner)).astype(BF) for e, p in zip(weights, probs_grad)]
            dq[h, r, :] = sum(nn(s, k[h, c, :]) for s, c in zip(score_grad, spans))
            for s, e, c in zip(score_grad, low, spans):
                dk[h, c, :] += tn(s, query)
                dv[h, c, :] += tn(e, scaled_grad)
        return carry

    lax.fori_loop(0, HEADS, head, 0)

    @pl.when(step == 0)
    def _():
        totals.ready()

    sums = jnp.zeros((1, 3 * GROUP), F32)
    together = lambda ref, r: jnp.concatenate([ref[h, r, :] for h in range(HEADS)], axis=1)
    for t in range(T // ROWS):
        r = rows_of(t, ROWS)
        context = together(ctx, r)
        grads[r, part[3]] = context
        total = nn(context, wd[step])
        if last:
            total += rest[0][r, :].astype(F32) + rest[1][...]
        out[r, :] += total
        projected_grad = jnp.concatenate(
            [
                turn(together(dq, r) * 0.125, r, True).astype(BF),
                turn(together(dk, r), r, True).astype(BF),
                together(dv, r).astype(BF),
            ],
            axis=1,
        )
        grads[r, : 3 * GROUP] = projected_grad
        sums += jnp.sum(projected_grad.astype(F32), axis=0, keepdims=True)
        dn[r, :] += nt(projected_grad, w[step])
    gb[...] = sums

    @pl.when(step == count - 1)
    def _():
        start_all(totals.stores())

    for t in range(4):
        grad = tn(na[:, rows_of(t, 256)], grads[:, : 3 * GROUP]).astype(BF)
        qkv_stage[step, 0, t] = grad[:128]
        qkv_stage[step, 1, t] = grad[128:]
    grad = tn(grads[:, part[3]], gr[...])
    first_half, second_half = grad[:, :WIDE], grad[:, WIDE:]
    sides = (
        jnp.where(core == 0, first_half, second_half).astype(BF),
        jnp.where(core == 0, second_half, first_half).astype(BF),
    )
    for side, value in enumerate(sides):
        for pair in range(2):
            dense_stage[step, side, pair] = value[rows_of(pair, 128)]
    start_all(results(step))

    @pl.when(step == count - 1)
    def _():
        for index in range(count):
            wait_all(results(index))
        wait_all(totals.stores())


def attn_unit(first, count, table, na, gr, bias, tables, pieces, parts, totals, rest=()):
    olds = list(parts) + list(totals)
    given = tuple(old is not None for old in olds)
    inputs = [old for old in olds if old is not None]
    apart = isinstance(pieces, list)
    pieces = pieces if apart else [pieces]
    aliases = {7 + len(pieces) + len(rest) + n: (0, 1, 3, 4)[i] for n, i in enumerate(i for i in range(4) if given[i])}
    one = pl.Buffered(1)
    whole = pl.BlockSpec((T, D), lambda i: (0, 0), pipeline_mode=one)
    turns = pl.BlockSpec((T, 128), lambda i: (0, 0), pipeline_mode=one)
    anywhere = pl.BlockSpec(memory_space=pl.ANY)
    head_rows = lambda dtype: pltpu.VMEM((HEADS, T, HD), dtype)
    return pl.pallas_call(
        functools.partial(attn_unit_kernel, first, count, given, apart, len(rest) > 0),
        grid=(count,),
        in_specs=[pl.BlockSpec(memory_space=pltpu.SMEM), whole, whole, pl.BlockSpec((1, 3 * GROUP), lambda i: (0, first + i))]
        + [turns] * 3
        + [anywhere] * len(pieces)
        + [pl.BlockSpec(value.shape, lambda i: (0, 0), pipeline_mode=one) for value in rest]
        + [anywhere] * len(inputs),
        out_specs=[anywhere, anywhere, pl.BlockSpec((1, 3 * GROUP), lambda i: (0, i)), anywhere, anywhere],
        out_shape=[jax.ShapeDtypeStruct((4, 128, 2 * D), BF)] * 2
        + [jax.ShapeDtypeStruct((1, 3 * GROUP * count), F32)]
        + [jax.ShapeDtypeStruct((T, D), F32)] * 2,
        input_output_aliases=aliases,
        scratch_shapes=[pltpu.VMEM((count, D, 3 * GROUP), BF), pltpu.VMEM((count, GROUP, D), BF)]
        + [head_rows(BF)] * 5
        + [head_rows(F32)] * 3
        + [
            pltpu.VMEM((T, 4 * GROUP), BF),
            pltpu.VMEM((T, D), F32),
            pltpu.VMEM((T, D), F32),
            pltpu.VMEM((count, 2, 4, 128, 3 * GROUP), BF),
            pltpu.VMEM((count, 2, 2, 128, WIDE), BF),
            pltpu.SemaphoreType.DMA((count, 16)),
            pltpu.SemaphoreType.DMA((count, 6)),
            pltpu.SemaphoreType.DMA((2,)),
        ],
        compiler_params=pltpu.CompilerParams(vmem_limit_bytes=VMEM_UNIT),
        cost_estimate=LONG,
        name="attn_unit",
    )(table, na, gr, bias, *tables, *pieces, *rest, *inputs)


def qkv_blocks(pair):
    return [
        (part * D + (2 * group + shard) * 256 + pair * 128, group * 768 + part * 256 + shard * 128)
        for group in range(2)
        for part in range(3)
        for shard in range(2)
    ]


def attn_pack_kernel(pair, table, qkv, dense, *refs):
    *pieces, sems = refs
    copies = []
    for side, piece in enumerate(pieces):
        half = table[0] ^ side
        rows = pl.ds(pl.multiple_of(half * 128, 128), 128)
        made = [(qkv.at[rows, pl.ds(a, 128)], piece.at[0, :, pl.ds(b, 128)]) for a, b in qkv_blocks(pair)]
        made.append((dense.at[pl.ds(pair * 128, 128), columns_at(half * 512, 512)], piece.at[0, :, pl.ds(1536, 512)]))
        copies += [pltpu.make_async_copy(a, b, sems.at[side * 13 + i]) for i, (a, b) in enumerate(made)]
    start_all(copies)
    wait_all(copies)


def mlp_pack_kernel(unit, table, inner, outer, piece, sems):
    core = table[0]
    rows = pl.ds(pl.multiple_of(core * 128, 128), 128)
    made = [(inner.at[rows, pl.ds(a * 1024 + unit * 512, 512)], piece.at[0, 0, :, pl.ds(a * 512, 512)]) for a in range(4)]
    for part in range(2):
        source = outer.at[pl.ds(pl.multiple_of(unit * 512 + core * 256 + part * 128, 128), 128), :]
        made.append((source, piece.at[0, 1, :, pl.ds(part * D, D)]))
    copies = [pltpu.make_async_copy(a, b, sems.at[i]) for i, (a, b) in enumerate(made)]
    start_all(copies)
    wait_all(copies)


def pack(kernel, shape, count, sides, name, table, *weights):
    anywhere = pl.BlockSpec(memory_space=pl.ANY)
    return pl.pallas_call(
        kernel,
        in_specs=[pl.BlockSpec(memory_space=pltpu.SMEM)] + [anywhere] * len(weights),
        out_specs=[pl.BlockSpec(memory_space=pltpu.VMEM)] * sides,
        out_shape=[jax.ShapeDtypeStruct(shape, BF)] * sides,
        scratch_shapes=[pltpu.SemaphoreType.DMA((count * sides,))],
        cost_estimate=LONG,
        name=name,
    )(table, *weights)


def attn_place_kernel(table, *refs):
    *values, grad_qkv, grad_d = refs
    for i, value in enumerate(values):
        pair, half, part = i // 4, table[0] ^ (i // 2 % 2), table[10] ^ (i % 2)
        rows = pl.ds(pl.multiple_of(half * 128 + part * 64, 64), 64)
        for a, b in qkv_blocks(pair):
            grad_qkv[rows, pl.ds(a, 128)] = value[0, :, pl.ds(b, 128)].astype(F32)
        rows = pl.ds(pl.multiple_of(pair * 128 + part * 64, 64), 64)
        grad_d[rows, columns_at(half * 512, 512)] = value[0, :, pl.ds(1536, 512)].astype(F32)


def mlp_place_kernel(table, *refs):
    *values, grad_wi, grad_wo = refs
    for i, value in enumerate(values):
        unit, half = i // 4, table[0] ^ (i // 2 % 2)

        @pl.when(table[10] == i % 2)
        def _():
            rows = pl.ds(pl.multiple_of(half * 128, 128), 128)
            for tile in range(4):
                columns = pl.ds(tile * 1024 + unit * 512, 512)
                grad_wi[rows, columns] = value[0, rows_of(tile // 2, 128), rows_of(tile % 2, 512)].astype(F32)

        @pl.when(table[10] != i % 2)
        def _():
            for f in range(2):
                for part in range(2):
                    rows = pl.ds(unit * 512 + f * 256 + part * 128, 128)
                    columns = columns_at(half * 512, 512)
                    grad_wo[rows, columns] = value[0, rows_of(f, 128), rows_of(part, 512)].astype(F32)


def place(kernel, shapes, name, table, *values):
    inside = pl.BlockSpec(memory_space=pltpu.VMEM)
    return pl.pallas_call(
        kernel,
        in_specs=[pl.BlockSpec(memory_space=pltpu.SMEM)] + [inside] * len(values),
        out_specs=[inside] * len(shapes),
        out_shape=[jax.ShapeDtypeStruct(shape, F32) for shape in shapes],
        compiler_params=pltpu.CompilerParams(vmem_limit_bytes=VMEM),
        name=name,
    )(table, *values)


def add_kernel(*refs):
    *sources, target = refs
    target[...] = sum(source[...].astype(F32) for source in sources).astype(BF)


def add(*sources, count=1, cost=LONG):
    rows, columns = sources[0][0].shape[1:]
    steps = 2
    read = lambda first, stride: pl.BlockSpec(
        (1, rows // steps, columns), lambda i: (first + stride * (i // steps), i % steps, 0)
    )
    return pl.pallas_call(
        add_kernel,
        grid=(count * steps,),
        in_specs=[read(first, stride) for _, first, stride in sources],
        out_specs=read(0, 1),
        out_shape=jax.ShapeDtypeStruct((count, rows, columns), BF),
        cost_estimate=cost,
        name="add",
    )(*(array for array, _, _ in sources))


def split_add_kernel(table, *refs):
    *sources, kept, sent = refs
    total = sum(source[...].astype(F32) for source in sources).astype(BF)
    half = total.shape[1] // 2
    for parity in range(2):

        @pl.when(table[10] == parity)
        def _():
            kept[...] = total[:, rows_of(parity, half)]
            sent[...] = total[:, rows_of(1 - parity, half)]


def split_add(table, *arrays, cost=LONG):
    rows, columns = arrays[0].shape[1:]
    return pl.pallas_call(
        split_add_kernel,
        grid=(1,),
        in_specs=[pl.BlockSpec(memory_space=pltpu.SMEM)]
        + [pl.BlockSpec((1, rows, columns), lambda i: (0, 0, 0))] * len(arrays),
        out_specs=[pl.BlockSpec((1, rows // 2, columns), lambda i: (0, 0, 0))] * 2,
        out_shape=[jax.ShapeDtypeStruct((1, rows // 2, columns), BF)] * 2,
        cost_estimate=cost,
        name="split_add",
    )(table, *arrays)


AXES = ("z", "core", "y", "x")


def exchange(value, partner):
    pairs = []
    for z in range(4):
        for core in range(2):
            for shard in range(4):
                to_z, to_core, to_shard = partner(z, core, shard)
                pairs.append(((z * 2 + core) * 4 + shard, (to_z * 2 + to_core) * 4 + to_shard))
    return lax.ppermute(value, AXES, pairs)


to_core = lambda z, core, shard: (z, 1 - core, shard)
to_first = lambda z, core, shard: (z, core, shard ^ (1 + core))
to_second = lambda z, core, shard: (z, core, shard ^ (2 - core))
to_x = lambda z, core, shard: (z, core, shard ^ 1)
to_y = lambda z, core, shard: (z, core, shard ^ 2)
to_xy = lambda z, core, shard: (z, core, shard ^ 3)
to_below = lambda z, core, shard: (z ^ 1, core, shard)
to_two = lambda z, core, shard: (z ^ 2, core, shard)


def wide(value):
    return value.astype(F32)


def shards(
    layer_input, seq_lengths, out_grad, attn_gain, attn_shift, mlp_gain, mlp_shift, qkv_weight, qkv_bias,
    dense_weight, dense_bias, inner_weight, inner_bias, outer_weight, outer_bias,
):
    core = lax.axis_index("core")
    own = lax.axis_index("y") * 2 + lax.axis_index("x")
    steps = jnp.where(core == 0, jnp.array([0, 2, 1, 3], jnp.int32), jnp.array([0, 1, 2, 3], jnp.int32))
    shard_of = own ^ steps
    difference = own ^ jnp.arange(4, dtype=jnp.int32)
    block_of = jnp.where(core == 1, difference, ((difference & 1) << 1) | (difference >> 1))
    parity = lax.axis_index("z") % 2
    table = jnp.concatenate([core[None], seq_lengths, block_of, shard_of, parity[None]]).astype(jnp.int32)

    gather = lambda piece: lax.all_gather(piece, ("core", "y", "x"), axis=0, tiled=True)
    pack_attn = lambda pair, sides: pack(
        functools.partial(attn_pack_kernel, pair), (1, 128, 2 * D), 13, sides, "attn_pack", table, qkv_weight, dense_weight
    )
    pack_mlp = lambda unit: pack(
        functools.partial(mlp_pack_kernel, unit), (1, 2, 128, 2 * D), 6, 1, "mlp_pack", table, inner_weight, outer_weight
    )[0]

    def after(done, *values):
        return lax.optimization_barrier((done,) + values)

    part, rest = pack_attn(0, 2)
    vectors = (attn_gain, attn_shift, mlp_gain, mlp_shift, dense_bias, outer_bias, qkv_bias, inner_bias)
    part, table = after(part, table)
    from_first = exchange(part, to_first)
    from_second = exchange(part, to_second)
    packed = [pack_mlp(0), pack_mlp(1)]
    vectors = [vector.reshape(-1, 128) for vector in vectors]
    ends = np.cumsum([vector.shape[0] for vector in vectors])
    vectors = sum(jnp.pad(v, ((end - v.shape[0], 26 - end), (0, 0))) for v, end in zip(vectors, ends))
    vectors = [vectors] + [exchange(vectors, to) for to in (to_x, to_y, to_xy)]
    from_first, from_second, table, *packed = after(from_first, from_second, table, *packed)
    from_both = exchange(from_first, to_second)
    core_first = exchange(from_first, to_core)
    core_second = exchange(from_second, to_core)
    gain_a, shift_a, gain_m, shift_m, bias_out, *biases = spread(table, vectors)
    bias_pairs, bias_units = biases[:2], biases[2:]
    na, nm, gr = norm(table, layer_input, out_grad, (gain_a, shift_a, gain_m, shift_m))
    packed_b = pack_attn(1, 1)[0]
    from_both, na, packed_b, *packed = after(from_both, na, packed_b, *packed)
    pieces = [None] + [gather(piece) for piece in packed]
    na, from_both = after(na, from_both)
    core_both = exchange(from_both, to_core)
    pieces[0] = [part, from_second, from_first, from_both, rest, core_first, core_second, core_both]
    tables = [jnp.asarray(t) for t in rotary_tables()]

    far_blocks = lambda keep, got, cost=LONG: add((keep, 2, 1), (got, 1, 2), count=2, cost=cost)
    near_block = lambda keep, got, far, cost=LONG: add((keep, 1, 1), (got, 2, 1), (far, 1, 1), cost=cost)
    own_block = lambda *arrays: add(*((array, 0, 1) for array in arrays))
    plus = lambda total, got: add((total, 0, 1), (got, 0, 1), cost=None)

    none = (None, None)
    attn_call = lambda first, count, pair, parts, totals, rest=(): attn_unit(
        first, count, table, na, gr, bias_pairs[pair], tables, pieces[3 * pair], parts, totals, rest
    )
    mlp_call = lambda first, count, unit, parts, totals: mlp_unit(
        first, count, table, nm, gr, bias_units[unit], pieces[1 + unit], parts, totals
    )

    keep_a, send_a, gb0, out, dna = attn_call(0, 2, 0, none, none)
    got_a = exchange(send_a, to_core)
    out, keep_a, got_a = after(out, keep_a, got_a)
    far_a = far_blocks(keep_a, got_a)
    out, far_a = after(out, far_a)
    far_a = exchange(far_a, to_first)

    keep_m, send_m, gbi0, out, dnm = mlp_call(0, 4, 0, none, (out, None))
    got_m = exchange(send_m, to_core)
    out, keep_a, got_a, far_a = after(out, keep_a, got_a, far_a)
    near_a = near_block(keep_a, got_a, far_a)
    near_a, keep_m, got_m = after(near_a, keep_m, got_m)
    far_m = far_blocks(keep_m, got_m)
    out, near_a, far_m = after(out, near_a, far_m)
    near_a = exchange(near_a, to_second)
    far_m = exchange(far_m, to_first)

    keep_n, send_n, gbi1a, out, dnm = mlp_call(0, 2, 1, none, (out, dnm))
    out, keep_a, got_a, far_a, near_a, keep_m, got_m, far_m = after(
        out, keep_a, got_a, far_a, near_a, keep_m, got_m, far_m
    )
    kept_a, sent_a = split_add(table, keep_a, got_a, far_a, near_a)
    near_m = near_block(keep_m, got_m, far_m)
    out, kept_a, sent_a, near_m, packed_b = after(out, kept_a, sent_a, near_m, packed_b)
    pieces.append(gather(packed_b))
    sent_a = exchange(sent_a, to_below)
    near_m = exchange(near_m, to_second)

    keep_n, send_n, gbi1b, out, dnm = mlp_call(2, 2, 1, (keep_n, send_n), (out, dnm))
    got_n = exchange(send_n, to_core)
    out, kept_a, sent_a, keep_m, got_m, far_m, near_m = after(
        out, kept_a, sent_a, keep_m, got_m, far_m, near_m
    )
    kept_m, sent_m = split_add(table, keep_m, got_m, far_m, near_m)
    kept_a = plus(kept_a, sent_a)
    kept_m, sent_m, kept_a, keep_n, got_n = after(kept_m, sent_m, kept_a, keep_n, got_n)
    far_n = far_blocks(keep_n, got_n)
    out, kept_m, sent_m, kept_a, far_n = after(out, kept_m, sent_m, kept_a, far_n)
    got_kept_a = exchange(kept_a, to_two)
    sent_m = exchange(sent_m, to_below)
    far_n = exchange(far_n, to_first)

    keep_b, send_b, gb1a, out, dna = attn_call(0, 1, 1, none, (out, dna))
    out, kept_a, got_kept_a, kept_m, sent_m, keep_n, got_n, far_n = after(
        out, kept_a, got_kept_a, kept_m, sent_m, keep_n, got_n, far_n
    )
    kept_a = plus(kept_a, got_kept_a)
    kept_m = plus(kept_m, sent_m)
    near_n = near_block(keep_n, got_n, far_n)
    out, kept_a, kept_m, near_n = after(out, kept_a, kept_m, near_n)
    got_kept_m = exchange(kept_m, to_two)
    near_n = exchange(near_n, to_second)
    pieces_a = [kept_a, exchange(kept_a, to_below), exchange(kept_a, to_core)]

    rest = (layer_input, bias_out)
    keep_b, send_b, gb1b, layer_output, dna = attn_call(1, 1, 1, (keep_b, send_b), (out, dna), rest)
    got_b = exchange(send_b, to_core)
    layer_output, keep_n, got_n, far_n, near_n, kept_m, got_kept_m, *pieces_a = after(
        layer_output, keep_n, got_n, far_n, near_n, kept_m, got_kept_m, *pieces_a
    )
    kept_n, sent_n = split_add(table, keep_n, got_n, far_n, near_n)
    kept_n, sent_n, keep_b, got_b = after(kept_n, sent_n, keep_b, got_b)
    far_b = far_blocks(keep_b, got_b, None)
    far_b, kept_n, sent_n, kept_m, got_kept_m, dna, dnm = after(far_b, kept_n, sent_n, kept_m, got_kept_m, dna, dnm)
    far_b = exchange(far_b, to_first)
    sent_n = exchange(sent_n, to_below)
    pieces_a.append(exchange(pieces_a[1], to_core))

    bias_sums = [gb0, gb1a, gb1b, gbi0, gbi1a, gbi1b]
    input_grad, small = finish(table, layer_input, gr, dna, dnm, (gain_a, gain_m), bias_sums)
    small, far_b, keep_b, got_b = after(small, far_b, keep_b, got_b)
    near_b = near_block(keep_b, got_b, far_b, None)
    near_b, small, kept_n, sent_n = after(near_b, small, kept_n, sent_n)
    near_b = exchange(near_b, to_second)
    got_small = exchange(small, to_core)
    kept_n = plus(kept_n, sent_n)
    kept_m = plus(kept_m, got_kept_m)
    kept_n, kept_m, near_b, small, got_small = after(kept_n, kept_m, near_b, small, got_small)
    kept_b, sent_b = split_add(table, keep_b, got_b, far_b, near_b, cost=None)
    small = small + got_small
    kept_b, sent_b, small, kept_m = after(kept_b, sent_b, small, kept_m)
    sent_b = exchange(sent_b, to_below)
    got_kept_n = exchange(kept_n, to_two)
    got_small = exchange(small, to_x)
    pieces_m = [kept_m, exchange(kept_m, to_below), exchange(kept_m, to_core)]
    small, got_small, kept_b, sent_b = after(small, got_small, kept_b, sent_b)
    kept_b = plus(kept_b, sent_b)
    small = small + got_small
    kept_b, small, kept_n, got_kept_n = after(kept_b, small, kept_n, got_kept_n)
    got_kept_b = exchange(kept_b, to_two)
    got_small = exchange(small, to_y)
    kept_n = plus(kept_n, got_kept_n)
    pieces_n = [kept_n, exchange(kept_n, to_below), exchange(kept_n, to_core)]
    small, got_small, kept_b, got_kept_b, *pieces_n = after(small, got_small, kept_b, got_kept_b, *pieces_n)
    kept_b = plus(kept_b, got_kept_b)
    small = small + got_small
    kept_b, small = after(kept_b, small)
    pieces_b = [kept_b, exchange(kept_b, to_below), exchange(kept_b, to_core)]
    pieces_n.append(exchange(pieces_n[1], to_core))
    pieces_m.append(exchange(pieces_m[1], to_core))
    got_small = exchange(small, to_below)
    grad_wi, grad_wo = place(mlp_place_kernel, ((256, FF), (1024, D)), "mlp_place", table, *pieces_m, *pieces_n)
    grad_wi, small, got_small, *pieces_b = after(grad_wi, small, got_small, *pieces_b)
    pieces_b.append(exchange(pieces_b[1], to_core))
    small = small + got_small
    got_small = exchange(small, to_two)
    grad_qkv, grad_d = place(
        attn_place_kernel, ((256, 3 * D), (256, D)), "attn_place", table, *pieces_a, *pieces_b
    )
    grad_d, small, got_small = after(grad_d, small, got_small)
    small = lax.dynamic_index_in_dim(small + got_small, own, 0, keepdims=False)
    g_ga, g_sa, g_gm, g_sm, g_bd, g_bqkv, g_bi = jnp.split(small, np.cumsum([256] * 5 + [768]))
    return (
        layer_output, input_grad, g_ga, g_sa, g_gm, g_sm, grad_qkv, g_bqkv, grad_d, g_bd, grad_wi, g_bi, grad_wo, g_bd,
    )


def solution(mesh):
    replicas, shard_count = mesh.shape["rep"], mesh.shape["shard"]
    shape = (replicas // 2, 2, 2, shard_count // 2)
    cut = Mesh(mesh.devices.reshape(shape), ("z", "core", "y", "x"))
    both = P(("z", "core", "y", "x"), None)
    shard = P(("y", "x"))
    matrix = P(("y", "x"), None)
    weights = (shard,) * 4 + (matrix, shard) * 4
    body = shards if (replicas, shard_count) == (8, 4) else general_shards
    return jax.shard_map(
        body,
        mesh=cut,
        in_specs=(both, P(("z", "core", "y", "x")), both) + weights,
        out_specs=(both, both) + weights,
        check_vma=False,
    )
```

```python
import functools

import jax
import jax.numpy as jnp
import numpy as np
from jax import lax
from jax.experimental import pallas as pl
from jax.experimental.pallas import tpu as pltpu
from jax.sharding import Mesh, PartitionSpec as P

D = 1024
H = 16
FF = 4096
HD = 64
ROT = 16
T = 1024
GROUP = 256
HEADS = GROUP // HD
ROWS = 256
EPSILON = 1e-05
MASKED = -1e30
BF = jnp.bfloat16
F32 = jnp.float32
VMEM = 60 * 2**20


def nn(a, b):
    return lax.dot_general(a, b, (((1,), (0,)), ((), ())), preferred_element_type=F32)


def nt(a, b):
    return lax.dot_general(a, b, (((1,), (1,)), ((), ())), preferred_element_type=F32)


def tn(a, b):
    return lax.dot_general(a, b, (((0,), (0,)), ((), ())), preferred_element_type=F32)


def rows_of(index, size):
    return slice(index * size, (index + 1) * size)


def rotary_tables():
    half = ROT // 2
    inverse = 1.0 / np.float32(10000.0) ** (np.arange(half, dtype=np.float32) * np.float32(2.0 / ROT))
    angles = np.arange(T, dtype=np.float32)[:, None] * inverse.astype(np.float32)[None, :]
    cosine = np.ones((T, HD), np.float32)
    ahead = np.zeros((T, HD), np.float32)
    behind = np.zeros((T, HD), np.float32)
    cosine[:, :half] = np.cos(angles)
    cosine[:, half:ROT] = np.cos(angles)
    ahead[:, :half] = -np.sin(angles)
    behind[:, half:ROT] = np.sin(angles)
    return [np.tile(table, (1, 2)) for table in (cosine, ahead, behind)]


def add_columns(ref, rows, value, order):
    width = value.shape[1] // len(order)
    for place, block in enumerate(order):
        ref[rows, rows_of(block, width)] += value[:, rows_of(place, width)]


def mlp_kernel(order, nm, gr, wi, bi, wo, out, dn, gwi, gwo, gbi, act, ig):
    @pl.when(pl.program_id(0) == 0)
    def _():
        out[...] = jnp.zeros_like(out)
        dn[...] = jnp.zeros_like(dn)

    bias_sum = jnp.zeros(gbi.shape, F32)
    for t in range(T // ROWS):
        r = rows_of(t, ROWS)
        inner = nn(nm[r, :], wi[...]) + bi[...]
        grad = nt(gr[r, :], wo[...])
        normal = 0.5 * lax.erf(inner * 0.7071067811865476) + 0.5
        slope = normal + inner * jnp.exp(-0.5 * inner * inner) * 0.3989422804014327
        act[r, :] = (inner * normal).astype(BF)
        inner_grad = (grad * slope).astype(BF)
        ig[r, :] = inner_grad
        bias_sum += jnp.sum(inner_grad.astype(F32), axis=0, keepdims=True)
    gbi[...] = bias_sum
    for t in range(T // ROWS):
        r = rows_of(t, ROWS)
        out[r, :] += nn(act[r, :], wo[...])
        add_columns(dn, r, nt(ig[r, :], wi[...]), order)
    for d in range(D // ROWS):
        r = rows_of(d, ROWS)
        gwi[r, :] = tn(nm[:, r], ig[...]).astype(BF)
    step = min(ROWS, act.shape[1])
    for f in range(act.shape[1] // step):
        r = rows_of(f, step)
        gwo[r, :] = tn(act[:, r], gr[...]).astype(BF)


def mlp(order, nm, gr, wi, bi, wo):
    tile = FF // len(order)
    half = len(order) // 2
    one = pl.Buffered(1)
    whole = lambda: pl.BlockSpec((T, D), lambda i: (0, 0), pipeline_mode=one)
    total = lambda: pl.BlockSpec((T, D), lambda i: (0, 0))
    columns = lambda rows: pl.BlockSpec((rows, tile), lambda i: (0, (i % half) * 2 + i // half))
    return pl.pallas_call(
        functools.partial(mlp_kernel, order),
        grid=(FF // tile,),
        in_specs=[whole(), whole(), columns(D), columns(1), pl.BlockSpec((tile, D), lambda i: (i, 0))],
        out_specs=[total(), total(), columns(D), pl.BlockSpec((tile, D), lambda i: (i, 0)), columns(1)],
        out_shape=[
            jax.ShapeDtypeStruct((T, D), F32),
            jax.ShapeDtypeStruct((T, D), F32),
            jax.ShapeDtypeStruct((D, FF), BF),
            jax.ShapeDtypeStruct((FF, D), BF),
            jax.ShapeDtypeStruct((1, FF), F32),
        ],
        scratch_shapes=[pltpu.VMEM((T, tile), BF), pltpu.VMEM((T, tile), BF)],
        compiler_params=pltpu.CompilerParams(vmem_limit_bytes=VMEM),
        cost_estimate=pl.CostEstimate(flops=12 * T * D * FF, bytes_accessed=60 * 2**20, transcendentals=2 * T * FF),
        name="mlp",
    )(nm, gr, wi, bi, wo)


def attn_kernel(
    order, length, na, gr, wq, wk, wv, bq, bk, bv, wd, cosine, ahead, behind,
    out, dn, gwq, gwk, gwv, gwd, gb,
    q, k, v, dc, ctx, dq, dk, dv, grads,
):
    @pl.when(pl.program_id(0) == 0)
    def _():
        out[...] = jnp.zeros_like(out)
        dn[...] = jnp.zeros_like(dn)

    def turn(x, r, back):
        parts = []
        for p in range(GROUP // 128):
            pair = x[:, rows_of(p, 128)]
            straight = pair * cosine[r, :]
            across = (
                pltpu.roll(pair, 128 - ROT // 2, 1) * ahead[r, :]
                + pltpu.roll(pair, ROT // 2, 1) * behind[r, :]
            )
            parts.append(straight - across if back else straight + across)
        return jnp.concatenate(parts, axis=1)

    for t in range(T // ROWS):
        r = rows_of(t, ROWS)
        x = na[r, :]
        queries = (turn(nn(x, wq[...]) + bq[...], r, False).astype(BF) * 0.125).astype(BF)
        keys = turn(nn(x, wk[...]) + bk[...], r, False).astype(BF)
        values = (nn(x, wv[...]) + bv[...]).astype(BF)
        context_grad = nt(gr[r, :], wd[...]).astype(BF)
        for h in range(HEADS):
            c = rows_of(h, HD)
            q[h, r, :] = queries[:, c]
            k[h, r, :] = keys[:, c]
            v[h, r, :] = values[:, c]
            dc[h, r, :] = context_grad[:, c]

    block = 256
    inside = lax.broadcasted_iota(jnp.int32, (1, T), 1) < length[0]
    bias = jnp.where(inside, 0.0, MASKED).astype(F32)
    below = lax.broadcasted_iota(jnp.int32, (block, block), 1) <= lax.broadcasted_iota(jnp.int32, (block, block), 0)
    causal = jnp.where(below, 0.0, MASKED).astype(F32)

    def head(h, carry):
        dk[h] = jnp.zeros((T, HD), F32)
        dv[h] = jnp.zeros((T, HD), F32)
        for i in range(T // block):
            r = rows_of(i, block)
            spans = ([slice(0, i * block)] if i else []) + [r]
            query = q[h, r, :]
            scores = [nt(query, k[h, c, :]) + bias[:, c] for c in spans]
            scores[-1] += causal
            top = functools.reduce(jnp.maximum, [jnp.max(s, axis=1, keepdims=True) for s in scores])
            weights = [jnp.exp(s - top) for s in scores]
            scale = 1.0 / sum(jnp.sum(w, axis=1, keepdims=True) for w in weights)
            low = [w.astype(BF) for w in weights]
            context = sum(nn(w, v[h, c, :]) for w, c in zip(low, spans))
            ctx[h, r, :] = (context * scale).astype(BF)
            scaled_grad = (dc[h, r, :].astype(F32) * scale).astype(BF)
            probs_grad = [nt(scaled_grad, v[h, c, :]) for c in spans]
            inner = scale * sum(jnp.sum(w * p, axis=1, keepdims=True) for w, p in zip(weights, probs_grad))
            score_grad = [(w * (p - inner)).astype(BF) for w, p in zip(weights, probs_grad)]
            dq[h, r, :] = sum(nn(s, k[h, c, :]) for s, c in zip(score_grad, spans))
            for s, w, c in zip(score_grad, low, spans):
                dk[h, c, :] += tn(s, query)
                dv[h, c, :] += tn(w, scaled_grad)
        return carry

    lax.fori_loop(0, HEADS, head, 0)

    sums = [jnp.zeros((1, GROUP), F32) for _ in range(3)]
    together = lambda ref, r: jnp.concatenate([ref[h, r, :] for h in range(HEADS)], axis=1)
    for t in range(T // ROWS):
        r = rows_of(t, ROWS)
        context = together(ctx, r)
        grads[r, 3 * GROUP :] = context
        out[r, :] += nn(context, wd[...])
        pieces = (
            turn(together(dq, r) * 0.125, r, True).astype(BF),
            turn(together(dk, r), r, True).astype(BF),
            together(dv, r).astype(BF),
        )
        for p, piece in enumerate(pieces):
            grads[r, rows_of(p, GROUP)] = piece
            sums[p] += jnp.sum(piece.astype(F32), axis=0, keepdims=True)
        normed_grad = sum(nt(piece, w[...]) for piece, w in zip(pieces, (wq, wk, wv)))
        add_columns(dn, r, normed_grad, order)
    for p in range(3):
        gb[p : p + 1, :] = sums[p]
    for d in range(D // ROWS):
        r = rows_of(d, ROWS)
        x = na[:, r]
        for p, g in enumerate((gwq, gwk, gwv)):
            g[r, :] = tn(x, grads[:, rows_of(p, GROUP)]).astype(BF)
    gwd[...] = tn(grads[:, 3 * GROUP :], gr[...]).astype(BF)


def attn(order, length, na, gr, weight, bias, wd):
    groups = D // GROUP
    one = pl.Buffered(1)
    whole = lambda shape: pl.BlockSpec(shape, lambda i: (0, 0), pipeline_mode=one)
    total = lambda: pl.BlockSpec((T, D), lambda i: (0, 0))
    columns = lambda rows, part=0: pl.BlockSpec((rows, GROUP), lambda i: (0, i + part * groups))
    head_rows = lambda dtype: pltpu.VMEM((HEADS, T, HD), dtype)
    return pl.pallas_call(
        functools.partial(attn_kernel, order),
        grid=(groups,),
        in_specs=[pl.BlockSpec(memory_space=pltpu.SMEM), whole((T, D)), whole((T, D))]
        + [columns(D, p) for p in range(3)]
        + [columns(1, p) for p in range(3)]
        + [pl.BlockSpec((GROUP, D), lambda i: (i, 0))]
        + [whole((T, 128))] * 3,
        out_specs=[total(), total()] + [columns(D)] * 3 + [pl.BlockSpec((GROUP, D), lambda i: (i, 0)), columns(3)],
        out_shape=[jax.ShapeDtypeStruct((T, D), F32)] * 2
        + [jax.ShapeDtypeStruct((D, D), BF)] * 4
        + [jax.ShapeDtypeStruct((3, D), F32)],
        scratch_shapes=[head_rows(BF)] * 5 + [head_rows(F32)] * 3 + [pltpu.VMEM((T, 4 * GROUP), BF)],
        compiler_params=pltpu.CompilerParams(vmem_limit_bytes=VMEM),
        cost_estimate=pl.CostEstimate(flops=90 * 10**9, bytes_accessed=40 * 2**20, transcendentals=10 * 2**20),
        name="attn",
    )(length, na, gr, weight, weight, weight, bias, bias, bias, wd, *map(jnp.asarray, rotary_tables()))


def general_shards(
    layer_input, seq_lengths, out_grad, attn_gain, attn_shift, mlp_gain, mlp_shift, qkv_weight, qkv_bias,
    dense_weight, dense_bias, inner_weight, inner_bias, outer_weight, outer_bias,
):
    groupings = ("core", "y", "x")
    shard_count = lax.axis_size("y") * lax.axis_size("x")
    core = lax.axis_index("core")
    order = [2 * a + h for h in range(2) for a in range(shard_count)]

    def gather(piece):
        half = piece.shape[0] // 2
        mine = lax.dynamic_slice_in_dim(piece, core * half, half, 0)
        return lax.all_gather(mine, groupings, axis=0, tiled=True)

    def natural(rows):
        return jnp.swapaxes(rows.reshape(2, shard_count, -1, rows.shape[1]), 0, 1).reshape(rows.shape)

    def halves_first(rows):
        return jnp.swapaxes(rows.reshape(shard_count, 2, -1, rows.shape[1]), 0, 1).reshape(rows.shape)

    vectors = jnp.concatenate(
        [attn_gain, attn_shift, mlp_gain, mlp_shift, dense_bias, outer_bias, qkv_bias, inner_bias]
    )
    vectors = lax.all_gather(vectors, ("y", "x"), axis=0, tiled=False).astype(F32)
    sizes = [D] * 6 + [3 * D, FF]
    cuts = np.cumsum([size // shard_count for size in sizes])[:-1]
    gain_a, shift_a, gain_m, shift_m, bias_d, bias_o, bias_qkv, bias_i = (
        part.reshape(1, -1) for part in jnp.split(vectors, cuts, axis=1)
    )
    wi = gather(inner_weight)
    wo = gather(outer_weight)
    wqkv = gather(qkv_weight)
    wd = natural(gather(dense_weight))

    x = layer_input.astype(F32)
    mean = jnp.mean(x, axis=1, keepdims=True)
    centered = x - mean
    inverse = lax.rsqrt(jnp.mean(centered * centered, axis=1, keepdims=True) + EPSILON)
    unit = centered * inverse
    valid = jnp.arange(T, dtype=jnp.int32)[:, None] < seq_lengths[0]
    gr = jnp.where(valid, out_grad, jnp.zeros_like(out_grad))
    blocked = lambda rows: jnp.swapaxes(rows.reshape(T, shard_count, 2, -1), 1, 2).reshape(T, D)
    nm = blocked((unit * gain_m + shift_m).astype(BF))
    na = blocked((unit * gain_a + shift_a).astype(BF))

    out_m, dnm, gwi, gwo, gbi = mlp(order, nm, gr, wi, bias_i, wo)
    out_a, dna, gwq, gwk, gwv, gwd, gbqkv = attn(order, seq_lengths, na, gr, wqkv, bias_qkv, wd)

    def reduce(grad):
        part = lax.psum_scatter(grad, "core", scatter_dimension=0, tiled=True)
        part = lax.psum_scatter(part, ("y", "x"), scatter_dimension=0, tiled=True)
        part = lax.psum(part, "z")
        return lax.all_gather(part, "core", axis=0, tiled=True).astype(F32)

    grad_wi = reduce(gwi)
    grad_wo = reduce(gwo)
    grad_d = reduce(halves_first(gwd))
    grad_qkv = jnp.concatenate([reduce(g) for g in (gwq, gwk, gwv)], axis=1)

    layer_output = x + out_m + out_a + (bias_d + bias_o)
    g = dna * gain_a + dnm * gain_m
    gr32 = gr.astype(F32)
    input_grad = gr32 + inverse * (
        g - jnp.mean(g, axis=1, keepdims=True) - unit * jnp.mean(g * unit, axis=1, keepdims=True)
    )
    column = lambda rows: jnp.sum(rows, axis=0)
    parts = [column(dna * unit), column(dna), column(dnm * unit), column(dnm), column(gr32), gbqkv, gbi]
    small = jnp.concatenate([p.reshape(shard_count, -1) for p in parts], axis=1)
    small = lax.psum_scatter(small, ("y", "x"), scatter_dimension=0, tiled=True)
    small = lax.psum(small, ("z", "core"))
    cuts = np.cumsum([size // shard_count for size in [D] * 5 + [3 * D, FF]])[:-1]
    g_ga, g_sa, g_gm, g_sm, g_bd, g_bqkv, g_bi = (p.reshape(-1) for p in jnp.split(small, cuts, axis=1))
    return (
        layer_output, input_grad, g_ga, g_sa, g_gm, g_sm, grad_qkv, g_bqkv, grad_d, g_bd, grad_wi, g_bi, grad_wo, g_bd,
    )


WIDE = 512
VMEM_UNIT = 56 * 2**20
LONG = pl.CostEstimate(flops=10**13, bytes_accessed=2**20, transcendentals=0)


def columns_at(start, size):
    return pl.ds(pl.multiple_of(start, 128), size)


def spread_kernel(table, *refs):
    *given, gain_a, shift_a, gain_m, shift_m, bias, first_pair, second_pair, first_unit, second_unit = refs
    for j, ref in enumerate(given):
        shard = table[6] ^ j
        rows = ref[...].astype(F32)
        row = lambda k: rows[k : k + 1, :]
        for i, out in enumerate((gain_a, shift_a, gain_m, shift_m)):
            for k in range(2):
                out[:, columns_at(shard * 256 + k * 128, 128)] = row(2 * i + k)
        for k in range(2):
            bias[:, columns_at(shard * 256 + k * 128, 128)] = row(8 + k) + row(10 + k)
        for k in range(6):
            column = shard * 768 + k * 128
            part, owner = column >> 10, (column & 1023) >> 8
            target = (owner >> 1) * 768 + part * 256 + (owner & 1) * 128
            (first_pair, second_pair)[k % 2][:, columns_at(target, 128)] = row(12 + k)
        for k in range(8):
            (first_unit, second_unit)[k // 4][:, columns_at(shard * 512 + k % 4 * 128, 128)] = row(18 + k)


def spread(table, given):
    inside = pl.BlockSpec(memory_space=pltpu.VMEM)
    widths = [D] * 5 + [1536] * 2 + [2048] * 2
    return pl.pallas_call(
        spread_kernel,
        in_specs=[pl.BlockSpec(memory_space=pltpu.SMEM)] + [inside] * len(given),
        out_specs=[inside] * len(widths),
        out_shape=[jax.ShapeDtypeStruct((1, width), F32) for width in widths],
        name="spread",
    )(table, *given)


def norm_kernel(table, x, grad, gain_a, shift_a, gain_m, shift_m, na, nm, gr):
    values = x[...].astype(F32)
    mean = jnp.mean(values, axis=1, keepdims=True)
    centered = values - mean
    unit = centered * lax.rsqrt(jnp.mean(centered * centered, axis=1, keepdims=True) + EPSILON)
    rows = x.shape[0]
    position = pl.program_id(0) * rows + lax.broadcasted_iota(jnp.int32, (rows, 1), 0)
    gr[...] = jnp.where(position < table[1], grad[...].astype(F32), 0.0).astype(BF)
    for out, gain, shift in ((na, gain_a, shift_a), (nm, gain_m, shift_m)):
        normed = (unit * gain[...] + shift[...]).astype(BF)
        for a in range(4):
            for h in range(2):
                place = (table[2 + a] * 2 + (table[0] ^ h)) * 128
                out[:, columns_at(place, 128)] = normed[:, rows_of(a * 2 + h, 128)]


def norm(table, x, grad, vectors):
    tile = pl.BlockSpec((ROWS, D), lambda i: (i, 0))
    row = pl.BlockSpec((1, D), lambda i: (0, 0))
    return pl.pallas_call(
        norm_kernel,
        grid=(T // ROWS,),
        in_specs=[pl.BlockSpec(memory_space=pltpu.SMEM), tile, tile] + [row] * 4,
        out_specs=[tile] * 3,
        out_shape=[jax.ShapeDtypeStruct((T, D), BF)] * 3,
        compiler_params=pltpu.CompilerParams(vmem_limit_bytes=VMEM),
        cost_estimate=LONG,
        name="norm",
    )(table, x, grad, *vectors)


def finish_kernel(table, x, gr, dna, dnm, gain_a, gain_m, *refs):
    *bias_sums, input_grad, small, sums = refs
    values = x[...].astype(F32)
    mean = jnp.mean(values, axis=1, keepdims=True)
    centered = values - mean
    inverse = lax.rsqrt(jnp.mean(centered * centered, axis=1, keepdims=True) + EPSILON)
    unit = centered * inverse

    def natural(ref):
        places = [(table[2 + a] * 2 + (table[0] ^ h)) * 128 for a in range(4) for h in range(2)]
        return jnp.concatenate([ref[:, columns_at(place, 128)] for place in places], axis=1)

    normed_a, normed_m = natural(dna), natural(dnm)
    upper = gr[...].astype(F32)
    g = normed_a * gain_a[...] + normed_m * gain_m[...]
    input_grad[...] = upper + inverse * (
        g - jnp.mean(g, axis=1, keepdims=True) - unit * jnp.mean(g * unit, axis=1, keepdims=True)
    )

    @pl.when(pl.program_id(0) == 0)
    def _():
        sums[...] = jnp.zeros_like(sums)

    for i, rows in enumerate((normed_a * unit, normed_a, normed_m * unit, normed_m, upper)):
        sums[i : i + 1, :] += jnp.sum(rows, axis=0, keepdims=True)

    @pl.when(pl.program_id(0) == T // ROWS - 1)
    def _():
        for i in range(5):
            for a in range(4):
                small[a : a + 1, rows_of(i, 256)] = sums[i : i + 1, rows_of(a, 256)]
        pair_sums, unit_sums = bias_sums[:3], bias_sums[3:]
        for pair in range(2):
            for a, b in qkv_blocks(pair):
                value = pair_sums[0] if pair == 0 else pair_sums[1 + b // 768]
                small[a // 768 : a // 768 + 1, pl.ds(1280 + a % 768, 128)] = value[:, pl.ds(b if pair == 0 else b % 768, 128)]
        for a in range(4):
            small[a : a + 1, pl.ds(2048, 512)] = unit_sums[0][:, rows_of(a, 512)]
            small[a : a + 1, pl.ds(2560, 512)] = unit_sums[1 + a // 2][:, rows_of(a % 2, 512)]


def finish(table, x, gr, dna, dnm, vectors, bias_sums):
    tile = pl.BlockSpec((ROWS, D), lambda i: (i, 0))
    row = lambda value: pl.BlockSpec(value.shape, lambda i: (0, 0))
    return pl.pallas_call(
        finish_kernel,
        grid=(T // ROWS,),
        in_specs=[pl.BlockSpec(memory_space=pltpu.SMEM)] + [tile] * 4 + [row(v) for v in (*vectors, *bias_sums)],
        out_specs=[tile, pl.BlockSpec((4, 3072), lambda i: (0, 0))],
        out_shape=[jax.ShapeDtypeStruct((T, D), F32), jax.ShapeDtypeStruct((4, 3072), F32)],
        scratch_shapes=[pltpu.VMEM((5, D), F32)],
        compiler_params=pltpu.CompilerParams(vmem_limit_bytes=VMEM),
        cost_estimate=LONG,
        name="finish",
    )(table, x, gr, dna, dnm, *vectors, *bias_sums)


class Totals:
    def __init__(self, refs_in, refs_out, scratch, sems):
        self.fresh = [ref is None for ref in refs_in]
        self.refs_in, self.refs_out, self.scratch, self.sems = refs_in, refs_out, scratch, sems

    def loads(self):
        return [
            pltpu.make_async_copy(source, self.scratch[i], self.sems.at[i])
            for i, source in enumerate(self.refs_in)
            if source is not None
        ]

    def stores(self):
        return [
            pltpu.make_async_copy(source, target, self.sems.at[i])
            for i, (source, target) in enumerate(zip(self.scratch, self.refs_out))
        ]

    def begin(self):
        for copy in self.loads():
            copy.start()
        for target, source in zip(self.scratch, self.refs_in):
            if source is None:
                target[...] = jnp.zeros_like(target)

    def ready(self):
        for copy in self.loads():
            copy.wait()


def start_all(copies):
    for copy in copies:
        copy.start()


def wait_all(copies):
    for copy in copies:
        copy.wait()


def mlp_unit_kernel(first, count, given, table, nm, gr, bi, pieces, *refs):
    refs = list(refs)
    olds = [refs.pop(0) if is_given else None for is_given in given]
    keep, send, gbi, out_ref, dn_ref, wi, wo, act, ig, out, dn, inner_stage, outer_stage, sems, out_sems, total_sems = refs
    step = pl.program_id(0)
    core = table[0]
    totals = Totals(olds[2:], (out_ref, dn_ref), (out, dn), total_sems)

    def copies(index):
        slot, tile = index % 2, first + index
        made = []
        for t in range(4):
            for half in range(2):
                piece = (core ^ half) * 4 + table[6 + t]
                source = pieces.at[piece, 0, :, columns_at(tile * WIDE, WIDE)]
                made.append((source, wi.at[slot, pl.ds(t * 256 + half * 128, 128), :]))
        for h in range(2):
            for part in range(2):
                source = pieces.at[h * 4 + tile, 1, :, pl.ds(part * D, D)]
                made.append((source, wo.at[slot, pl.ds(h * 256 + part * 128, 128), :]))
        return [pltpu.make_async_copy(a, b, sems.at[slot, i]) for i, (a, b) in enumerate(made)]

    def results(index):
        slot, tile = index % 2, first + index
        made = []
        for side, target in enumerate((keep, send)):
            inner_part = target.at[:, pl.ds(pl.multiple_of(tile // 2 * 128, 128), 128), columns_at((tile % 2) * WIDE, WIDE)]
            made.append((inner_stage.at[slot, side], inner_part))
            made.append((outer_stage.at[slot, side], target.at[table[2 + tile], pl.ds(256, 256)]))
        return [pltpu.make_async_copy(a, b, out_sems.at[slot, i]) for i, (a, b) in enumerate(made)]

    @pl.when(step == 0)
    def _():
        start_all(copies(step))
        totals.begin()

    @pl.when(step < count - 1)
    def _():
        start_all(copies(step + 1))

    wait_all(copies(step))
    slot = step % 2

    bias_sum = jnp.zeros(gbi.shape, F32)
    for t in range(T // ROWS):
        r = rows_of(t, ROWS)
        inner = nn(nm[r, :], wi[slot]) + bi[...]
        grad = nt(gr[r, :], wo[slot])
        normal = 0.5 * lax.erf(inner * 0.7071067811865476) + 0.5
        slope = normal + inner * jnp.exp(-0.5 * inner * inner) * 0.3989422804014327
        act[r, :] = (inner * normal).astype(BF)
        inner_grad = (grad * slope).astype(BF)
        ig[r, :] = inner_grad
        bias_sum += jnp.sum(inner_grad.astype(F32), axis=0, keepdims=True)
    gbi[...] = bias_sum

    @pl.when(step == 0)
    def _():
        totals.ready()

    for t in range(T // ROWS):
        r = rows_of(t, ROWS)
        out[r, :] += nn(act[r, :], wo[slot])
        dn[r, :] += nt(ig[r, :], wi[slot])

    @pl.when(step == count - 1)
    def _():
        start_all(totals.stores())

    if count > 2:

        @pl.when(step >= 2)
        def _():
            wait_all(results(step - 2))

    for t in range(4):
        grad = tn(nm[:, rows_of(t, 256)], ig[...]).astype(BF)
        inner_stage[slot, 0, t] = grad[:128]
        inner_stage[slot, 1, t] = grad[128:]
    for f in range(2):
        grad = tn(act[:, rows_of(f, 256)], gr[...])
        low, high = grad[:, :WIDE], grad[:, WIDE:]
        sides = (jnp.where(core == 0, low, high).astype(BF), jnp.where(core == 0, high, low).astype(BF))
        for side, value in enumerate(sides):
            for half in range(2):
                outer_stage[slot, side, rows_of(f, 128), rows_of(half, WIDE)] = value[rows_of(half, 128)]
    start_all(results(step))

    @pl.when(step == count - 1)
    def _():
        if count > 1:
            wait_all(results(step - 1))
        wait_all(results(step))
        wait_all(totals.stores())


def mlp_unit(first, count, table, nm, gr, bi, pieces, parts, totals):
    olds = list(parts) + list(totals)
    given = tuple(old is not None for old in olds)
    inputs = [old for old in olds if old is not None]
    aliases = {5 + n: (0, 1, 3, 4)[i] for n, i in enumerate(i for i in range(4) if given[i])}
    whole = pl.BlockSpec((T, D), lambda i: (0, 0), pipeline_mode=pl.Buffered(1))
    anywhere = pl.BlockSpec(memory_space=pl.ANY)
    return pl.pallas_call(
        functools.partial(mlp_unit_kernel, first, count, given),
        grid=(count,),
        in_specs=[pl.BlockSpec(memory_space=pltpu.SMEM), whole, whole, pl.BlockSpec((1, WIDE), lambda i: (0, first + i)), anywhere]
        + [anywhere] * len(inputs),
        out_specs=[anywhere, anywhere, pl.BlockSpec((1, WIDE), lambda i: (0, i)), anywhere, anywhere],
        out_shape=[jax.ShapeDtypeStruct((4, 512, D), BF)] * 2
        + [jax.ShapeDtypeStruct((1, count * WIDE), F32)]
        + [jax.ShapeDtypeStruct((T, D), F32)] * 2,
        input_output_aliases=aliases,
        scratch_shapes=[
            pltpu.VMEM((2, D, WIDE), BF),
            pltpu.VMEM((2, WIDE, D), BF),
            pltpu.VMEM((T, WIDE), BF),
            pltpu.VMEM((T, WIDE), BF),
            pltpu.VMEM((T, D), F32),
            pltpu.VMEM((T, D), F32),
            pltpu.VMEM((2, 2, 4, 128, WIDE), BF),
            pltpu.VMEM((2, 2, 256, D), BF),
            pltpu.SemaphoreType.DMA((2, 12)),
            pltpu.SemaphoreType.DMA((2, 4)),
            pltpu.SemaphoreType.DMA((2,)),
        ],
        compiler_params=pltpu.CompilerParams(vmem_limit_bytes=VMEM_UNIT),
        cost_estimate=LONG,
        name="mlp_unit",
    )(table, nm, gr, bi, pieces, *inputs)


def attn_unit_kernel(first, count, given, apart, last, table, na, gr, bias, cosine, ahead, behind, *refs):
    refs = list(refs)
    pieces = [refs.pop(0) for _ in range(8 if apart else 1)]
    rest = [refs.pop(0) for _ in range(2 if last else 0)]
    olds = [refs.pop(0) if is_given else None for is_given in given]
    (
        keep, send, gb, out_ref, dn_ref,
        w, wd, q, k, v, dc, ctx, dq, dk, dv, grads, out, dn, qkv_stage, dense_stage, sems, out_sems, total_sems,
    ) = refs
    step = pl.program_id(0)
    core = table[0]
    totals = Totals(olds[2:], (out_ref, dn_ref), (out, dn), total_sems)

    def copies(index):
        group = first + index
        made = []
        for t in range(4):
            for half in range(2):
                if apart:
                    piece = pieces[half * 4 + t].at[0]
                    place = wd.at[table[6 + t] // 2, pl.ds(pl.multiple_of(table[6 + t] % 2 * 128, 128), 128), columns_at((core ^ half) * 512, 512)]
                    if isinstance(index, int) and index == 0:
                        made.append((piece.at[:, pl.ds(1536, 512)], place))
                else:
                    piece = pieces[0].at[(core ^ half) * 4 + table[6 + t]]
                made.append((piece.at[:, columns_at(group * 768, 768)], w.at[index, pl.ds(t * 256 + half * 128, 128), :]))
        for pair in range(0 if apart else 2):
            for h in range(2):
                source = pieces[0].at[h * 4 + group * 2 + pair, :, pl.ds(1536, 512)]
                made.append((source, wd.at[index, pl.ds(pair * 128, 128), pl.ds(h * 512, 512)]))
        return [pltpu.make_async_copy(a, b, sems.at[index, i]) for i, (a, b) in enumerate(made)]

    def results(index):
        group = first + index
        made = []
        for side, target in enumerate((keep, send)):
            made.append((qkv_stage.at[index, side], target.at[:, :, columns_at(group * 768, 768)]))
            for pair in range(2):
                place = target.at[table[2 + group * 2 + pair], :, pl.ds(1536, 512)]
                made.append((dense_stage.at[index, side, pair], place))
        return [pltpu.make_async_copy(a, b, out_sems.at[index, i]) for i, (a, b) in enumerate(made)]

    @pl.when(step == 0)
    def _():
        for index in range(count):
            start_all(copies(index))
        totals.begin()

    for index in range(count):

        @pl.when(step == index)
        def _():
            wait_all(copies(index))

    def turn(x, r, back):
        parts = []
        for p in range(GROUP // 128):
            pair = x[:, rows_of(p, 128)]
            straight = pair * cosine[r, :]
            across = (
                pltpu.roll(pair, 128 - ROT // 2, 1) * ahead[r, :]
                + pltpu.roll(pair, ROT // 2, 1) * behind[r, :]
            )
            parts.append(straight - across if back else straight + across)
        return jnp.concatenate(parts, axis=1)

    part = [slice(p * GROUP, (p + 1) * GROUP) for p in range(4)]
    for t in range(T // ROWS):
        r = rows_of(t, ROWS)
        x = na[r, :]
        projected = nn(x, w[step]) + bias[...]
        queries = (turn(projected[:, part[0]], r, False).astype(BF) * 0.125).astype(BF)
        keys = turn(projected[:, part[1]], r, False).astype(BF)
        values = projected[:, part[2]].astype(BF)
        context_grad = nt(gr[r, :], wd[step]).astype(BF)
        for h in range(HEADS):
            c = rows_of(h, HD)
            q[h, r, :] = queries[:, c]
            k[h, r, :] = keys[:, c]
            v[h, r, :] = values[:, c]
            dc[h, r, :] = context_grad[:, c]

    block = 512
    inside = lax.broadcasted_iota(jnp.int32, (1, T), 1) < table[1]
    outside = jnp.where(inside, 0.0, MASKED).astype(F32)
    below = lax.broadcasted_iota(jnp.int32, (block, block), 1) <= lax.broadcasted_iota(jnp.int32, (block, block), 0)
    causal = jnp.where(below, 0.0, MASKED).astype(F32)

    def head(h, carry):
        dk[h] = jnp.zeros((HD, T), F32)
        dv[h] = jnp.zeros((HD, T), F32)
        for i in range(T // block):
            r = rows_of(i, block)
            spans = ([slice(0, i * block)] if i else []) + [r]
            query = q[h, r, :]
            scores = [nt(query, k[h, c, :]) + outside[:, c] for c in spans]
            scores[-1] += causal
            top = functools.reduce(jnp.maximum, [jnp.max(s, axis=1, keepdims=True) for s in scores])
            weights = [jnp.exp(s - top) for s in scores]
            scale = 1.0 / sum(jnp.sum(e, axis=1, keepdims=True) for e in weights)
            low = [e.astype(BF) for e in weights]
            context = sum(nn(e, v[h, c, :]) for e, c in zip(low, spans))
            ctx[h, r, :] = (context * scale).astype(BF)
            scaled_grad = (dc[h, r, :].astype(F32) * scale).astype(BF)
            probs_grad = [nt(scaled_grad, v[h, c, :]) for c in spans]
            inner = scale * sum(jnp.sum(e * p, axis=1, keepdims=True) for e, p in zip(weights, probs_grad))
            score_grad = [(e * (p - inner)).astype(BF) for e, p in zip(weights, probs_grad)]
            dq[h, r, :] = sum(nn(s, k[h, c, :]) for s, c in zip(score_grad, spans))
            query_turned, grad_turned = query.T, scaled_grad.T
            for s, e, c in zip(score_grad, low, spans):
                dk[h, :, c] += nn(query_turned, s)
                dv[h, :, c] += nn(grad_turned, e)
        return carry

    lax.fori_loop(0, HEADS, head, 0)

    @pl.when(step == 0)
    def _():
        totals.ready()

    sums = jnp.zeros((1, 3 * GROUP), F32)
    together = lambda ref, r: jnp.concatenate([ref[h, r, :] for h in range(HEADS)], axis=1)
    for t in range(T // ROWS):
        r = rows_of(t, ROWS)
        context = together(ctx, r)
        grads[r, part[3]] = context
        total = nn(context, wd[step])
        if last:
            total += rest[0][r, :].astype(F32) + rest[1][...]
        out[r, :] += total
        projected_grad = jnp.concatenate(
            [
                turn(together(dq, r) * 0.125, r, True).astype(BF),
                turn(jnp.concatenate([dk[h, :, r] for h in range(HEADS)], axis=0).T, r, True).astype(BF),
                jnp.concatenate([dv[h, :, r] for h in range(HEADS)], axis=0).T.astype(BF),
            ],
            axis=1,
        )
        grads[r, : 3 * GROUP] = projected_grad
        sums += jnp.sum(projected_grad.astype(F32), axis=0, keepdims=True)
        dn[r, :] += nt(projected_grad, w[step])
    gb[...] = sums

    @pl.when(step == count - 1)
    def _():
        start_all(totals.stores())

    for t in range(4):
        grad = tn(na[:, rows_of(t, 256)], grads[:, : 3 * GROUP]).astype(BF)
        qkv_stage[step, 0, t] = grad[:128]
        qkv_stage[step, 1, t] = grad[128:]
    grad = tn(grads[:, part[3]], gr[...])
    first_half, second_half = grad[:, :WIDE], grad[:, WIDE:]
    sides = (
        jnp.where(core == 0, first_half, second_half).astype(BF),
        jnp.where(core == 0, second_half, first_half).astype(BF),
    )
    for side, value in enumerate(sides):
        for pair in range(2):
            dense_stage[step, side, pair] = value[rows_of(pair, 128)]
    start_all(results(step))

    @pl.when(step == count - 1)
    def _():
        for index in range(count):
            wait_all(results(index))
        wait_all(totals.stores())


def attn_unit(first, count, table, na, gr, bias, tables, pieces, parts, totals, rest=()):
    olds = list(parts) + list(totals)
    given = tuple(old is not None for old in olds)
    inputs = [old for old in olds if old is not None]
    apart = isinstance(pieces, list)
    pieces = pieces if apart else [pieces]
    aliases = {7 + len(pieces) + len(rest) + n: (0, 1, 3, 4)[i] for n, i in enumerate(i for i in range(4) if given[i])}
    one = pl.Buffered(1)
    whole = pl.BlockSpec((T, D), lambda i: (0, 0), pipeline_mode=one)
    turns = pl.BlockSpec((T, 128), lambda i: (0, 0), pipeline_mode=one)
    anywhere = pl.BlockSpec(memory_space=pl.ANY)
    head_rows = lambda dtype: pltpu.VMEM((HEADS, T, HD), dtype)
    return pl.pallas_call(
        functools.partial(attn_unit_kernel, first, count, given, apart, len(rest) > 0),
        grid=(count,),
        in_specs=[pl.BlockSpec(memory_space=pltpu.SMEM), whole, whole, pl.BlockSpec((1, 3 * GROUP), lambda i: (0, first + i))]
        + [turns] * 3
        + [anywhere] * len(pieces)
        + [pl.BlockSpec(value.shape, lambda i: (0, 0), pipeline_mode=one) for value in rest]
        + [anywhere] * len(inputs),
        out_specs=[anywhere, anywhere, pl.BlockSpec((1, 3 * GROUP), lambda i: (0, i)), anywhere, anywhere],
        out_shape=[jax.ShapeDtypeStruct((4, 128, 2 * D), BF)] * 2
        + [jax.ShapeDtypeStruct((1, 3 * GROUP * count), F32)]
        + [jax.ShapeDtypeStruct((T, D), F32)] * 2,
        input_output_aliases=aliases,
        scratch_shapes=[pltpu.VMEM((count, D, 3 * GROUP), BF), pltpu.VMEM((count, GROUP, D), BF)]
        + [head_rows(BF)] * 5
        + [head_rows(F32)] + [pltpu.VMEM((HEADS, HD, T), F32)] * 2
        + [
            pltpu.VMEM((T, 4 * GROUP), BF),
            pltpu.VMEM((T, D), F32),
            pltpu.VMEM((T, D), F32),
            pltpu.VMEM((count, 2, 4, 128, 3 * GROUP), BF),
            pltpu.VMEM((count, 2, 2, 128, WIDE), BF),
            pltpu.SemaphoreType.DMA((count, 16)),
            pltpu.SemaphoreType.DMA((count, 6)),
            pltpu.SemaphoreType.DMA((2,)),
        ],
        compiler_params=pltpu.CompilerParams(vmem_limit_bytes=VMEM_UNIT),
        cost_estimate=LONG,
        name="attn_unit",
    )(table, na, gr, bias, *tables, *pieces, *rest, *inputs)


def qkv_blocks(pair):
    return [
        (part * D + (2 * group + shard) * 256 + pair * 128, group * 768 + part * 256 + shard * 128)
        for group in range(2)
        for part in range(3)
        for shard in range(2)
    ]


def attn_pack_kernel(pair, table, qkv, dense, *refs):
    *pieces, sems = refs
    copies = []
    for side, piece in enumerate(pieces):
        half = table[0] ^ side
        rows = pl.ds(pl.multiple_of(half * 128, 128), 128)
        made = [(qkv.at[rows, pl.ds(a, 128)], piece.at[0, :, pl.ds(b, 128)]) for a, b in qkv_blocks(pair)]
        made.append((dense.at[pl.ds(pair * 128, 128), columns_at(half * 512, 512)], piece.at[0, :, pl.ds(1536, 512)]))
        copies += [pltpu.make_async_copy(a, b, sems.at[side * 13 + i]) for i, (a, b) in enumerate(made)]
    start_all(copies)
    wait_all(copies)


def mlp_pack_kernel(unit, table, inner, outer, piece, sems):
    core = table[0]
    rows = pl.ds(pl.multiple_of(core * 128, 128), 128)
    made = [(inner.at[rows, pl.ds(a * 1024 + unit * 512, 512)], piece.at[0, 0, :, pl.ds(a * 512, 512)]) for a in range(4)]
    for part in range(2):
        source = outer.at[pl.ds(pl.multiple_of(unit * 512 + core * 256 + part * 128, 128), 128), :]
        made.append((source, piece.at[0, 1, :, pl.ds(part * D, D)]))
    copies = [pltpu.make_async_copy(a, b, sems.at[i]) for i, (a, b) in enumerate(made)]
    start_all(copies)
    wait_all(copies)


def pack(kernel, shape, count, sides, name, table, *weights):
    anywhere = pl.BlockSpec(memory_space=pl.ANY)
    return pl.pallas_call(
        kernel,
        in_specs=[pl.BlockSpec(memory_space=pltpu.SMEM)] + [anywhere] * len(weights),
        out_specs=[pl.BlockSpec(memory_space=pltpu.VMEM)] * sides,
        out_shape=[jax.ShapeDtypeStruct(shape, BF)] * sides,
        scratch_shapes=[pltpu.SemaphoreType.DMA((count * sides,))],
        cost_estimate=LONG,
        name=name,
    )(table, *weights)


def attn_place_kernel(table, *refs):
    *values, grad_qkv, grad_d = refs
    for i, value in enumerate(values):
        pair, half, part = i // 4, table[0] ^ (i // 2 % 2), table[10] ^ (i % 2)
        rows = pl.ds(pl.multiple_of(half * 128 + part * 64, 64), 64)
        for a, b in qkv_blocks(pair):
            grad_qkv[rows, pl.ds(a, 128)] = value[0, :, pl.ds(b, 128)].astype(F32)
        rows = pl.ds(pl.multiple_of(pair * 128 + part * 64, 64), 64)
        grad_d[rows, columns_at(half * 512, 512)] = value[0, :, pl.ds(1536, 512)].astype(F32)


def mlp_place_kernel(table, *refs):
    *values, grad_wi, grad_wo = refs
    for i, value in enumerate(values):
        unit, half = i // 4, table[0] ^ (i // 2 % 2)

        @pl.when(table[10] == i % 2)
        def _():
            rows = pl.ds(pl.multiple_of(half * 128, 128), 128)
            for tile in range(4):
                columns = pl.ds(tile * 1024 + unit * 512, 512)
                grad_wi[rows, columns] = value[0, rows_of(tile // 2, 128), rows_of(tile % 2, 512)].astype(F32)

        @pl.when(table[10] != i % 2)
        def _():
            for f in range(2):
                for part in range(2):
                    rows = pl.ds(unit * 512 + f * 256 + part * 128, 128)
                    columns = columns_at(half * 512, 512)
                    grad_wo[rows, columns] = value[0, rows_of(f, 128), rows_of(part, 512)].astype(F32)


def place(kernel, shapes, name, table, *values):
    inside = pl.BlockSpec(memory_space=pltpu.VMEM)
    return pl.pallas_call(
        kernel,
        in_specs=[pl.BlockSpec(memory_space=pltpu.SMEM)] + [inside] * len(values),
        out_specs=[inside] * len(shapes),
        out_shape=[jax.ShapeDtypeStruct(shape, F32) for shape in shapes],
        compiler_params=pltpu.CompilerParams(vmem_limit_bytes=VMEM),
        name=name,
    )(table, *values)


def add_kernel(*refs):
    *sources, target = refs
    target[...] = sum(source[...].astype(F32) for source in sources).astype(BF)


def add(*sources, count=1, cost=LONG):
    rows, columns = sources[0][0].shape[1:]
    steps = 2
    read = lambda first, stride: pl.BlockSpec(
        (1, rows // steps, columns), lambda i: (first + stride * (i // steps), i % steps, 0)
    )
    return pl.pallas_call(
        add_kernel,
        grid=(count * steps,),
        in_specs=[read(first, stride) for _, first, stride in sources],
        out_specs=read(0, 1),
        out_shape=jax.ShapeDtypeStruct((count, rows, columns), BF),
        cost_estimate=cost,
        name="add",
    )(*(array for array, _, _ in sources))


def sums_kernel(plan, table, *refs):
    refs = list(refs)
    taken = [[refs.pop(0) for _ in range(count)] for count, _ in plan]
    for sources, (_, split) in zip(taken, plan):
        total = sum(source[...].astype(F32) for source in sources).astype(BF)
        if not split:
            refs.pop(0)[...] = total
            continue
        kept, sent = refs.pop(0), refs.pop(0)

        @pl.when(pl.program_id(0) == table[10])
        def _():
            kept[...] = total

        @pl.when(pl.program_id(0) != table[10])
        def _():
            sent[...] = total


def sums(table, *jobs, cost=LONG):
    specs, arrays, out_specs, out_shapes, plan = [], [], [], [], []
    for split, sources in jobs:
        sources = [source if isinstance(source, tuple) else (source, 0) for source in sources]
        rows, columns = sources[0][0].shape[1] // 2, sources[0][0].shape[2]
        for array, block in sources:
            arrays.append(array)
            specs.append(pl.BlockSpec((1, rows, columns), lambda i, block=block: (block, i, 0)))
        plan.append((len(sources), split))
        place = (lambda i: (0, 0, 0)) if split else (lambda i: (0, i, 0))
        for _ in range(1 + split):
            out_specs.append(pl.BlockSpec((1, rows, columns), place))
            out_shapes.append(jax.ShapeDtypeStruct((1, rows * (1 if split else 2), columns), BF))
    return pl.pallas_call(
        functools.partial(sums_kernel, plan),
        grid=(2,),
        in_specs=[pl.BlockSpec(memory_space=pltpu.SMEM)] + specs,
        out_specs=out_specs,
        out_shape=out_shapes,
        compiler_params=pltpu.CompilerParams(vmem_limit_bytes=VMEM // 2),
        cost_estimate=cost,
        name="sums",
    )(table, *arrays)


AXES = ("z", "core", "y", "x")


def exchange(value, partner):
    pairs = []
    for z in range(4):
        for core in range(2):
            for shard in range(4):
                to_z, to_core, to_shard = partner(z, core, shard)
                pairs.append(((z * 2 + core) * 4 + shard, (to_z * 2 + to_core) * 4 + to_shard))
    return lax.ppermute(value, AXES, pairs)


to_core = lambda z, core, shard: (z, 1 - core, shard)
to_first = lambda z, core, shard: (z, core, shard ^ (1 + core))
to_second = lambda z, core, shard: (z, core, shard ^ (2 - core))
to_x = lambda z, core, shard: (z, core, shard ^ 1)
to_y = lambda z, core, shard: (z, core, shard ^ 2)
to_xy = lambda z, core, shard: (z, core, shard ^ 3)
to_below = lambda z, core, shard: (z ^ 1, core, shard)
to_two = lambda z, core, shard: (z ^ 2, core, shard)


def wide(value):
    return value.astype(F32)


def shards(
    layer_input, seq_lengths, out_grad, attn_gain, attn_shift, mlp_gain, mlp_shift, qkv_weight, qkv_bias,
    dense_weight, dense_bias, inner_weight, inner_bias, outer_weight, outer_bias,
):
    core = lax.axis_index("core")
    place_in_group = lax.axis_index("y") * 2 + lax.axis_index("x")
    steps = jnp.where(core == 0, jnp.array([0, 2, 1, 3], jnp.int32), jnp.array([0, 1, 2, 3], jnp.int32))
    shard_of = place_in_group ^ steps
    difference = place_in_group ^ jnp.arange(4, dtype=jnp.int32)
    block_of = jnp.where(core == 1, difference, ((difference & 1) << 1) | (difference >> 1))
    parity = lax.axis_index("z") % 2
    table = jnp.concatenate([core[None], seq_lengths, block_of, shard_of, parity[None]]).astype(jnp.int32)

    gather = lambda piece: lax.all_gather(piece, ("core", "y", "x"), axis=0, tiled=True)
    pack_attn = lambda pair, sides: pack(
        functools.partial(attn_pack_kernel, pair), (1, 128, 2 * D), 13, sides, "attn_pack", table, qkv_weight, dense_weight
    )
    pack_mlp = lambda unit: pack(
        functools.partial(mlp_pack_kernel, unit), (1, 2, 128, 2 * D), 6, 1, "mlp_pack", table, inner_weight, outer_weight
    )[0]

    def after(done, *values):
        return lax.optimization_barrier((done,) + values)

    part, rest = pack_attn(0, 2)
    from_first = exchange(part, to_first)
    from_second = exchange(part, to_second)
    vectors = (attn_gain, attn_shift, mlp_gain, mlp_shift, dense_bias, outer_bias, qkv_bias, inner_bias)
    part, table, *vectors = after(part, table, *vectors)
    vectors = [vector.reshape(-1, 128) for vector in vectors]
    ends = np.cumsum([vector.shape[0] for vector in vectors])
    vectors = sum(jnp.pad(v, ((end - v.shape[0], 26 - end), (0, 0))) for v, end in zip(vectors, ends))
    packed = [pack_mlp(0), pack_mlp(1)]
    vectors = [vectors] + [exchange(vectors, to) for to in (to_x, to_y, to_xy)]
    from_first, from_second, table, *packed = after(from_first, from_second, table, *packed)
    from_both = exchange(from_first, to_second)
    core_first = exchange(from_first, to_core)
    core_second = exchange(from_second, to_core)
    gain_a, shift_a, gain_m, shift_m, bias_out, *biases = spread(table, vectors)
    bias_pairs, bias_units = biases[:2], biases[2:]
    na, nm, gr = norm(table, layer_input, out_grad, (gain_a, shift_a, gain_m, shift_m))
    pieces = [None] + [gather(piece) for piece in packed]
    na, from_both = after(na, from_both)
    core_both = exchange(from_both, to_core)
    pieces[0] = [part, from_second, from_first, from_both, rest, core_first, core_second, core_both]
    tables = [jnp.asarray(t) for t in rotary_tables()]

    far_blocks = lambda keep, got, cost=LONG: add((keep, 2, 1), (got, 1, 2), count=2, cost=cost)
    near = lambda keep, got, far: (False, [(keep, 1), (got, 2), (far, 1)])
    own = lambda *arrays: (True, arrays)
    plus = lambda *arrays: (False, arrays)

    none = (None, None)
    attn_call = lambda first, count, pair, parts, totals, rest=(): attn_unit(
        first, count, table, na, gr, bias_pairs[pair], tables, pieces[3 * pair], parts, totals, rest
    )
    mlp_call = lambda first, count, unit, parts, totals: mlp_unit(
        first, count, table, nm, gr, bias_units[unit], pieces[1 + unit], parts, totals
    )

    keep_a, send_a, gb0, out, dna = attn_call(0, 2, 0, none, none)
    got_a = exchange(send_a, to_core)
    out, table = after(out, table)
    packed_b = pack_attn(1, 1)[0]
    out, keep_a, got_a, packed_b = after(out, keep_a, got_a, packed_b)
    far_a = far_blocks(keep_a, got_a)
    out, far_a = after(out, far_a)
    far_a = exchange(far_a, to_first)

    keep_m, send_m, gbi0, out, dnm = mlp_call(0, 4, 0, none, (out, None))
    got_m = exchange(send_m, to_core)
    out, keep_a, got_a, far_a = after(out, keep_a, got_a, far_a)
    (near_a,) = sums(table, near(keep_a, got_a, far_a))
    near_a, keep_m, got_m = after(near_a, keep_m, got_m)
    far_m = far_blocks(keep_m, got_m)
    out, near_a, far_m = after(out, near_a, far_m)
    near_a = exchange(near_a, to_second)
    far_m = exchange(far_m, to_first)

    keep_n, send_n, gbi1a, out, dnm = mlp_call(0, 2, 1, none, (out, dnm))
    out, keep_a, got_a, far_a, near_a, keep_m, got_m, far_m = after(
        out, keep_a, got_a, far_a, near_a, keep_m, got_m, far_m
    )
    kept_a, sent_a, near_m = sums(table, own(keep_a, got_a, far_a, near_a), near(keep_m, got_m, far_m))
    out, kept_a, sent_a, near_m, packed_b = after(out, kept_a, sent_a, near_m, packed_b)
    pieces.append(gather(packed_b))
    sent_a = exchange(sent_a, to_below)
    near_m = exchange(near_m, to_second)

    keep_n, send_n, gbi1b, out, dnm = mlp_call(2, 2, 1, (keep_n, send_n), (out, dnm))
    got_n = exchange(send_n, to_core)
    out, kept_a, sent_a, keep_m, got_m, far_m, near_m = after(
        out, kept_a, sent_a, keep_m, got_m, far_m, near_m
    )
    kept_m, sent_m, kept_a = sums(table, own(keep_m, got_m, far_m, near_m), plus(kept_a, sent_a))
    kept_m, sent_m, kept_a, keep_n, got_n = after(kept_m, sent_m, kept_a, keep_n, got_n)
    far_n = far_blocks(keep_n, got_n)
    out, kept_m, sent_m, kept_a, far_n = after(out, kept_m, sent_m, kept_a, far_n)
    got_kept_a = exchange(kept_a, to_two)
    sent_m = exchange(sent_m, to_below)
    far_n = exchange(far_n, to_first)

    keep_b, send_b, gb1a, out, dna = attn_call(0, 1, 1, none, (out, dna))
    out, kept_a, got_kept_a, kept_m, sent_m, keep_n, got_n, far_n = after(
        out, kept_a, got_kept_a, kept_m, sent_m, keep_n, got_n, far_n
    )
    kept_a, kept_m, near_n = sums(
        table, plus(kept_a, got_kept_a), plus(kept_m, sent_m), near(keep_n, got_n, far_n)
    )
    out, kept_a, kept_m, near_n = after(out, kept_a, kept_m, near_n)
    got_kept_m = exchange(kept_m, to_two)
    near_n = exchange(near_n, to_second)
    pieces_a = [kept_a, exchange(kept_a, to_below), exchange(kept_a, to_core)]

    rest = (layer_input, bias_out)
    keep_b, send_b, gb1b, layer_output, dna = attn_call(1, 1, 1, (keep_b, send_b), (out, dna), rest)
    got_b = exchange(send_b, to_core)
    layer_output, keep_n, got_n, far_n, near_n, kept_m, got_kept_m, *pieces_a = after(
        layer_output, keep_n, got_n, far_n, near_n, kept_m, got_kept_m, *pieces_a
    )
    kept_n, sent_n, kept_m = sums(table, own(keep_n, got_n, far_n, near_n), plus(kept_m, got_kept_m))
    kept_n, sent_n, keep_b, got_b = after(kept_n, sent_n, keep_b, got_b)
    sent_n = exchange(sent_n, to_below)
    pieces_m = [kept_m, exchange(kept_m, to_below), exchange(kept_m, to_core)]
    far_b = far_blocks(keep_b, got_b, None)
    far_b, dna, dnm = after(far_b, dna, dnm)
    far_b = exchange(far_b, to_first)
    pieces_a.append(exchange(pieces_a[1], to_core))

    bias_sums = [gb0, gb1a, gb1b, gbi0, gbi1a, gbi1b]
    input_grad, small = finish(table, layer_input, gr, dna, dnm, (gain_a, gain_m), bias_sums)
    small, kept_n, sent_n = after(small, kept_n, sent_n)
    (kept_n,) = sums(table, plus(kept_n, sent_n), cost=None)
    kept_n, small, far_b, keep_b, got_b = after(kept_n, small, far_b, keep_b, got_b)
    got_kept_n = exchange(kept_n, to_two)
    (near_b,) = sums(table, near(keep_b, got_b, far_b))
    near_b, small = after(near_b, small)
    near_b = exchange(near_b, to_second)
    got_small = exchange(small, to_core)
    near_b, small, got_small, *pieces_m = after(near_b, small, got_small, *pieces_m)
    kept_b, sent_b = sums(table, own(keep_b, got_b, far_b, near_b), cost=None)
    small = small + got_small
    kept_b, sent_b, small, *pieces_m = after(kept_b, sent_b, small, *pieces_m)
    sent_b = exchange(sent_b, to_below)
    got_small = exchange(small, to_x)
    pieces_m.append(exchange(pieces_m[1], to_core))
    small, got_small, kept_b, sent_b = after(small, got_small, kept_b, sent_b)
    small = small + got_small
    (kept_b,) = sums(table, plus(kept_b, sent_b), cost=None)
    kept_b, small, kept_n, got_kept_n = after(kept_b, small, kept_n, got_kept_n)
    got_kept_b = exchange(kept_b, to_two)
    got_small = exchange(small, to_y)
    (kept_n,) = sums(table, plus(kept_n, got_kept_n), cost=None)
    pieces_n = [kept_n, exchange(kept_n, to_below), exchange(kept_n, to_core)]
    small, got_small, kept_b, got_kept_b, *pieces_n = after(small, got_small, kept_b, got_kept_b, *pieces_n)
    (kept_b,) = sums(table, plus(kept_b, got_kept_b), cost=None)
    small = small + got_small
    kept_b, small = after(kept_b, small)
    pieces_b = [kept_b, exchange(kept_b, to_below), exchange(kept_b, to_core)]
    pieces_n.append(exchange(pieces_n[1], to_core))
    got_small = exchange(small, to_below)
    grad_wi, grad_wo = place(mlp_place_kernel, ((256, FF), (1024, D)), "mlp_place", table, *pieces_m, *pieces_n)
    grad_wi, small, got_small, *pieces_b = after(grad_wi, small, got_small, *pieces_b)
    pieces_b.append(exchange(pieces_b[1], to_core))
    small = small + got_small
    got_small = exchange(small, to_two)
    grad_qkv, grad_d = place(
        attn_place_kernel, ((256, 3 * D), (256, D)), "attn_place", table, *pieces_a, *pieces_b
    )
    grad_d, small, got_small = after(grad_d, small, got_small)
    small = lax.dynamic_index_in_dim(small + got_small, place_in_group, 0, keepdims=False)
    g_ga, g_sa, g_gm, g_sm, g_bd, g_bqkv, g_bi = jnp.split(small, np.cumsum([256] * 5 + [768]))
    return (
        layer_output, input_grad, g_ga, g_sa, g_gm, g_sm, grad_qkv, g_bqkv, grad_d, g_bd, grad_wi, g_bi, grad_wo, g_bd,
    )


def solution(mesh):
    replicas, shard_count = mesh.shape["rep"], mesh.shape["shard"]
    shape = (replicas // 2, 2, 2, shard_count // 2)
    cut = Mesh(mesh.devices.reshape(shape), ("z", "core", "y", "x"))
    both = P(("z", "core", "y", "x"), None)
    shard = P(("y", "x"))
    matrix = P(("y", "x"), None)
    weights = (shard,) * 4 + (matrix, shard) * 4
    body = shards if (replicas, shard_count) == (8, 4) else general_shards
    return jax.shard_map(
        body,
        mesh=cut,
        in_specs=(both, P(("z", "core", "y", "x")), both) + weights,
        out_specs=(both, both) + weights,
        check_vma=False,
    )
```

```python
import functools

import jax
import jax.numpy as jnp
import numpy as np
from jax import lax
from jax.experimental import pallas as pl
from jax.experimental.pallas import tpu as pltpu
from jax.sharding import Mesh, PartitionSpec as P

D = 1024
H = 16
FF = 4096
HD = 64
ROT = 16
T = 1024
GROUP = 256
HEADS = GROUP // HD
ROWS = 256
EPSILON = 1e-05
MASKED = -1e30
BF = jnp.bfloat16
F32 = jnp.float32
VMEM = 60 * 2**20


def nn(a, b):
    return lax.dot_general(a, b, (((1,), (0,)), ((), ())), preferred_element_type=F32)


def nt(a, b):
    return lax.dot_general(a, b, (((1,), (1,)), ((), ())), preferred_element_type=F32)


def tn(a, b):
    return lax.dot_general(a, b, (((0,), (0,)), ((), ())), preferred_element_type=F32)


def rows_of(index, size):
    return slice(index * size, (index + 1) * size)


def rotary_tables():
    half = ROT // 2
    inverse = 1.0 / np.float32(10000.0) ** (np.arange(half, dtype=np.float32) * np.float32(2.0 / ROT))
    angles = np.arange(T, dtype=np.float32)[:, None] * inverse.astype(np.float32)[None, :]
    cosine = np.ones((T, HD), np.float32)
    ahead = np.zeros((T, HD), np.float32)
    behind = np.zeros((T, HD), np.float32)
    cosine[:, :half] = np.cos(angles)
    cosine[:, half:ROT] = np.cos(angles)
    ahead[:, :half] = -np.sin(angles)
    behind[:, half:ROT] = np.sin(angles)
    return [np.tile(table, (1, 2)) for table in (cosine, ahead, behind)]


def add_columns(ref, rows, value, order):
    width = value.shape[1] // len(order)
    for place, block in enumerate(order):
        ref[rows, rows_of(block, width)] += value[:, rows_of(place, width)]


def mlp_kernel(order, nm, gr, wi, bi, wo, out, dn, gwi, gwo, gbi, act, ig):
    @pl.when(pl.program_id(0) == 0)
    def _():
        out[...] = jnp.zeros_like(out)
        dn[...] = jnp.zeros_like(dn)

    bias_sum = jnp.zeros(gbi.shape, F32)
    for t in range(T // ROWS):
        r = rows_of(t, ROWS)
        inner = nn(nm[r, :], wi[...]) + bi[...]
        grad = nt(gr[r, :], wo[...])
        normal = 0.5 * lax.erf(inner * 0.7071067811865476) + 0.5
        slope = normal + inner * jnp.exp(-0.5 * inner * inner) * 0.3989422804014327
        act[r, :] = (inner * normal).astype(BF)
        inner_grad = (grad * slope).astype(BF)
        ig[r, :] = inner_grad
        bias_sum += jnp.sum(inner_grad.astype(F32), axis=0, keepdims=True)
    gbi[...] = bias_sum
    for t in range(T // ROWS):
        r = rows_of(t, ROWS)
        out[r, :] += nn(act[r, :], wo[...])
        add_columns(dn, r, nt(ig[r, :], wi[...]), order)
    for d in range(D // ROWS):
        r = rows_of(d, ROWS)
        gwi[r, :] = tn(nm[:, r], ig[...]).astype(BF)
    step = min(ROWS, act.shape[1])
    for f in range(act.shape[1] // step):
        r = rows_of(f, step)
        gwo[r, :] = tn(act[:, r], gr[...]).astype(BF)


def mlp(order, nm, gr, wi, bi, wo):
    tile = FF // len(order)
    half = len(order) // 2
    one = pl.Buffered(1)
    whole = lambda: pl.BlockSpec((T, D), lambda i: (0, 0), pipeline_mode=one)
    total = lambda: pl.BlockSpec((T, D), lambda i: (0, 0))
    columns = lambda rows: pl.BlockSpec((rows, tile), lambda i: (0, (i % half) * 2 + i // half))
    return pl.pallas_call(
        functools.partial(mlp_kernel, order),
        grid=(FF // tile,),
        in_specs=[whole(), whole(), columns(D), columns(1), pl.BlockSpec((tile, D), lambda i: (i, 0))],
        out_specs=[total(), total(), columns(D), pl.BlockSpec((tile, D), lambda i: (i, 0)), columns(1)],
        out_shape=[
            jax.ShapeDtypeStruct((T, D), F32),
            jax.ShapeDtypeStruct((T, D), F32),
            jax.ShapeDtypeStruct((D, FF), BF),
            jax.ShapeDtypeStruct((FF, D), BF),
            jax.ShapeDtypeStruct((1, FF), F32),
        ],
        scratch_shapes=[pltpu.VMEM((T, tile), BF), pltpu.VMEM((T, tile), BF)],
        compiler_params=pltpu.CompilerParams(vmem_limit_bytes=VMEM),
        cost_estimate=pl.CostEstimate(flops=12 * T * D * FF, bytes_accessed=60 * 2**20, transcendentals=2 * T * FF),
        name="mlp",
    )(nm, gr, wi, bi, wo)


def attn_kernel(
    order, length, na, gr, wq, wk, wv, bq, bk, bv, wd, cosine, ahead, behind,
    out, dn, gwq, gwk, gwv, gwd, gb,
    q, k, v, dc, ctx, dq, dk, dv, grads,
):
    @pl.when(pl.program_id(0) == 0)
    def _():
        out[...] = jnp.zeros_like(out)
        dn[...] = jnp.zeros_like(dn)

    def turn(x, r, back):
        parts = []
        for p in range(GROUP // 128):
            pair = x[:, rows_of(p, 128)]
            straight = pair * cosine[r, :]
            across = (
                pltpu.roll(pair, 128 - ROT // 2, 1) * ahead[r, :]
                + pltpu.roll(pair, ROT // 2, 1) * behind[r, :]
            )
            parts.append(straight - across if back else straight + across)
        return jnp.concatenate(parts, axis=1)

    for t in range(T // ROWS):
        r = rows_of(t, ROWS)
        x = na[r, :]
        queries = (turn(nn(x, wq[...]) + bq[...], r, False).astype(BF) * 0.125).astype(BF)
        keys = turn(nn(x, wk[...]) + bk[...], r, False).astype(BF)
        values = (nn(x, wv[...]) + bv[...]).astype(BF)
        context_grad = nt(gr[r, :], wd[...]).astype(BF)
        for h in range(HEADS):
            c = rows_of(h, HD)
            q[h, r, :] = queries[:, c]
            k[h, r, :] = keys[:, c]
            v[h, r, :] = values[:, c]
            dc[h, r, :] = context_grad[:, c]

    block = 256
    inside = lax.broadcasted_iota(jnp.int32, (1, T), 1) < length[0]
    bias = jnp.where(inside, 0.0, MASKED).astype(F32)
    below = lax.broadcasted_iota(jnp.int32, (block, block), 1) <= lax.broadcasted_iota(jnp.int32, (block, block), 0)
    causal = jnp.where(below, 0.0, MASKED).astype(F32)

    def head(h, carry):
        dk[h] = jnp.zeros((T, HD), F32)
        dv[h] = jnp.zeros((T, HD), F32)
        for i in range(T // block):
            r = rows_of(i, block)
            spans = ([slice(0, i * block)] if i else []) + [r]
            query = q[h, r, :]
            scores = [nt(query, k[h, c, :]) + bias[:, c] for c in spans]
            scores[-1] += causal
            top = functools.reduce(jnp.maximum, [jnp.max(s, axis=1, keepdims=True) for s in scores])
            weights = [jnp.exp(s - top) for s in scores]
            scale = 1.0 / sum(jnp.sum(w, axis=1, keepdims=True) for w in weights)
            low = [w.astype(BF) for w in weights]
            context = sum(nn(w, v[h, c, :]) for w, c in zip(low, spans))
            ctx[h, r, :] = (context * scale).astype(BF)
            scaled_grad = (dc[h, r, :].astype(F32) * scale).astype(BF)
            probs_grad = [nt(scaled_grad, v[h, c, :]) for c in spans]
            inner = scale * sum(jnp.sum(w * p, axis=1, keepdims=True) for w, p in zip(weights, probs_grad))
            score_grad = [(w * (p - inner)).astype(BF) for w, p in zip(weights, probs_grad)]
            dq[h, r, :] = sum(nn(s, k[h, c, :]) for s, c in zip(score_grad, spans))
            for s, w, c in zip(score_grad, low, spans):
                dk[h, c, :] += tn(s, query)
                dv[h, c, :] += tn(w, scaled_grad)
        return carry

    lax.fori_loop(0, HEADS, head, 0)

    sums = [jnp.zeros((1, GROUP), F32) for _ in range(3)]
    together = lambda ref, r: jnp.concatenate([ref[h, r, :] for h in range(HEADS)], axis=1)
    for t in range(T // ROWS):
        r = rows_of(t, ROWS)
        context = together(ctx, r)
        grads[r, 3 * GROUP :] = context
        out[r, :] += nn(context, wd[...])
        pieces = (
            turn(together(dq, r) * 0.125, r, True).astype(BF),
            turn(together(dk, r), r, True).astype(BF),
            together(dv, r).astype(BF),
        )
        for p, piece in enumerate(pieces):
            grads[r, rows_of(p, GROUP)] = piece
            sums[p] += jnp.sum(piece.astype(F32), axis=0, keepdims=True)
        normed_grad = sum(nt(piece, w[...]) for piece, w in zip(pieces, (wq, wk, wv)))
        add_columns(dn, r, normed_grad, order)
    for p in range(3):
        gb[p : p + 1, :] = sums[p]
    for d in range(D // ROWS):
        r = rows_of(d, ROWS)
        x = na[:, r]
        for p, g in enumerate((gwq, gwk, gwv)):
            g[r, :] = tn(x, grads[:, rows_of(p, GROUP)]).astype(BF)
    gwd[...] = tn(grads[:, 3 * GROUP :], gr[...]).astype(BF)


def attn(order, length, na, gr, weight, bias, wd):
    groups = D // GROUP
    one = pl.Buffered(1)
    whole = lambda shape: pl.BlockSpec(shape, lambda i: (0, 0), pipeline_mode=one)
    total = lambda: pl.BlockSpec((T, D), lambda i: (0, 0))
    columns = lambda rows, part=0: pl.BlockSpec((rows, GROUP), lambda i: (0, i + part * groups))
    head_rows = lambda dtype: pltpu.VMEM((HEADS, T, HD), dtype)
    return pl.pallas_call(
        functools.partial(attn_kernel, order),
        grid=(groups,),
        in_specs=[pl.BlockSpec(memory_space=pltpu.SMEM), whole((T, D)), whole((T, D))]
        + [columns(D, p) for p in range(3)]
        + [columns(1, p) for p in range(3)]
        + [pl.BlockSpec((GROUP, D), lambda i: (i, 0))]
        + [whole((T, 128))] * 3,
        out_specs=[total(), total()] + [columns(D)] * 3 + [pl.BlockSpec((GROUP, D), lambda i: (i, 0)), columns(3)],
        out_shape=[jax.ShapeDtypeStruct((T, D), F32)] * 2
        + [jax.ShapeDtypeStruct((D, D), BF)] * 4
        + [jax.ShapeDtypeStruct((3, D), F32)],
        scratch_shapes=[head_rows(BF)] * 5 + [head_rows(F32)] * 3 + [pltpu.VMEM((T, 4 * GROUP), BF)],
        compiler_params=pltpu.CompilerParams(vmem_limit_bytes=VMEM),
        cost_estimate=pl.CostEstimate(flops=90 * 10**9, bytes_accessed=40 * 2**20, transcendentals=10 * 2**20),
        name="attn",
    )(length, na, gr, weight, weight, weight, bias, bias, bias, wd, *map(jnp.asarray, rotary_tables()))


def general_shards(
    layer_input, seq_lengths, out_grad, attn_gain, attn_shift, mlp_gain, mlp_shift, qkv_weight, qkv_bias,
    dense_weight, dense_bias, inner_weight, inner_bias, outer_weight, outer_bias,
):
    groupings = ("core", "y", "x")
    shard_count = lax.axis_size("y") * lax.axis_size("x")
    core = lax.axis_index("core")
    order = [2 * a + h for h in range(2) for a in range(shard_count)]

    def gather(piece):
        half = piece.shape[0] // 2
        mine = lax.dynamic_slice_in_dim(piece, core * half, half, 0)
        return lax.all_gather(mine, groupings, axis=0, tiled=True)

    def natural(rows):
        return jnp.swapaxes(rows.reshape(2, shard_count, -1, rows.shape[1]), 0, 1).reshape(rows.shape)

    def halves_first(rows):
        return jnp.swapaxes(rows.reshape(shard_count, 2, -1, rows.shape[1]), 0, 1).reshape(rows.shape)

    vectors = jnp.concatenate(
        [attn_gain, attn_shift, mlp_gain, mlp_shift, dense_bias, outer_bias, qkv_bias, inner_bias]
    )
    vectors = lax.all_gather(vectors, ("y", "x"), axis=0, tiled=False).astype(F32)
    sizes = [D] * 6 + [3 * D, FF]
    cuts = np.cumsum([size // shard_count for size in sizes])[:-1]
    gain_a, shift_a, gain_m, shift_m, bias_d, bias_o, bias_qkv, bias_i = (
        part.reshape(1, -1) for part in jnp.split(vectors, cuts, axis=1)
    )
    wi = gather(inner_weight)
    wo = gather(outer_weight)
    wqkv = gather(qkv_weight)
    wd = natural(gather(dense_weight))

    x = layer_input.astype(F32)
    mean = jnp.mean(x, axis=1, keepdims=True)
    centered = x - mean
    inverse = lax.rsqrt(jnp.mean(centered * centered, axis=1, keepdims=True) + EPSILON)
    unit = centered * inverse
    valid = jnp.arange(T, dtype=jnp.int32)[:, None] < seq_lengths[0]
    gr = jnp.where(valid, out_grad, jnp.zeros_like(out_grad))
    blocked = lambda rows: jnp.swapaxes(rows.reshape(T, shard_count, 2, -1), 1, 2).reshape(T, D)
    nm = blocked((unit * gain_m + shift_m).astype(BF))
    na = blocked((unit * gain_a + shift_a).astype(BF))

    out_m, dnm, gwi, gwo, gbi = mlp(order, nm, gr, wi, bias_i, wo)
    out_a, dna, gwq, gwk, gwv, gwd, gbqkv = attn(order, seq_lengths, na, gr, wqkv, bias_qkv, wd)

    def reduce(grad):
        part = lax.psum_scatter(grad, "core", scatter_dimension=0, tiled=True)
        part = lax.psum_scatter(part, ("y", "x"), scatter_dimension=0, tiled=True)
        part = lax.psum(part, "z")
        return lax.all_gather(part, "core", axis=0, tiled=True).astype(F32)

    grad_wi = reduce(gwi)
    grad_wo = reduce(gwo)
    grad_d = reduce(halves_first(gwd))
    grad_qkv = jnp.concatenate([reduce(g) for g in (gwq, gwk, gwv)], axis=1)

    layer_output = x + out_m + out_a + (bias_d + bias_o)
    g = dna * gain_a + dnm * gain_m
    gr32 = gr.astype(F32)
    input_grad = gr32 + inverse * (
        g - jnp.mean(g, axis=1, keepdims=True) - unit * jnp.mean(g * unit, axis=1, keepdims=True)
    )
    column = lambda rows: jnp.sum(rows, axis=0)
    parts = [column(dna * unit), column(dna), column(dnm * unit), column(dnm), column(gr32), gbqkv, gbi]
    small = jnp.concatenate([p.reshape(shard_count, -1) for p in parts], axis=1)
    small = lax.psum_scatter(small, ("y", "x"), scatter_dimension=0, tiled=True)
    small = lax.psum(small, ("z", "core"))
    cuts = np.cumsum([size // shard_count for size in [D] * 5 + [3 * D, FF]])[:-1]
    g_ga, g_sa, g_gm, g_sm, g_bd, g_bqkv, g_bi = (p.reshape(-1) for p in jnp.split(small, cuts, axis=1))
    return (
        layer_output, input_grad, g_ga, g_sa, g_gm, g_sm, grad_qkv, g_bqkv, grad_d, g_bd, grad_wi, g_bi, grad_wo, g_bd,
    )


WIDE = 512
VMEM_UNIT = 56 * 2**20
LONG = pl.CostEstimate(flops=10**13, bytes_accessed=2**20, transcendentals=0)


def columns_at(start, size):
    return pl.ds(pl.multiple_of(start, 128), size)


def spread_kernel(table, *refs):
    *given, gain_a, shift_a, gain_m, shift_m, bias, first_pair, second_pair, first_unit, second_unit = refs
    for j, ref in enumerate(given):
        shard = table[6] ^ j
        rows = ref[...].astype(F32)
        row = lambda k: rows[k : k + 1, :]
        for i, out in enumerate((gain_a, shift_a, gain_m, shift_m)):
            for k in range(2):
                out[:, columns_at(shard * 256 + k * 128, 128)] = row(2 * i + k)
        for k in range(2):
            bias[:, columns_at(shard * 256 + k * 128, 128)] = row(8 + k) + row(10 + k)
        for k in range(6):
            column = shard * 768 + k * 128
            part, owner = column >> 10, (column & 1023) >> 8
            target = (owner >> 1) * 768 + part * 256 + (owner & 1) * 128
            (first_pair, second_pair)[k % 2][:, columns_at(target, 128)] = row(12 + k)
        for k in range(8):
            (first_unit, second_unit)[k // 4][:, columns_at(shard * 512 + k % 4 * 128, 128)] = row(18 + k)


def spread(table, given):
    inside = pl.BlockSpec(memory_space=pltpu.VMEM)
    widths = [D] * 5 + [1536] * 2 + [2048] * 2
    return pl.pallas_call(
        spread_kernel,
        in_specs=[pl.BlockSpec(memory_space=pltpu.SMEM)] + [inside] * len(given),
        out_specs=[inside] * len(widths),
        out_shape=[jax.ShapeDtypeStruct((1, width), F32) for width in widths],
        name="spread",
    )(table, *given)


def norm_kernel(table, x, grad, gain_a, shift_a, gain_m, shift_m, na, nm, gr):
    values = x[...].astype(F32)
    mean = jnp.mean(values, axis=1, keepdims=True)
    centered = values - mean
    unit = centered * lax.rsqrt(jnp.mean(centered * centered, axis=1, keepdims=True) + EPSILON)
    rows = x.shape[0]
    position = pl.program_id(0) * rows + lax.broadcasted_iota(jnp.int32, (rows, 1), 0)
    gr[...] = jnp.where(position < table[1], grad[...].astype(F32), 0.0).astype(BF)
    for out, gain, shift in ((na, gain_a, shift_a), (nm, gain_m, shift_m)):
        normed = (unit * gain[...] + shift[...]).astype(BF)
        for a in range(4):
            for h in range(2):
                place = (table[2 + a] * 2 + (table[0] ^ h)) * 128
                out[:, columns_at(place, 128)] = normed[:, rows_of(a * 2 + h, 128)]


def norm(table, x, grad, vectors):
    tile = pl.BlockSpec((ROWS, D), lambda i: (i, 0))
    row = pl.BlockSpec((1, D), lambda i: (0, 0))
    return pl.pallas_call(
        norm_kernel,
        grid=(T // ROWS,),
        in_specs=[pl.BlockSpec(memory_space=pltpu.SMEM), tile, tile] + [row] * 4,
        out_specs=[tile] * 3,
        out_shape=[jax.ShapeDtypeStruct((T, D), BF)] * 3,
        compiler_params=pltpu.CompilerParams(vmem_limit_bytes=VMEM),
        cost_estimate=LONG,
        name="norm",
    )(table, x, grad, *vectors)


def finish_kernel(table, x, gr, dna, dnm, gain_a, gain_m, *refs):
    *bias_sums, input_grad, small, sums = refs
    values = x[...].astype(F32)
    mean = jnp.mean(values, axis=1, keepdims=True)
    centered = values - mean
    inverse = lax.rsqrt(jnp.mean(centered * centered, axis=1, keepdims=True) + EPSILON)
    unit = centered * inverse

    def natural(ref):
        places = [(table[2 + a] * 2 + (table[0] ^ h)) * 128 for a in range(4) for h in range(2)]
        return jnp.concatenate([ref[:, columns_at(place, 128)] for place in places], axis=1)

    normed_a, normed_m = natural(dna), natural(dnm)
    upper = gr[...].astype(F32)
    g = normed_a * gain_a[...] + normed_m * gain_m[...]
    input_grad[...] = upper + inverse * (
        g - jnp.mean(g, axis=1, keepdims=True) - unit * jnp.mean(g * unit, axis=1, keepdims=True)
    )

    @pl.when(pl.program_id(0) == 0)
    def _():
        sums[...] = jnp.zeros_like(sums)

    for i, rows in enumerate((normed_a * unit, normed_a, normed_m * unit, normed_m, upper)):
        sums[i : i + 1, :] += jnp.sum(rows, axis=0, keepdims=True)

    @pl.when(pl.program_id(0) == T // ROWS - 1)
    def _():
        for i in range(5):
            for a in range(4):
                small[a : a + 1, rows_of(i, 256)] = sums[i : i + 1, rows_of(a, 256)]
        pair_sums, unit_sums = bias_sums[:3], bias_sums[3:]
        for pair in range(2):
            for a, b in qkv_blocks(pair):
                value = pair_sums[0] if pair == 0 else pair_sums[1 + b // 768]
                small[a // 768 : a // 768 + 1, pl.ds(1280 + a % 768, 128)] = value[:, pl.ds(b if pair == 0 else b % 768, 128)]
        for a in range(4):
            small[a : a + 1, pl.ds(2048, 512)] = unit_sums[0][:, rows_of(a, 512)]
            small[a : a + 1, pl.ds(2560, 512)] = unit_sums[1 + a // 2][:, rows_of(a % 2, 512)]


def finish(table, x, gr, dna, dnm, vectors, bias_sums):
    tile = pl.BlockSpec((ROWS, D), lambda i: (i, 0))
    row = lambda value: pl.BlockSpec(value.shape, lambda i: (0, 0))
    return pl.pallas_call(
        finish_kernel,
        grid=(T // ROWS,),
        in_specs=[pl.BlockSpec(memory_space=pltpu.SMEM)] + [tile] * 4 + [row(v) for v in (*vectors, *bias_sums)],
        out_specs=[tile, pl.BlockSpec((4, 3072), lambda i: (0, 0))],
        out_shape=[jax.ShapeDtypeStruct((T, D), F32), jax.ShapeDtypeStruct((4, 3072), F32)],
        scratch_shapes=[pltpu.VMEM((5, D), F32)],
        compiler_params=pltpu.CompilerParams(vmem_limit_bytes=VMEM),
        cost_estimate=LONG,
        name="finish",
    )(table, x, gr, dna, dnm, *vectors, *bias_sums)


class Totals:
    def __init__(self, refs_in, refs_out, scratch, sems):
        self.fresh = [ref is None for ref in refs_in]
        self.refs_in, self.refs_out, self.scratch, self.sems = refs_in, refs_out, scratch, sems

    def loads(self):
        return [
            pltpu.make_async_copy(source, self.scratch[i], self.sems.at[i])
            for i, source in enumerate(self.refs_in)
            if source is not None
        ]

    def stores(self):
        return [
            pltpu.make_async_copy(source, target, self.sems.at[i])
            for i, (source, target) in enumerate(zip(self.scratch, self.refs_out))
        ]

    def begin(self):
        for copy in self.loads():
            copy.start()
        for target, source in zip(self.scratch, self.refs_in):
            if source is None:
                target[...] = jnp.zeros_like(target)

    def ready(self):
        for copy in self.loads():
            copy.wait()


def start_all(copies):
    for copy in copies:
        copy.start()


def wait_all(copies):
    for copy in copies:
        copy.wait()


def mlp_unit_kernel(first, count, given, table, nm, gr, bi, pieces, *refs):
    refs = list(refs)
    olds = [refs.pop(0) if is_given else None for is_given in given]
    keep, send, gbi, out_ref, dn_ref, wi, wo, act, ig, out, dn, inner_stage, outer_stage, sems, out_sems, total_sems = refs
    step = pl.program_id(0)
    core = table[0]
    totals = Totals(olds[2:], (out_ref, dn_ref), (out, dn), total_sems)

    def copies(index):
        slot, tile = index % 2, first + index
        made = []
        for t in range(4):
            for half in range(2):
                piece = (core ^ half) * 4 + table[6 + t]
                source = pieces.at[piece, 0, :, columns_at(tile * WIDE, WIDE)]
                made.append((source, wi.at[slot, pl.ds(t * 256 + half * 128, 128), :]))
        for h in range(2):
            for part in range(2):
                source = pieces.at[h * 4 + tile, 1, :, pl.ds(part * D, D)]
                made.append((source, wo.at[slot, pl.ds(h * 256 + part * 128, 128), :]))
        return [pltpu.make_async_copy(a, b, sems.at[slot, i]) for i, (a, b) in enumerate(made)]

    def results(index):
        slot, tile = index % 2, first + index
        made = []
        for side, target in enumerate((keep, send)):
            inner_part = target.at[:, pl.ds(pl.multiple_of(tile // 2 * 128, 128), 128), columns_at((tile % 2) * WIDE, WIDE)]
            made.append((inner_stage.at[slot, side], inner_part))
            made.append((outer_stage.at[slot, side], target.at[table[2 + tile], pl.ds(256, 256)]))
        return [pltpu.make_async_copy(a, b, out_sems.at[slot, i]) for i, (a, b) in enumerate(made)]

    @pl.when(step == 0)
    def _():
        start_all(copies(step))
        totals.begin()

    @pl.when(step < count - 1)
    def _():
        start_all(copies(step + 1))

    wait_all(copies(step))
    slot = step % 2

    bias_sum = jnp.zeros(gbi.shape, F32)
    for t in range(T // WIDE):
        r = rows_of(t, WIDE)
        inner = nn(nm[r, :], wi[slot]) + bi[...]
        grad = nt(gr[r, :], wo[slot])
        normal = 0.5 * lax.erf(inner * 0.7071067811865476) + 0.5
        slope = normal + inner * jnp.exp(-0.5 * inner * inner) * 0.3989422804014327
        act[r, :] = (inner * normal).astype(BF)
        inner_grad = (grad * slope).astype(BF)
        ig[r, :] = inner_grad
        bias_sum += jnp.sum(inner_grad.astype(F32), axis=0, keepdims=True)
    gbi[...] = bias_sum

    @pl.when(step == 0)
    def _():
        totals.ready()

    for t in range(T // WIDE):
        r = rows_of(t, WIDE)
        out[r, :] += nn(act[r, :], wo[slot])
        dn[r, :] += nt(ig[r, :], wi[slot])

    @pl.when(step == count - 1)
    def _():
        start_all(totals.stores())

    if count > 2:

        @pl.when(step >= 2)
        def _():
            wait_all(results(step - 2))

    for t in range(4):
        grad = tn(nm[:, rows_of(t, 256)], ig[...]).astype(BF)
        inner_stage[slot, 0, t] = grad[:128]
        inner_stage[slot, 1, t] = grad[128:]
    for f in range(2):
        grad = tn(act[:, rows_of(f, 256)], gr[...])
        low, high = grad[:, :WIDE], grad[:, WIDE:]
        sides = (jnp.where(core == 0, low, high).astype(BF), jnp.where(core == 0, high, low).astype(BF))
        for side, value in enumerate(sides):
            for half in range(2):
                outer_stage[slot, side, rows_of(f, 128), rows_of(half, WIDE)] = value[rows_of(half, 128)]
    start_all(results(step))

    @pl.when(step == count - 1)
    def _():
        if count > 1:
            wait_all(results(step - 1))
        wait_all(results(step))
        wait_all(totals.stores())


def mlp_unit(first, count, table, nm, gr, bi, pieces, parts, totals):
    olds = list(parts) + list(totals)
    given = tuple(old is not None for old in olds)
    inputs = [old for old in olds if old is not None]
    aliases = {5 + n: (0, 1, 3, 4)[i] for n, i in enumerate(i for i in range(4) if given[i])}
    whole = pl.BlockSpec((T, D), lambda i: (0, 0), pipeline_mode=pl.Buffered(1))
    anywhere = pl.BlockSpec(memory_space=pl.ANY)
    return pl.pallas_call(
        functools.partial(mlp_unit_kernel, first, count, given),
        grid=(count,),
        in_specs=[pl.BlockSpec(memory_space=pltpu.SMEM), whole, whole, pl.BlockSpec((1, WIDE), lambda i: (0, first + i)), anywhere]
        + [anywhere] * len(inputs),
        out_specs=[anywhere, anywhere, pl.BlockSpec((1, WIDE), lambda i: (0, i)), anywhere, anywhere],
        out_shape=[jax.ShapeDtypeStruct((4, 512, D), BF)] * 2
        + [jax.ShapeDtypeStruct((1, count * WIDE), F32)]
        + [jax.ShapeDtypeStruct((T, D), F32)] * 2,
        input_output_aliases=aliases,
        scratch_shapes=[
            pltpu.VMEM((2, D, WIDE), BF),
            pltpu.VMEM((2, WIDE, D), BF),
            pltpu.VMEM((T, WIDE), BF),
            pltpu.VMEM((T, WIDE), BF),
            pltpu.VMEM((T, D), F32),
            pltpu.VMEM((T, D), F32),
            pltpu.VMEM((2, 2, 4, 128, WIDE), BF),
            pltpu.VMEM((2, 2, 256, D), BF),
            pltpu.SemaphoreType.DMA((2, 12)),
            pltpu.SemaphoreType.DMA((2, 4)),
            pltpu.SemaphoreType.DMA((2,)),
        ],
        compiler_params=pltpu.CompilerParams(vmem_limit_bytes=VMEM_UNIT),
        cost_estimate=LONG,
        name="mlp_unit",
    )(table, nm, gr, bi, pieces, *inputs)


def attn_unit_kernel(first, count, given, apart, last, table, na, gr, bias, cosine, ahead, behind, *refs):
    refs = list(refs)
    pieces = [refs.pop(0) for _ in range(8 if apart else 1)]
    rest = [refs.pop(0) for _ in range(2 if last else 0)]
    olds = [refs.pop(0) if is_given else None for is_given in given]
    (
        keep, send, gb, out_ref, dn_ref,
        w, wd, q, k, v, dc, ctx, dq, dk, dv, grads, out, dn, qkv_stage, dense_stage, sems, out_sems, total_sems,
    ) = refs
    step = pl.program_id(0)
    core = table[0]
    totals = Totals(olds[2:], (out_ref, dn_ref), (out, dn), total_sems)

    def copies(index):
        group = first + index
        made = []
        for t in range(4):
            for half in range(2):
                if apart:
                    piece = pieces[half * 4 + t].at[0]
                    place = wd.at[table[6 + t] // 2, pl.ds(pl.multiple_of(table[6 + t] % 2 * 128, 128), 128), columns_at((core ^ half) * 512, 512)]
                    if isinstance(index, int) and index == 0:
                        made.append((piece.at[:, pl.ds(1536, 512)], place))
                else:
                    piece = pieces[0].at[(core ^ half) * 4 + table[6 + t]]
                made.append((piece.at[:, columns_at(group * 768, 768)], w.at[index, pl.ds(t * 256 + half * 128, 128), :]))
        for pair in range(0 if apart else 2):
            for h in range(2):
                source = pieces[0].at[h * 4 + group * 2 + pair, :, pl.ds(1536, 512)]
                made.append((source, wd.at[index, pl.ds(pair * 128, 128), pl.ds(h * 512, 512)]))
        return [pltpu.make_async_copy(a, b, sems.at[index, i]) for i, (a, b) in enumerate(made)]

    def results(index):
        group = first + index
        made = []
        for side, target in enumerate((keep, send)):
            made.append((qkv_stage.at[index, side], target.at[:, :, columns_at(group * 768, 768)]))
            for pair in range(2):
                place = target.at[table[2 + group * 2 + pair], :, pl.ds(1536, 512)]
                made.append((dense_stage.at[index, side, pair], place))
        return [pltpu.make_async_copy(a, b, out_sems.at[index, i]) for i, (a, b) in enumerate(made)]

    @pl.when(step == 0)
    def _():
        for index in range(count):
            start_all(copies(index))
        totals.begin()

    for index in range(count):

        @pl.when(step == index)
        def _():
            wait_all(copies(index))

    def turn(x, r, back):
        parts = []
        for p in range(GROUP // 128):
            pair = x[:, rows_of(p, 128)]
            straight = pair * cosine[r, :]
            across = (
                pltpu.roll(pair, 128 - ROT // 2, 1) * ahead[r, :]
                + pltpu.roll(pair, ROT // 2, 1) * behind[r, :]
            )
            parts.append(straight - across if back else straight + across)
        return jnp.concatenate(parts, axis=1)

    part = [slice(p * GROUP, (p + 1) * GROUP) for p in range(4)]
    for t in range(T // ROWS):
        r = rows_of(t, ROWS)
        x = na[r, :]
        projected = nn(x, w[step]) + bias[...]
        queries = (turn(projected[:, part[0]], r, False).astype(BF) * 0.125).astype(BF)
        keys = turn(projected[:, part[1]], r, False).astype(BF)
        values = projected[:, part[2]].astype(BF)
        context_grad = nt(gr[r, :], wd[step]).astype(BF)
        for h in range(HEADS):
            c = rows_of(h, HD)
            q[h, r, :] = queries[:, c]
            k[h, r, :] = keys[:, c]
            v[h, r, :] = values[:, c]
            dc[h, r, :] = context_grad[:, c]

    block = 512
    inside = lax.broadcasted_iota(jnp.int32, (1, T), 1) < table[1]
    outside = jnp.where(inside, 0.0, MASKED).astype(F32)
    below = lax.broadcasted_iota(jnp.int32, (block, block), 1) <= lax.broadcasted_iota(jnp.int32, (block, block), 0)
    causal = jnp.where(below, 0.0, MASKED).astype(F32)

    def head(h, carry):
        dk[h] = jnp.zeros((HD, T), F32)
        dv[h] = jnp.zeros((HD, T), F32)
        for i in range(T // block):
            r = rows_of(i, block)
            spans = ([slice(0, i * block)] if i else []) + [r]
            query = q[h, r, :]
            scores = [nt(query, k[h, c, :]) + outside[:, c] for c in spans]
            scores[-1] += causal
            top = functools.reduce(jnp.maximum, [jnp.max(s, axis=1, keepdims=True) for s in scores])
            weights = [jnp.exp(s - top) for s in scores]
            scale = 1.0 / sum(jnp.sum(e, axis=1, keepdims=True) for e in weights)
            low = [e.astype(BF) for e in weights]
            context = sum(nn(e, v[h, c, :]) for e, c in zip(low, spans))
            ctx[h, r, :] = (context * scale).astype(BF)
            scaled_grad = (dc[h, r, :].astype(F32) * scale).astype(BF)
            probs_grad = [nt(scaled_grad, v[h, c, :]) for c in spans]
            inner = scale * sum(jnp.sum(e * p, axis=1, keepdims=True) for e, p in zip(weights, probs_grad))
            score_grad = [(e * (p - inner)).astype(BF) for e, p in zip(weights, probs_grad)]
            dq[h, r, :] = sum(nn(s, k[h, c, :]) for s, c in zip(score_grad, spans))
            query_turned, grad_turned = query.T, scaled_grad.T
            for s, e, c in zip(score_grad, low, spans):
                dk[h, :, c] += nn(query_turned, s)
                dv[h, :, c] += nn(grad_turned, e)
        return carry

    lax.fori_loop(0, HEADS // 2, lambda p, carry: head(2 * p + 1, head(2 * p, carry)), 0)

    @pl.when(step == 0)
    def _():
        totals.ready()

    sums = jnp.zeros((1, 3 * GROUP), F32)
    together = lambda ref, r: jnp.concatenate([ref[h, r, :] for h in range(HEADS)], axis=1)
    for t in range(T // ROWS):
        r = rows_of(t, ROWS)
        context = together(ctx, r)
        grads[r, part[3]] = context
        total = nn(context, wd[step])
        if last:
            total += rest[0][r, :].astype(F32) + rest[1][...]
        out[r, :] += total
        projected_grad = jnp.concatenate(
            [
                turn(together(dq, r) * 0.125, r, True).astype(BF),
                turn(jnp.concatenate([dk[h, :, r] for h in range(HEADS)], axis=0).T, r, True).astype(BF),
                jnp.concatenate([dv[h, :, r] for h in range(HEADS)], axis=0).T.astype(BF),
            ],
            axis=1,
        )
        grads[r, : 3 * GROUP] = projected_grad
        sums += jnp.sum(projected_grad.astype(F32), axis=0, keepdims=True)
        dn[r, :] += nt(projected_grad, w[step])
    gb[...] = sums

    @pl.when(step == count - 1)
    def _():
        start_all(totals.stores())

    for t in range(4):
        grad = tn(na[:, rows_of(t, 256)], grads[:, : 3 * GROUP]).astype(BF)
        qkv_stage[step, 0, t] = grad[:128]
        qkv_stage[step, 1, t] = grad[128:]
    grad = tn(grads[:, part[3]], gr[...])
    first_half, second_half = grad[:, :WIDE], grad[:, WIDE:]
    sides = (
        jnp.where(core == 0, first_half, second_half).astype(BF),
        jnp.where(core == 0, second_half, first_half).astype(BF),
    )
    for side, value in enumerate(sides):
        for pair in range(2):
            dense_stage[step, side, pair] = value[rows_of(pair, 128)]
    start_all(results(step))

    @pl.when(step == count - 1)
    def _():
        for index in range(count):
            wait_all(results(index))
        wait_all(totals.stores())


def attn_unit(first, count, table, na, gr, bias, tables, pieces, parts, totals, rest=()):
    olds = list(parts) + list(totals)
    given = tuple(old is not None for old in olds)
    inputs = [old for old in olds if old is not None]
    apart = isinstance(pieces, list)
    pieces = pieces if apart else [pieces]
    aliases = {7 + len(pieces) + len(rest) + n: (0, 1, 3, 4)[i] for n, i in enumerate(i for i in range(4) if given[i])}
    one = pl.Buffered(1)
    whole = pl.BlockSpec((T, D), lambda i: (0, 0), pipeline_mode=one)
    turns = pl.BlockSpec((T, 128), lambda i: (0, 0), pipeline_mode=one)
    anywhere = pl.BlockSpec(memory_space=pl.ANY)
    head_rows = lambda dtype: pltpu.VMEM((HEADS, T, HD), dtype)
    return pl.pallas_call(
        functools.partial(attn_unit_kernel, first, count, given, apart, len(rest) > 0),
        grid=(count,),
        in_specs=[pl.BlockSpec(memory_space=pltpu.SMEM), whole, whole, pl.BlockSpec((1, 3 * GROUP), lambda i: (0, first + i))]
        + [turns] * 3
        + [anywhere] * len(pieces)
        + [pl.BlockSpec(value.shape, lambda i: (0, 0), pipeline_mode=one) for value in rest]
        + [anywhere] * len(inputs),
        out_specs=[anywhere, anywhere, pl.BlockSpec((1, 3 * GROUP), lambda i: (0, i)), anywhere, anywhere],
        out_shape=[jax.ShapeDtypeStruct((4, 128, 2 * D), BF)] * 2
        + [jax.ShapeDtypeStruct((1, 3 * GROUP * count), F32)]
        + [jax.ShapeDtypeStruct((T, D), F32)] * 2,
        input_output_aliases=aliases,
        scratch_shapes=[pltpu.VMEM((count, D, 3 * GROUP), BF), pltpu.VMEM((count, GROUP, D), BF)]
        + [head_rows(BF)] * 5
        + [head_rows(F32)] + [pltpu.VMEM((HEADS, HD, T), F32)] * 2
        + [
            pltpu.VMEM((T, 4 * GROUP), BF),
            pltpu.VMEM((T, D), F32),
            pltpu.VMEM((T, D), F32),
            pltpu.VMEM((count, 2, 4, 128, 3 * GROUP), BF),
            pltpu.VMEM((count, 2, 2, 128, WIDE), BF),
            pltpu.SemaphoreType.DMA((count, 16)),
            pltpu.SemaphoreType.DMA((count, 6)),
            pltpu.SemaphoreType.DMA((2,)),
        ],
        compiler_params=pltpu.CompilerParams(vmem_limit_bytes=VMEM_UNIT),
        cost_estimate=LONG,
        name="attn_unit",
    )(table, na, gr, bias, *tables, *pieces, *rest, *inputs)


def qkv_blocks(pair):
    return [
        (part * D + (2 * group + shard) * 256 + pair * 128, group * 768 + part * 256 + shard * 128)
        for group in range(2)
        for part in range(3)
        for shard in range(2)
    ]


def attn_pack_kernel(pair, table, qkv, dense, *refs):
    *pieces, sems = refs
    copies = []
    for side, piece in enumerate(pieces):
        half = table[0] ^ side
        rows = pl.ds(pl.multiple_of(half * 128, 128), 128)
        made = [(qkv.at[rows, pl.ds(a, 128)], piece.at[0, :, pl.ds(b, 128)]) for a, b in qkv_blocks(pair)]
        made.append((dense.at[pl.ds(pair * 128, 128), columns_at(half * 512, 512)], piece.at[0, :, pl.ds(1536, 512)]))
        copies += [pltpu.make_async_copy(a, b, sems.at[side * 13 + i]) for i, (a, b) in enumerate(made)]
    start_all(copies)
    wait_all(copies)


def mlp_pack_kernel(unit, table, inner, outer, piece, sems):
    core = table[0]
    rows = pl.ds(pl.multiple_of(core * 128, 128), 128)
    made = [(inner.at[rows, pl.ds(a * 1024 + unit * 512, 512)], piece.at[0, 0, :, pl.ds(a * 512, 512)]) for a in range(4)]
    for part in range(2):
        source = outer.at[pl.ds(pl.multiple_of(unit * 512 + core * 256 + part * 128, 128), 128), :]
        made.append((source, piece.at[0, 1, :, pl.ds(part * D, D)]))
    copies = [pltpu.make_async_copy(a, b, sems.at[i]) for i, (a, b) in enumerate(made)]
    start_all(copies)
    wait_all(copies)


def pack(kernel, shape, count, sides, name, table, *weights):
    anywhere = pl.BlockSpec(memory_space=pl.ANY)
    return pl.pallas_call(
        kernel,
        in_specs=[pl.BlockSpec(memory_space=pltpu.SMEM)] + [anywhere] * len(weights),
        out_specs=[pl.BlockSpec(memory_space=pltpu.VMEM)] * sides,
        out_shape=[jax.ShapeDtypeStruct(shape, BF)] * sides,
        scratch_shapes=[pltpu.SemaphoreType.DMA((count * sides,))],
        cost_estimate=LONG,
        name=name,
    )(table, *weights)


def attn_place_kernel(table, *refs):
    *values, grad_qkv, grad_d = refs
    for i, value in enumerate(values):
        pair, half, part = i // 4, table[0] ^ (i // 2 % 2), table[10] ^ (i % 2)
        rows = pl.ds(pl.multiple_of(half * 128 + part * 64, 64), 64)
        for a, b in qkv_blocks(pair):
            grad_qkv[rows, pl.ds(a, 128)] = value[0, :, pl.ds(b, 128)].astype(F32)
        rows = pl.ds(pl.multiple_of(pair * 128 + part * 64, 64), 64)
        grad_d[rows, columns_at(half * 512, 512)] = value[0, :, pl.ds(1536, 512)].astype(F32)


def mlp_place_kernel(table, *refs):
    *values, grad_wi, grad_wo = refs
    for i, value in enumerate(values):
        unit, half = i // 4, table[0] ^ (i // 2 % 2)

        @pl.when(table[10] == i % 2)
        def _():
            rows = pl.ds(pl.multiple_of(half * 128, 128), 128)
            for tile in range(4):
                columns = pl.ds(tile * 1024 + unit * 512, 512)
                grad_wi[rows, columns] = value[0, rows_of(tile // 2, 128), rows_of(tile % 2, 512)].astype(F32)

        @pl.when(table[10] != i % 2)
        def _():
            for f in range(2):
                for part in range(2):
                    rows = pl.ds(unit * 512 + f * 256 + part * 128, 128)
                    columns = columns_at(half * 512, 512)
                    grad_wo[rows, columns] = value[0, rows_of(f, 128), rows_of(part, 512)].astype(F32)


def place(kernel, shapes, name, table, *values):
    inside = pl.BlockSpec(memory_space=pltpu.VMEM)
    return pl.pallas_call(
        kernel,
        in_specs=[pl.BlockSpec(memory_space=pltpu.SMEM)] + [inside] * len(values),
        out_specs=[inside] * len(shapes),
        out_shape=[jax.ShapeDtypeStruct(shape, F32) for shape in shapes],
        compiler_params=pltpu.CompilerParams(vmem_limit_bytes=VMEM),
        name=name,
    )(table, *values)


def add_kernel(*refs):
    *sources, target = refs
    target[...] = sum(source[...].astype(F32) for source in sources).astype(BF)


def add(*sources, count=1, cost=LONG):
    rows, columns = sources[0][0].shape[1:]
    steps = 2
    read = lambda first, stride: pl.BlockSpec(
        (1, rows // steps, columns), lambda i: (first + stride * (i // steps), i % steps, 0)
    )
    return pl.pallas_call(
        add_kernel,
        grid=(count * steps,),
        in_specs=[read(first, stride) for _, first, stride in sources],
        out_specs=read(0, 1),
        out_shape=jax.ShapeDtypeStruct((count, rows, columns), BF),
        cost_estimate=cost,
        name="add",
    )(*(array for array, _, _ in sources))


def sums_kernel(plan, table, *refs):
    refs = list(refs)
    taken = [[refs.pop(0) for _ in range(count)] for count, _ in plan]
    for sources, (_, split) in zip(taken, plan):
        total = sum(source[...].astype(F32) for source in sources).astype(BF)
        if not split:
            refs.pop(0)[...] = total
            continue
        kept, sent = refs.pop(0), refs.pop(0)

        @pl.when(pl.program_id(0) == table[10])
        def _():
            kept[...] = total

        @pl.when(pl.program_id(0) != table[10])
        def _():
            sent[...] = total


def sums(table, *jobs, cost=LONG):
    specs, arrays, out_specs, out_shapes, plan = [], [], [], [], []
    for split, sources in jobs:
        sources = [source if isinstance(source, tuple) else (source, 0) for source in sources]
        rows, columns = sources[0][0].shape[1] // 2, sources[0][0].shape[2]
        for array, block in sources:
            arrays.append(array)
            specs.append(pl.BlockSpec((1, rows, columns), lambda i, block=block: (block, i, 0)))
        plan.append((len(sources), split))
        place = (lambda i: (0, 0, 0)) if split else (lambda i: (0, i, 0))
        for _ in range(1 + split):
            out_specs.append(pl.BlockSpec((1, rows, columns), place))
            out_shapes.append(jax.ShapeDtypeStruct((1, rows * (1 if split else 2), columns), BF))
    return pl.pallas_call(
        functools.partial(sums_kernel, plan),
        grid=(2,),
        in_specs=[pl.BlockSpec(memory_space=pltpu.SMEM)] + specs,
        out_specs=out_specs,
        out_shape=out_shapes,
        compiler_params=pltpu.CompilerParams(vmem_limit_bytes=VMEM // 2),
        cost_estimate=cost,
        name="sums",
    )(table, *arrays)


AXES = ("z", "core", "y", "x")


def exchange(value, partner):
    pairs = []
    for z in range(4):
        for core in range(2):
            for shard in range(4):
                to_z, to_core, to_shard = partner(z, core, shard)
                pairs.append(((z * 2 + core) * 4 + shard, (to_z * 2 + to_core) * 4 + to_shard))
    return lax.ppermute(value, AXES, pairs)


to_core = lambda z, core, shard: (z, 1 - core, shard)
to_first = lambda z, core, shard: (z, core, shard ^ (1 + core))
to_second = lambda z, core, shard: (z, core, shard ^ (2 - core))
to_x = lambda z, core, shard: (z, core, shard ^ 1)
to_y = lambda z, core, shard: (z, core, shard ^ 2)
to_xy = lambda z, core, shard: (z, core, shard ^ 3)
to_below = lambda z, core, shard: (z ^ 1, core, shard)
to_two = lambda z, core, shard: (z ^ 2, core, shard)


def wide(value):
    return value.astype(F32)


def shards(
    layer_input, seq_lengths, out_grad, attn_gain, attn_shift, mlp_gain, mlp_shift, qkv_weight, qkv_bias,
    dense_weight, dense_bias, inner_weight, inner_bias, outer_weight, outer_bias,
):
    core = lax.axis_index("core")
    place_in_group = lax.axis_index("y") * 2 + lax.axis_index("x")
    steps = jnp.where(core == 0, jnp.array([0, 2, 1, 3], jnp.int32), jnp.array([0, 1, 2, 3], jnp.int32))
    shard_of = place_in_group ^ steps
    difference = place_in_group ^ jnp.arange(4, dtype=jnp.int32)
    block_of = jnp.where(core == 1, difference, ((difference & 1) << 1) | (difference >> 1))
    parity = lax.axis_index("z") % 2
    table = jnp.concatenate([core[None], seq_lengths, block_of, shard_of, parity[None]]).astype(jnp.int32)

    gather = lambda piece: lax.all_gather(piece, ("core", "y", "x"), axis=0, tiled=True)
    pack_attn = lambda pair, sides: pack(
        functools.partial(attn_pack_kernel, pair), (1, 128, 2 * D), 13, sides, "attn_pack", table, qkv_weight, dense_weight
    )
    pack_mlp = lambda unit: pack(
        functools.partial(mlp_pack_kernel, unit), (1, 2, 128, 2 * D), 6, 1, "mlp_pack", table, inner_weight, outer_weight
    )[0]

    def after(done, *values):
        return lax.optimization_barrier((done,) + values)

    part, rest = pack_attn(0, 2)
    from_first = exchange(part, to_first)
    from_second = exchange(part, to_second)
    vectors = (attn_gain, attn_shift, mlp_gain, mlp_shift, dense_bias, outer_bias, qkv_bias, inner_bias)
    part, table, *vectors = after(part, table, *vectors)
    vectors = [vector.reshape(-1, 128) for vector in vectors]
    ends = np.cumsum([vector.shape[0] for vector in vectors])
    vectors = sum(jnp.pad(v, ((end - v.shape[0], 26 - end), (0, 0))) for v, end in zip(vectors, ends))
    packed = [pack_mlp(0), pack_mlp(1)]
    vectors = [vectors] + [exchange(vectors, to) for to in (to_x, to_y, to_xy)]
    from_first, from_second, table, *packed = after(from_first, from_second, table, *packed)
    from_both = exchange(from_first, to_second)
    core_first = exchange(from_first, to_core)
    core_second = exchange(from_second, to_core)
    gain_a, shift_a, gain_m, shift_m, bias_out, *biases = spread(table, vectors)
    bias_pairs, bias_units = biases[:2], biases[2:]
    na, nm, gr = norm(table, layer_input, out_grad, (gain_a, shift_a, gain_m, shift_m))
    pieces = [None] + [gather(piece) for piece in packed]
    na, from_both = after(na, from_both)
    core_both = exchange(from_both, to_core)
    pieces[0] = [part, from_second, from_first, from_both, rest, core_first, core_second, core_both]
    tables = [jnp.asarray(t) for t in rotary_tables()]

    far_blocks = lambda keep, got, cost=LONG: add((keep, 2, 1), (got, 1, 2), count=2, cost=cost)
    near = lambda keep, got, far: (False, [(keep, 1), (got, 2), (far, 1)])
    own = lambda *arrays: (True, arrays)
    plus = lambda *arrays: (False, arrays)

    none = (None, None)
    attn_call = lambda first, count, pair, parts, totals, rest=(): attn_unit(
        first, count, table, na, gr, bias_pairs[pair], tables, pieces[3 * pair], parts, totals, rest
    )
    mlp_call = lambda first, count, unit, parts, totals: mlp_unit(
        first, count, table, nm, gr, bias_units[unit], pieces[1 + unit], parts, totals
    )

    keep_a, send_a, gb0, out, dna = attn_call(0, 2, 0, none, none)
    got_a = exchange(send_a, to_core)
    out, table = after(out, table)
    packed_b = pack_attn(1, 1)[0]
    out, keep_a, got_a, packed_b = after(out, keep_a, got_a, packed_b)
    far_a = far_blocks(keep_a, got_a)
    out, far_a = after(out, far_a)
    far_a = exchange(far_a, to_first)

    keep_m, send_m, gbi0, out, dnm = mlp_call(0, 4, 0, none, (out, None))
    got_m = exchange(send_m, to_core)
    out, keep_a, got_a, far_a = after(out, keep_a, got_a, far_a)
    (near_a,) = sums(table, near(keep_a, got_a, far_a))
    near_a, keep_m, got_m = after(near_a, keep_m, got_m)
    far_m = far_blocks(keep_m, got_m)
    out, near_a, far_m = after(out, near_a, far_m)
    near_a = exchange(near_a, to_second)
    far_m = exchange(far_m, to_first)

    keep_n, send_n, gbi1a, out, dnm = mlp_call(0, 2, 1, none, (out, dnm))
    out, keep_a, got_a, far_a, near_a, keep_m, got_m, far_m = after(
        out, keep_a, got_a, far_a, near_a, keep_m, got_m, far_m
    )
    kept_a, sent_a, near_m = sums(table, own(keep_a, got_a, far_a, near_a), near(keep_m, got_m, far_m))
    out, kept_a, sent_a, near_m, packed_b = after(out, kept_a, sent_a, near_m, packed_b)
    pieces.append(gather(packed_b))
    sent_a = exchange(sent_a, to_below)
    near_m = exchange(near_m, to_second)

    keep_n, send_n, gbi1b, out, dnm = mlp_call(2, 2, 1, (keep_n, send_n), (out, dnm))
    got_n = exchange(send_n, to_core)
    out, kept_a, sent_a, keep_m, got_m, far_m, near_m = after(
        out, kept_a, sent_a, keep_m, got_m, far_m, near_m
    )
    kept_m, sent_m, kept_a = sums(table, own(keep_m, got_m, far_m, near_m), plus(kept_a, sent_a))
    kept_m, sent_m, kept_a, keep_n, got_n = after(kept_m, sent_m, kept_a, keep_n, got_n)
    far_n = far_blocks(keep_n, got_n)
    out, kept_m, sent_m, kept_a, far_n = after(out, kept_m, sent_m, kept_a, far_n)
    got_kept_a = exchange(kept_a, to_two)
    sent_m = exchange(sent_m, to_below)
    far_n = exchange(far_n, to_first)

    keep_b, send_b, gb1a, out, dna = attn_call(0, 1, 1, none, (out, dna))
    out, kept_a, got_kept_a, kept_m, sent_m, keep_n, got_n, far_n = after(
        out, kept_a, got_kept_a, kept_m, sent_m, keep_n, got_n, far_n
    )
    kept_a, kept_m, near_n = sums(
        table, plus(kept_a, got_kept_a), plus(kept_m, sent_m), near(keep_n, got_n, far_n)
    )
    out, kept_a, kept_m, near_n = after(out, kept_a, kept_m, near_n)
    got_kept_m = exchange(kept_m, to_two)
    near_n = exchange(near_n, to_second)
    pieces_a = [kept_a, exchange(kept_a, to_below), exchange(kept_a, to_core)]

    rest = (layer_input, bias_out)
    keep_b, send_b, gb1b, layer_output, dna = attn_call(1, 1, 1, (keep_b, send_b), (out, dna), rest)
    got_b = exchange(send_b, to_core)
    layer_output, keep_n, got_n, far_n, near_n, kept_m, got_kept_m, *pieces_a = after(
        layer_output, keep_n, got_n, far_n, near_n, kept_m, got_kept_m, *pieces_a
    )
    kept_n, sent_n, kept_m = sums(table, own(keep_n, got_n, far_n, near_n), plus(kept_m, got_kept_m))
    kept_n, sent_n, keep_b, got_b = after(kept_n, sent_n, keep_b, got_b)
    sent_n = exchange(sent_n, to_below)
    pieces_m = [kept_m, exchange(kept_m, to_below), exchange(kept_m, to_core)]
    far_b = far_blocks(keep_b, got_b, None)
    far_b, dna, dnm = after(far_b, dna, dnm)
    far_b = exchange(far_b, to_first)
    pieces_a.append(exchange(pieces_a[1], to_core))

    bias_sums = [gb0, gb1a, gb1b, gbi0, gbi1a, gbi1b]
    input_grad, small = finish(table, layer_input, gr, dna, dnm, (gain_a, gain_m), bias_sums)
    small, kept_n, sent_n = after(small, kept_n, sent_n)
    (kept_n,) = sums(table, plus(kept_n, sent_n), cost=None)
    kept_n, small, far_b, keep_b, got_b = after(kept_n, small, far_b, keep_b, got_b)
    got_kept_n = exchange(kept_n, to_two)
    (near_b,) = sums(table, near(keep_b, got_b, far_b))
    near_b, small = after(near_b, small)
    near_b = exchange(near_b, to_second)
    got_small = exchange(small, to_core)
    near_b, small, got_small, *pieces_m = after(near_b, small, got_small, *pieces_m)
    kept_b, sent_b = sums(table, own(keep_b, got_b, far_b, near_b), cost=None)
    small = small + got_small
    kept_b, sent_b, small, *pieces_m = after(kept_b, sent_b, small, *pieces_m)
    sent_b = exchange(sent_b, to_below)
    got_small = exchange(small, to_x)
    pieces_m.append(exchange(pieces_m[1], to_core))
    small, got_small, kept_b, sent_b = after(small, got_small, kept_b, sent_b)
    small = small + got_small
    (kept_b,) = sums(table, plus(kept_b, sent_b), cost=None)
    kept_b, small, kept_n, got_kept_n = after(kept_b, small, kept_n, got_kept_n)
    got_kept_b = exchange(kept_b, to_two)
    got_small = exchange(small, to_y)
    (kept_n,) = sums(table, plus(kept_n, got_kept_n), cost=None)
    pieces_n = [kept_n, exchange(kept_n, to_below), exchange(kept_n, to_core)]
    small, got_small, kept_b, got_kept_b, *pieces_n = after(small, got_small, kept_b, got_kept_b, *pieces_n)
    (kept_b,) = sums(table, plus(kept_b, got_kept_b), cost=None)
    small = small + got_small
    kept_b, small = after(kept_b, small)
    pieces_b = [kept_b, exchange(kept_b, to_below), exchange(kept_b, to_core)]
    pieces_n.append(exchange(pieces_n[1], to_core))
    got_small = exchange(small, to_below)
    grad_wi, grad_wo = place(mlp_place_kernel, ((256, FF), (1024, D)), "mlp_place", table, *pieces_m, *pieces_n)
    grad_wi, small, got_small, *pieces_b = after(grad_wi, small, got_small, *pieces_b)
    pieces_b.append(exchange(pieces_b[1], to_core))
    small = small + got_small
    got_small = exchange(small, to_two)
    grad_qkv, grad_d = place(
        attn_place_kernel, ((256, 3 * D), (256, D)), "attn_place", table, *pieces_a, *pieces_b
    )
    grad_d, small, got_small = after(grad_d, small, got_small)
    small = lax.dynamic_index_in_dim(small + got_small, place_in_group, 0, keepdims=False)
    g_ga, g_sa, g_gm, g_sm, g_bd, g_bqkv, g_bi = jnp.split(small, np.cumsum([256] * 5 + [768]))
    return (
        layer_output, input_grad, g_ga, g_sa, g_gm, g_sm, grad_qkv, g_bqkv, grad_d, g_bd, grad_wi, g_bi, grad_wo, g_bd,
    )


def solution(mesh):
    replicas, shard_count = mesh.shape["rep"], mesh.shape["shard"]
    shape = (replicas // 2, 2, 2, shard_count // 2)
    cut = Mesh(mesh.devices.reshape(shape), ("z", "core", "y", "x"))
    both = P(("z", "core", "y", "x"), None)
    shard = P(("y", "x"))
    matrix = P(("y", "x"), None)
    weights = (shard,) * 4 + (matrix, shard) * 4
    body = shards if (replicas, shard_count) == (8, 4) else general_shards
    return jax.shard_map(
        body,
        mesh=cut,
        in_specs=(both, P(("z", "core", "y", "x")), both) + weights,
        out_specs=(both, both) + weights,
        check_vma=False,
    )
```
